32 devices in a mesh: tm: 2 (over core), space: 16 (over z, y, x).
Axes of the slice: x: 2, y: 2, z: 4, core: 2. Of those that a mesh axis runs over, the one named last changes fastest.
Arguments:
- field_a: float32 [2, 8, 96, 18432], P('tm', None, 'space'), may hold values from -6 to 6
- field_b: float32 [2, 8, 96, 18432], P('tm', None, 'space'), may hold values from -6 to 6
- pairs: int32 [4, 16, 2], replicated, may hold values from 0 to 7
- signs: int32 [4, 16], replicated, may hold values from -1 to 1, as said below
Outputs:
- correlator: float32 [2, 4, 96, 18432], P('tm', None, 'space')
- first_diff: float32 [2, 4, 96, 18432], P('tm', None, 'space')
- second_diff: float32 [2, 4, 96, 18432], P('tm', None, 'space')
The draws below stay inside these ranges and needn't reach their ends.
Inputs may be any that keep to these rules, and one draw needn't show every extreme that they name: `signs`: each coefficient is -1 or 1.
All inputs are finite; a program needn't handle non-finite values.
Results may differ from the reference program's by a relative error of at most 0.0001.
Values sent between devices are 32-bit elements; how exact they have to be, the bound alone decides.
No kernel may reach another device: no remote copies, remote signals or barrier semaphores. Data moves between devices by JAX's collectives and lax.ppermute only.
A program may use at most 256 MiB of HBM per device.

```python
import jax
import jax.numpy as jnp
from jax import lax

NX = 96
NY = 96
NZ = 96
NC = 8
NCH = 4
NPAIR = 16
TIMES = 2


def draw_signs(key, part):
    return (jax.random.randint(key, (NCH, NPAIR), 0, 2) * 2 - 1).astype(jnp.int32)


def place_ends(drawn, key, smallest, top_value):
    longest = drawn.shape.index(max(drawn.shape))
    spots = []
    for shift in (0, 1):
        where = [jax.random.randint(jax.random.fold_in(key, axis), (), 0, length) for axis, length in enumerate(drawn.shape)]
        where[longest] = (where[longest] + shift) % drawn.shape[longest]
        spots.append(tuple(where))
    return drawn.at[spots[0]].set(smallest).at[spots[1]].set(top_value)


def block_levels(rng, extent, pieces, low, largest):
    loudness = 1.0
    for axis_at, shards_of in pieces:
        heights = jax.random.uniform(jax.random.fold_in(jax.random.fold_in(rng, 6), axis_at), (shards_of,), jnp.float32, low / len(pieces), largest / len(pieces))
        loudness = loudness * jnp.repeat(jnp.exp(heights), extent[axis_at] // shards_of).reshape((-1,) + (1,) * (len(extent) - 1 - axis_at))
    return loudness


def bell_draw(rng, shape, scale, reach, split=(), kind=jnp.bfloat16):
    level = block_levels(rng, shape, split, -0.22, 0.18) if split else 1.0
    array = jax.random.normal(rng, shape, jnp.float32) * scale * level
    return jnp.minimum(jnp.maximum(array, -reach), reach).astype(kind)


def setup_inputs(seed: int = 0) -> dict:
    splits = jax.random.split(jax.random.key(seed), 5)
    field_a = bell_draw(splits[0], (TIMES, NC, NX, NY * 2 * NZ), 1.0, 6.0, ((0, 2), (2, 16)), jnp.float32)
    field_b = bell_draw(splits[1], (TIMES, NC, NX, NY * 2 * NZ), 1.0, 6.0, ((0, 2), (2, 16)), jnp.float32)
    pairs = place_ends(jax.random.randint(splits[2], (NCH, NPAIR, 2), 0, NC), jax.random.fold_in(splits[2], 1), 0, NC - 1).astype(jnp.int32)
    signs = draw_signs(jax.random.fold_in(splits[4], 71), 0)
    return dict(field_a=field_a, field_b=field_b, pairs=pairs, signs=signs)


def reference(field_a, field_b, pairs, signs):
    indices = jnp.arange(NC, dtype=jnp.int32)
    first = (pairs[:, :, 0][:, :, None] == indices[None, None, :]).astype(jnp.float32)
    second = (pairs[:, :, 1][:, :, None] == indices[None, None, :]).astype(jnp.float32)
    weights = jnp.einsum('cp,cpi,cpj->cij', signs.astype(jnp.float32), first, second)
    shaped_a = field_a.reshape(TIMES, NC, NX, NY, 2 * NZ)
    shaped_b = field_b.reshape(TIMES, NC, NX, NY, 2 * NZ)

    def one_slice(operands):
        slice_a, slice_b = operands
        comp_a = slice_a[..., :NZ] + 1j * slice_a[..., NZ:]
        comp_b = slice_b[..., :NZ] + 1j * slice_b[..., NZ:]
        hat_a = jnp.fft.fftn(comp_a, axes=(1, 2, 3), norm="ortho")
        hat_b = jnp.conj(jnp.fft.fftn(comp_b, axes=(1, 2, 3), norm="ortho"))
        outputs = []
        for channel in range(NCH):
            mixed_b = jnp.einsum('ij,jxyz->ixyz', weights[channel], hat_b)
            outputs.append(jnp.sum(hat_a * mixed_b, axis=0))
        mixed = jnp.stack(outputs, axis=0)
        result = jnp.fft.ifftn(mixed, axes=(1, 2, 3), norm="ortho")
        return jnp.concatenate([jnp.real(result), jnp.imag(result)], axis=-1).astype(jnp.float32)

    correlator = lax.map(one_slice, (shaped_a, shaped_b))
    correlator = correlator.reshape(TIMES, NCH, NX, NY * 2 * NZ)
    later = jnp.roll(correlator, -1, axis=0)
    earlier = jnp.roll(correlator, 1, axis=0)
    first_diff = later - correlator
    second_diff = later - 2.0 * correlator + earlier
    return correlator, first_diff, second_diff
```

```python
import functools
import math

import jax
import jax.numpy as jnp
import ml_dtypes
import numpy as np
from jax import lax
from jax.experimental import pallas as pl
from jax.experimental.pallas import tpu as pltpu
from jax.sharding import PartitionSpec as P

highest = lax.Precision.HIGHEST
LANES = 128
SUB = 8


def unitary(length):
    index = np.arange(length)
    angle = (index[:, None] * index[None, :] % length) * (2.0 * np.pi / length)
    return np.cos(angle) / math.sqrt(length), np.sin(angle) / math.sqrt(length)


def halves(table):
    high = table.astype(np.float32).astype(ml_dtypes.bfloat16)
    low = (table - high.astype(np.float64)).astype(np.float32).astype(ml_dtypes.bfloat16)
    return np.stack([high, low])


def owned(devices, length):
    each = length // devices
    me = np.arange(devices)
    return ((me[:, None] ^ me[None, :]) * each)[:, :, None] + np.arange(each)


def rows_forward(devices, length):
    cos, sin = unitary(length)
    out = []
    for spots in owned(devices, length):
        k = spots.reshape(devices, -1, 2).transpose(2, 0, 1).reshape(-1)
        y = np.arange(length).reshape(-1, 2).T.reshape(-1)
        c, s = cos[k][:, y], sin[k][:, y]
        out.append(halves(np.block([[c, s], [-s, c]])))
    return np.stack(out)


def rows_inverse(devices, length):
    cos, sin = unitary(length)
    out = []
    for spots in owned(devices, length):
        y = np.arange(length).reshape(-1, 2).T.reshape(-1)
        blocks = []
        for e in range(2):
            k = spots.reshape(devices, -1, 2)[:, :, e].T.reshape(-1)
            c, s = cos[y][:, k], sin[y][:, k]
            blocks.append(np.block([[c, -s], [s, c]]))
        out.append(halves(np.concatenate(blocks)))
    return np.stack(out)


def columns_forward(devices, length):
    cos, sin = unitary(length)
    out = []
    for spots in owned(devices, length):
        c, s = cos[:, spots.reshape(-1)], sin[:, spots.reshape(-1)]
        out.append(halves(np.block([[c, s], [-s, c]])))
    return np.stack(out)


def columns_inverse(devices, length):
    cos, sin = unitary(length)
    out = []
    for spots in owned(devices, length):
        c, s = cos[spots.reshape(-1)], sin[spots.reshape(-1)]
        out.append(halves(np.block([[c, -s], [s, c]])))
    return np.stack(out)


def depth_forward(length, first, count):
    cos, sin = unitary(length)
    k = np.tile(np.arange(first, first + count), LANES // count)
    matrix = np.block([[cos[:, k], -sin[:, k]], [sin[:, k], cos[:, k]]])
    gap = np.zeros((2 * LANES - 2 * length, 2 * LANES))
    both = np.stack([np.concatenate([matrix, gap]), np.concatenate([gap, matrix])])
    return np.stack([halves(b) for b in both], axis=1)


def depth_inverse(length, wide):
    cos, sin = unitary(length)
    out = []
    for half in range(2):
        rows = []
        for first, count, lanes in ((0, wide, (0, 1)), (wide, length - wide, (half / 2, half / 2 + 0.5))):
            k = np.tile(np.arange(first, first + count), LANES // count)
            keep = np.zeros((LANES, 1))
            keep[int(lanes[0] * LANES) : int(lanes[1] * LANES)] = 1.0
            rows.append(np.concatenate([cos[k], sin[k]], axis=1) * keep)
            rows.append(np.concatenate([-sin[k], cos[k]], axis=1) * keep)
        matrix = np.concatenate(rows)
        gap = np.zeros((matrix.shape[0], 2 * LANES - 2 * length))
        both = (np.concatenate([matrix, gap], axis=1), np.concatenate([gap, matrix], axis=1))
        out.append(np.stack([halves(b) for b in both], axis=1))
    return np.stack(out)


def split(value):
    high = value.astype(jnp.bfloat16)
    return high, (value - high.astype(jnp.float32)).astype(jnp.bfloat16)


def dot3(left, right):
    dot = functools.partial(jnp.dot, preferred_element_type=jnp.float32)
    return dot(left[0], right[0]) + (dot(left[0], right[1]) + dot(left[1], right[0]))


def lane_index(shape):
    return lax.broadcasted_iota(jnp.int32, shape, len(shape) - 1)


def forward_kernel(narrow, sites, pairs_y, a0, a1, b0, b1, depth, table, out, staged, spectra):
    step = pl.program_id(0)
    groups = 1 if narrow else 2
    width = LANES // 4 if narrow else LANES // 2
    block = 2 * groups * sites * SUB
    rows = pairs_y * SUB
    y_table = (table[0], table[1])

    def one(field, which):
        def stage(p, carry):
            for q in range(3):
                start = pl.multiple_of((p * 3 + q) * LANES, LANES)
                staged[q, pl.ds(pl.multiple_of(p * SUB, SUB), sites), :] = field[0, 0, :, pl.ds(start, LANES)]
            return carry

        lax.fori_loop(0, pairs_y, stage, 0, unroll=4)
        for e in range(2):
            left = split(jnp.concatenate([staged[e], staged[e + 1]], axis=1))
            result = dot3(left, (depth[0, e], depth[1, e]))
            for part in range(2):
                spectra[which, part * 2 + e] = result[:, part * LANES : (part + 1) * LANES]

    def rows_of(which, x):
        return jnp.concatenate(
            [spectra[which, k, pl.ds(x, pairs_y, stride=SUB), :] for k in range(4)], axis=0
        )

    def send(load, group, slot):
        right = split(jnp.concatenate([load(x) for x in range(sites)], axis=1))
        result = dot3(y_table, right)
        half = result.shape[0] // 4
        for part in range(2):
            even = result[2 * part * half : (2 * part + 1) * half]
            odd = result[(2 * part + 1) * half : (2 * part + 2) * half]
            merged = jnp.where(lane_index(even.shape) // width % 2 == 0, even, odd)
            for x in range(sites):
                start = ((part * groups + group) * sites + x) * SUB + slot
                out[pl.ds(start, half, stride=block), :] = merged[:, x * LANES : (x + 1) * LANES]

    for group, (low, high) in enumerate(((a0, a1), (b0, b1))):
        one(low, 0)
        one(high, 1)
        if narrow:

            def load(x):
                first, second = rows_of(0, x), rows_of(1, x)
                return jnp.where(lane_index(first.shape) < LANES // 2, first, second)

            send(load, 0, group * 4 + step)
        else:
            send(functools.partial(rows_of, 0), group, step)
            send(functools.partial(rows_of, 1), group, step + 4)


def forward(field_a, field_b, depth, table, narrow):
    _, components, sites, flat = field_a.shape
    groups = 1 if narrow else 2
    size = table.shape[1] // 2
    pairs_y = size // 2
    lines = size // 2
    rows = lines * 2 * groups * sites * SUB
    spot = lambda shift: pl.BlockSpec((1, 1, sites, flat), lambda c: (0, c + shift, 0, 0))
    half = components // 2
    whole = lambda value: pl.BlockSpec(value.shape, lambda c: (0,) * value.ndim)
    return pl.pallas_call(
        functools.partial(forward_kernel, narrow, sites, pairs_y),
        grid=(half,),
        in_specs=[spot(0), spot(half), spot(0), spot(half), whole(depth), whole(table)],
        out_specs=pl.BlockSpec((rows, LANES), lambda c: (0, 0)),
        out_shape=jax.ShapeDtypeStruct((rows, LANES), jnp.float32),
        scratch_shapes=[
            pltpu.VMEM((3, pairs_y * SUB, LANES), jnp.float32),
            pltpu.VMEM((2, 4, pairs_y * SUB, LANES), jnp.float32),
        ],
        compiler_params=pltpu.CompilerParams(vmem_limit_bytes=40 << 20),
        cost_estimate=pl.CostEstimate(flops=8 * 10**9, bytes_accessed=12 * 10**6, transcendentals=0),
        name="forward_narrow" if narrow else "forward_wide",
    )(field_a, field_a, field_b, field_b, depth, table)


def middle_kernel(narrow, devices, sites, channels, count, pairs, signs, *refs):
    pieces, (table_f, table_i, out, lines, hats, mixed) = refs[:devices], refs[devices:]
    groups = 1 if narrow else 2
    size = devices * sites
    both = 2 * size
    for s, piece in enumerate(pieces):
        for part in range(2):
            for g in range(groups):
                for x in range(sites):
                    at = part * size + s * sites + x
                    lines[g, pl.ds(at, SUB, stride=both), :] = piece[0, part, g, x * SUB : (x + 1) * SUB, :]
    forward_table = (table_f[0], table_f[1])
    for g in range(groups):
        for quad in range(2):
            tiles = [lines[g, (quad * 4 + j) * both : (quad * 4 + j + 1) * both, :] for j in range(4)]
            result = dot3(forward_table, split(jnp.concatenate(tiles, axis=1)))
            for j in range(4):
                hat = result[:, j * LANES : (j + 1) * LANES]
                if narrow:
                    hats[quad, j] = hat
                    hats[quad, j + 4] = pltpu.roll(hat, LANES // 2, axis=1)
                else:
                    hats[g, quad * 4 + j] = hat

    def channel(c, carry):
        def pair(p, totals):
            i, j = pairs[c, 2 * p], pairs[c, 2 * p + 1]
            sign = signs[c, p].astype(jnp.float32)
            a_re, a_im = hats[0, i, 0:size, :], hats[0, i, size:both, :]
            b_re, b_im = hats[1, j, 0:size, :] * sign, hats[1, j, size:both, :] * sign
            return (
                totals[0] + (a_re * b_re + a_im * b_im),
                totals[1] + (a_im * b_re - a_re * b_im),
            )

        zero = jnp.zeros((size, LANES), jnp.float32)
        real, imag = lax.fori_loop(0, count, pair, (zero, zero))
        mixed[c, 0:size, :] = real
        mixed[c, size:both, :] = imag
        return carry

    lax.fori_loop(0, channels, channel, 0)
    inverse_table = (table_i[0], table_i[1])
    if narrow:
        tiles = []
        for c in range(0, channels, 2):
            other = pltpu.roll(mixed[c + 1], LANES // 2, axis=1)
            tiles.append(jnp.where(lane_index(other.shape) < LANES // 2, mixed[c], other))
    else:
        tiles = [mixed[c] for c in range(channels)]
    result = dot3(inverse_table, split(jnp.concatenate(tiles, axis=1)))
    for t in range(len(tiles)):
        for part in range(2):
            value = result[part * size : (part + 1) * size, t * LANES : (t + 1) * LANES]
            if narrow:
                out[0, pl.ds(2 * t + part, size, stride=4), :] = value
            else:
                out[0, part, pl.ds(t, size, stride=4), :] = value


def middle(pieces, pairs, signs, table_f, table_i, sites, channels, narrow):
    devices = len(pieces)
    size = devices * sites
    steps = pieces[0].shape[0]
    block = pieces[0].shape[1:]
    whole = lambda value: pl.BlockSpec(value.shape, lambda r: (0,) * value.ndim)
    smem = pl.BlockSpec(memory_space=pltpu.SMEM)
    rows = size * 4
    shape = (rows, LANES) if narrow else (2, rows, LANES)
    groups = 1 if narrow else 2
    return pl.pallas_call(
        functools.partial(middle_kernel, narrow, devices, sites, channels, signs.shape[1]),
        grid=(steps,),
        in_specs=[smem, smem]
        + [pl.BlockSpec((1,) + block, lambda r: (r,) + (0,) * len(block))] * devices
        + [whole(table_f), whole(table_i)],
        out_specs=pl.BlockSpec((1,) + shape, lambda r: (r,) + (0,) * len(shape)),
        out_shape=jax.ShapeDtypeStruct((steps,) + shape, jnp.float32),
        scratch_shapes=[
            pltpu.VMEM((groups, SUB * 2 * size, LANES), jnp.float32),
            pltpu.VMEM((2, SUB, 2 * size, LANES), jnp.float32),
            pltpu.VMEM((channels, 2 * size, LANES), jnp.float32),
        ],
        compiler_params=pltpu.CompilerParams(vmem_limit_bytes=40 << 20),
        cost_estimate=pl.CostEstimate(flops=4 * 10**9, bytes_accessed=10 * 10**6, transcendentals=0),
        name="middle_narrow" if narrow else "middle_wide",
    )(pairs, signs, *pieces, table_f, table_i)


def inverse_kernel(devices, sites, channels, pairs_y, *refs):
    wide, narrow = refs[:devices], refs[devices : 2 * devices]
    table, depth, out, lines_w, lines_n, staged = refs[2 * devices :]
    channel = pl.program_id(0)
    thirds = wide[0].shape[0]
    size = 2 * thirds * devices

    @pl.when(channel == 0)
    def _():
        for s in range(devices):
            for r in range(thirds):
                for v in range(sites * 4 // SUB):
                    tile = pl.ds(v * SUB, SUB)
                    at = r * devices + s
                    for part in range(2):
                        start = v * SUB * size + part * (size // 2) + at
                        lines_w[pl.ds(start, SUB, stride=size), :] = wide[s][r, part, tile, :]
                    start = v * SUB * (size // 2) + at
                    lines_n[pl.ds(start, SUB, stride=size // 2), :] = narrow[s][r, tile, :]

    y_table = (table[0], table[1])

    def rows_of(lines, spot, width):
        tiles = [lines[pl.ds(pl.multiple_of(spot(x) * size, SUB), size), :] for x in range(sites)]
        result = dot3(y_table, split(jnp.concatenate(tiles, axis=1)))
        half = result.shape[0] // 2
        first, second = result[:half], result[half:]
        return jnp.where(lane_index(first.shape) // width % 2 == 0, first, second)

    big = rows_of(lines_w, lambda x: x * 4 + channel, LANES // 2)
    small = rows_of(lines_n, lambda x: x * 2 + channel // 2, LANES // 4)
    products = []
    for e in range(2):
        rows = []
        for x in range(sites):
            lanes = slice(x * LANES, (x + 1) * LANES)
            rows.append(
                jnp.concatenate(
                    [
                        value[(2 * part + e) * pairs_y : (2 * part + e + 1) * pairs_y, lanes]
                        for value in (big, small)
                        for part in range(2)
                    ],
                    axis=1,
                )
            )
        left = split(jnp.concatenate(rows, axis=0))
        products.append(dot3(left, (depth[0, 0, e], depth[0, 1, e])))
    tiles = (
        products[0][:, :LANES],
        products[0][:, LANES:] + products[1][:, :LANES],
        products[1][:, LANES:],
    )
    for q in range(3):
        for x in range(sites):
            staged[q, pl.ds(x, pairs_y, stride=SUB), :] = tiles[q][x * pairs_y : (x + 1) * pairs_y]

    def store(p, carry):
        for q in range(3):
            start = pl.multiple_of((p * 3 + q) * LANES, LANES)
            out[0, 0, :, pl.ds(start, LANES)] = staged[q, pl.ds(pl.multiple_of(p * SUB, SUB), sites), :]
        return carry

    lax.fori_loop(0, pairs_y, store, 0, unroll=4)


def inverse(wide, narrow, table, depth, sites, channels, flat):
    devices = len(wide)
    size = table.shape[2]
    pairs_y = size // 2
    whole = lambda value: pl.BlockSpec(value.shape, lambda c: (0,) * value.ndim)
    return pl.pallas_call(
        functools.partial(inverse_kernel, devices, sites, channels, pairs_y),
        grid=(channels,),
        in_specs=[whole(v) for v in wide]
        + [whole(v) for v in narrow]
        + [whole(table), pl.BlockSpec((1,) + depth.shape[1:], lambda c: (c % 2, 0, 0, 0, 0))],
        out_specs=pl.BlockSpec((1, 1, sites, flat), lambda c: (0, c, 0, 0)),
        out_shape=jax.ShapeDtypeStruct((1, channels, sites, flat), jnp.float32),
        scratch_shapes=[
            pltpu.VMEM((sites * 4 * size, LANES), jnp.float32),
            pltpu.VMEM((sites * 2 * size, LANES), jnp.float32),
            pltpu.VMEM((3, pairs_y * SUB, LANES), jnp.float32),
        ],
        compiler_params=pltpu.CompilerParams(vmem_limit_bytes=40 << 20),
        cost_estimate=pl.CostEstimate(flops=8 * 10**9, bytes_accessed=6 * 10**6, transcendentals=0),
        name="inverse_rows_depth",
    )(*wide, *narrow, table, depth)


def exchange(pieces):
    devices = len(pieces)
    order = sorted(range(1, devices), key=lambda s: (s % 4, -(s // 8), s))
    got = [pieces[0]] + [None] * (devices - 1)
    for s in order:
        got[s] = lax.ppermute(pieces[s], "space", [(i, i ^ s) for i in range(devices)])
    return got


def fast_slice(field_a, field_b, pairs, signs, tables):
    _, components, sites, flat = field_a.shape
    devices = lax.axis_size("space")
    channels = pairs.shape[0]
    me = lax.axis_index("space")
    rows_f, rows_i, columns_f, columns_i = (
        lax.dynamic_index_in_dim(jnp.asarray(t), me, 0, False) for t in tables[:4]
    )
    depth_n, depth_w, depth_i = (jnp.asarray(t) for t in tables[4:])
    thirds = rows_f.shape[1] // 4 // devices
    flat_pairs = pairs.reshape(channels, -1)
    returned = []
    sent = []
    for narrow, depth in ((True, depth_n), (False, depth_w)):
        groups = 1 if narrow else 2
        packed = forward(field_a, field_b, depth, rows_f, narrow)
        packed = packed.reshape(devices, thirds, 2, groups, sites * SUB, LANES)
        sent.append(exchange([packed[s] for s in range(devices)]))
    for narrow, pieces in zip((True, False), sent):
        mixed = middle(pieces, flat_pairs, signs, columns_f, columns_i, sites, channels, narrow)
        rows = sites * 4
        if narrow:
            back = [mixed[:, s * rows : (s + 1) * rows] for s in range(devices)]
        else:
            back = [mixed[:, :, s * rows : (s + 1) * rows] for s in range(devices)]
        returned.append(exchange(back))
    return inverse(returned[1], returned[0], rows_i, depth_i, sites, channels, flat)


def neighbours(value):
    devices, length = lax.axis_size("tm"), value.shape[0]
    up = [(i, (i + 1) % devices) for i in range(devices)]
    down = [(j, i) for i, j in up]
    after = lax.ppermute(value[:1], "tm", down)
    before = after if devices == 2 and length == 1 else lax.ppermute(value[-1:], "tm", up)
    later = jnp.concatenate([value[1:], after], axis=0)
    earlier = jnp.concatenate([before, value[:-1]], axis=0)
    return later, earlier


def differences(correlator):
    later, earlier = neighbours(correlator)
    return correlator, later - correlator, later - 2.0 * correlator + earlier


def fast_device(tables, field_a, field_b, pairs, signs):
    parts = [
        fast_slice(field_a[t : t + 1], field_b[t : t + 1], pairs, signs, tables)
        for t in range(field_a.shape[0])
    ]
    return differences(jnp.concatenate(parts, axis=0))


def dft_tables(length):
    cos, sin = unitary(length)
    return jnp.asarray(cos, jnp.float32), jnp.asarray(sin, jnp.float32)


def swap_parts(values):
    half = values.shape[-1] // 2
    return jnp.concatenate([values[..., half:], -values[..., :half]], axis=-1)


def along_depth(values, inverse):
    cosines, sines = dft_tables(values.shape[-1] // 2)
    matrix = jnp.block([[cosines, -sines], [sines, cosines]])
    if inverse:
        return jnp.einsum("tcxyr,kr->tcxyk", values, matrix, precision=highest)
    return jnp.einsum("tcxyr,rk->tcxyk", values, matrix, precision=highest)


def along(values, sign, axis):
    cosines, sines = dft_tables(values.shape[axis])
    table = jnp.concatenate([cosines, sign * sines], axis=1)
    stacked = jnp.concatenate([values, swap_parts(values)], axis=axis)
    spec = "ky,tcxyr->tcxkr" if axis == 3 else "kx,tcxyr->tckyr"
    return jnp.einsum(spec, table, stacked, precision=highest)


def contract(weights, hat_a, hat_b):
    depth = hat_a.shape[-1] // 2
    outputs = []
    for channel in range(weights.shape[0]):
        mixed_b = jnp.einsum("ij,tjxyk->tixyk", weights[channel], hat_b, precision=highest)
        direct = jnp.sum(hat_a * mixed_b, axis=1)
        crossed = jnp.sum(hat_a * swap_parts(mixed_b), axis=1)
        real_part = direct[..., :depth] + direct[..., depth:]
        imag_part = -(crossed[..., :depth] + crossed[..., depth:])
        outputs.append(jnp.concatenate([real_part, imag_part], axis=-1))
    return jnp.stack(outputs, axis=1)


def any_device(depth, field_a, field_b, pairs, signs):
    as_five = lambda v: v.reshape(v.shape[:3] + (-1, 2 * depth))
    as_four = lambda v: v.reshape(v.shape[:3] + (-1,))
    indices = jnp.arange(field_a.shape[1], dtype=jnp.int32)
    first = (pairs[:, :, 0][:, :, None] == indices).astype(jnp.float32)
    second = (pairs[:, :, 1][:, :, None] == indices).astype(jnp.float32)
    weights = jnp.einsum("cp,cpi,cpj->cij", signs.astype(jnp.float32), first, second, precision=highest)
    hats = []
    for field in (field_a, field_b):
        partial = as_four(along(along_depth(as_five(field), False), 1.0, 3))
        lines = lax.all_to_all(partial, "space", split_axis=3, concat_axis=2, tiled=True)
        hats.append(along(as_five(lines), 1.0, 2))
    returned = as_four(along(contract(weights, *hats), -1.0, 2))
    sites = lax.all_to_all(returned, "space", split_axis=2, concat_axis=3, tiled=True)
    return differences(as_four(along_depth(along(as_five(sites), -1.0, 3), True)))


def solution(mesh):
    devices = mesh.shape["space"]
    times = mesh.shape["tm"]

    def program(field_a, field_b, pairs, signs):
        _, components, size, flat = field_a.shape
        depth = flat // size // 2
        wide = LANES // 2
        fits = (
            depth == size
            and 2 * depth == 3 * wide
            and components == SUB
            and pairs.shape[0] == 4
            and size % (2 * devices) == 0
            and devices & (devices - 1) == 0
            and (size // devices) * 4 % SUB == 0
            and size % (2 * SUB) == 0
        )
        if fits:
            tables = (
                rows_forward(devices, size),
                rows_inverse(devices, size),
                columns_forward(devices, size),
                columns_inverse(devices, size),
                depth_forward(depth, wide, depth - wide),
                depth_forward(depth, 0, wide),
                depth_inverse(depth, wide),
            )
            per_device = functools.partial(fast_device, tables)
        else:
            per_device = functools.partial(any_device, depth)
        spec = P("tm", None, "space", None)
        return jax.shard_map(
            per_device,
            mesh=mesh,
            in_specs=(spec, spec, P(), P()),
            out_specs=(spec, spec, spec),
            check_vma=False,
        )(field_a, field_b, pairs, signs)

    return program
```

```python
import functools
import math

import jax
import jax.numpy as jnp
import ml_dtypes
import numpy as np
from jax import lax
from jax.experimental import pallas as pl
from jax.experimental.pallas import tpu as pltpu
from jax.sharding import PartitionSpec as P

highest = lax.Precision.HIGHEST
LANES = 128
SUB = 8
GRANT = 56 << 20


def unitary(length):
    index = np.arange(length)
    angle = (index[:, None] * index[None, :] % length) * (2.0 * np.pi / length)
    return np.cos(angle) / math.sqrt(length), np.sin(angle) / math.sqrt(length)


def halves(table):
    high = table.astype(np.float32).astype(ml_dtypes.bfloat16)
    low = (table - high.astype(np.float64)).astype(np.float32).astype(ml_dtypes.bfloat16)
    return high, low


def left_table(table):
    high, low = halves(table)
    return np.concatenate([high, high, low], axis=1)


def right_table(table):
    high, low = halves(table)
    return np.concatenate([high, high, low], axis=0)


def owned(devices, length):
    each = length // devices
    me = np.arange(devices)
    return ((me[:, None] ^ me[None, :]) * each)[:, :, None] + np.arange(each)


def rows_forward(devices, length):
    cos, sin = unitary(length)
    out = []
    for spots in owned(devices, length):
        k = spots.reshape(devices, -1, 2).transpose(2, 0, 1).reshape(-1)
        y = np.arange(length).reshape(-1, 2).T.reshape(-1)
        c, s = cos[k][:, y], sin[k][:, y]
        out.append(left_table(np.block([[c, s], [-s, c]])))
    return np.stack(out)


def rows_inverse(devices, length):
    cos, sin = unitary(length)
    out = []
    for spots in owned(devices, length):
        y = np.arange(length).reshape(-1, 2).T.reshape(-1)
        blocks = []
        for e in range(2):
            k = spots.reshape(devices, -1, 2)[:, :, e].T.reshape(-1)
            c, s = cos[y][:, k], sin[y][:, k]
            blocks.append(np.block([[c, -s], [s, c]]))
        out.append(left_table(np.concatenate(blocks)))
    return np.stack(out)


def columns_forward(devices, length):
    cos, sin = unitary(length)
    out = []
    for spots in owned(devices, length):
        c, s = cos[:, spots.reshape(-1)], sin[:, spots.reshape(-1)]
        out.append(left_table(np.block([[c, s], [-s, c]])))
    return np.stack(out)


def columns_inverse(devices, length):
    cos, sin = unitary(length)
    out = []
    for spots in owned(devices, length):
        c, s = cos[spots.reshape(-1)], sin[spots.reshape(-1)]
        out.append(left_table(np.block([[c, -s], [s, c]])))
    return np.stack(out)


def depth_forward(length, first, count):
    cos, sin = unitary(length)
    k = np.tile(np.arange(first, first + count), LANES // count)
    matrix = np.block([[cos[:, k], -sin[:, k]], [sin[:, k], cos[:, k]]])
    gap = np.zeros((2 * LANES - 2 * length, 2 * LANES))
    both = np.stack([np.concatenate([matrix, gap]), np.concatenate([gap, matrix])])
    return np.stack([right_table(b) for b in both])


def depth_inverse(length, first, count, halves_of):
    cos, sin = unitary(length)
    k = np.tile(np.arange(first, first + count), LANES // count)
    out = []
    for half in range(halves_of):
        keep = (np.arange(LANES) * halves_of // LANES == half)[:, None] * 1.0
        matrix = np.block([[cos[k] * keep, sin[k] * keep], [-sin[k] * keep, cos[k] * keep]])
        gap = np.zeros((matrix.shape[0], 2 * LANES - 2 * length))
        both = (np.concatenate([matrix, gap], axis=1), np.concatenate([gap, matrix], axis=1))
        out.append(np.stack([right_table(b) for b in both]))
    return np.stack(out)


def split(value):
    high = value.astype(jnp.bfloat16)
    return high, (value - high.astype(jnp.float32)).astype(jnp.bfloat16)


def dot(left, right):
    return jnp.dot(left, right, preferred_element_type=jnp.float32)


def left_dot(table, value):
    high, low = split(value)
    return dot(table, jnp.concatenate([high, low, high], axis=0))


def lane_index(shape):
    return lax.broadcasted_iota(jnp.int32, shape, len(shape) - 1)


def forward_kernel(narrow, sites, pairs_y, field_a, field_b, depth, table, token, out, spectra):
    x = pl.program_id(0)
    groups = 1 if narrow else 2
    width = LANES // 4 if narrow else LANES // 2
    block = 2 * groups * sites * SUB
    slots = []
    for group, field in enumerate((field_a, field_b)):
        tiles = [
            jnp.concatenate(
                [field[0, 0, :, (3 * p + q) * LANES : (3 * p + q + 1) * LANES] for p in range(pairs_y)], axis=0
            )
            for q in range(3)
        ]
        tiles = [split(tile) for tile in tiles]
        for e in range(2):
            left = [tiles[e + k][part] for part in (0, 1, 0) for k in range(2)]
            result = dot(jnp.concatenate(left, axis=1), depth[e])
            for part in range(2):
                spectra[group, part * 2 + e] = result[:, part * LANES : (part + 1) * LANES]

        def rows_of(c, group=group):
            return jnp.concatenate(
                [spectra[group, k, pl.ds(c, pairs_y, stride=SUB), :] for k in range(4)], axis=0
            )

        if narrow:
            for c in range(SUB // 2):
                first, second = rows_of(c), rows_of(c + SUB // 2)
                pick = lane_index(first.shape) < LANES // 2
                slots.append((0, group * 4 + c, jnp.where(pick, first, second)))
        else:
            slots += [(group, c, rows_of(c)) for c in range(SUB)]

    for first in range(0, len(slots), SUB):
        batch = slots[first : first + SUB]
        result = left_dot(table[...], jnp.concatenate([value for _, _, value in batch], axis=1))
        half = result.shape[0] // 4
        for part in range(2):
            even = result[2 * part * half : (2 * part + 1) * half]
            odd = result[(2 * part + 1) * half : (2 * part + 2) * half]
            merged = jnp.where(lane_index(even.shape) // width % 2 == 0, even, odd)
            for i, (group, slot, _) in enumerate(batch):
                start = ((part * groups + group) * sites + x) * SUB + slot
                out[pl.ds(start, half, stride=block), :] = merged[:, i * LANES : (i + 1) * LANES]


def forward(field_a, field_b, depth, table, narrow, token):
    _, sites, components, flat = field_a.shape
    groups = 1 if narrow else 2
    size = table.shape[0] // 2
    pairs_y = size // 2
    lines = size // 2
    rows = lines * 2 * groups * sites * SUB
    spot = pl.BlockSpec((1, 1, components, flat), lambda x: (0, x, 0, 0))
    whole = lambda value: pl.BlockSpec(value.shape, lambda x: (0,) * value.ndim)
    return pl.pallas_call(
        functools.partial(forward_kernel, narrow, sites, pairs_y),
        grid=(sites,),
        in_specs=[spot, spot, whole(depth), whole(table), pl.BlockSpec(memory_space=pl.ANY)],
        out_specs=pl.BlockSpec((rows, LANES), lambda x: (0, 0)),
        out_shape=jax.ShapeDtypeStruct((rows, LANES), jnp.float32),
        scratch_shapes=[pltpu.VMEM((2, 4, pairs_y * SUB, LANES), jnp.float32)],
        compiler_params=pltpu.CompilerParams(vmem_limit_bytes=GRANT),
        cost_estimate=pl.CostEstimate(flops=8 * 10**9, bytes_accessed=12 * 10**6, transcendentals=0),
        name="forward_narrow" if narrow else "forward_wide",
    )(field_a, field_b, depth, table, token)


def each(refs):
    return [ref.at[i] for ref in refs for i in range(ref.shape[0])]


def middle_kernel(narrow, arrays, devices, sites, channels, count, pairs, signs, *refs):
    pieces, refs = each(refs[:arrays]), refs[arrays:]
    table_f, table_i, out, lines, hats, mixed, rows = refs
    groups = 1 if narrow else 2
    size = devices * sites
    both = 2 * size
    for s, piece in enumerate(pieces):
        for part in range(2):
            for g in range(groups):
                for x in range(sites):
                    at = part * size + s * sites + x
                    lines[g, pl.ds(at, SUB, stride=both), :] = piece[0, part, g, x * SUB : (x + 1) * SUB, :]
    for g in range(groups):
        for quad in range(2):
            tiles = [lines[g, (quad * 4 + j) * both : (quad * 4 + j + 1) * both, :] for j in range(4)]
            result = left_dot(table_f[...], jnp.concatenate(tiles, axis=1))
            for j in range(4):
                hat = result[:, j * LANES : (j + 1) * LANES]
                if narrow:
                    turned = pltpu.roll(hat, LANES // 2, axis=1)
                    places = ((quad, j, hat), (quad, j + SUB // 2, turned))
                else:
                    places = ((g, quad * 4 + j, hat),)
                for field, c, value in places:
                    hats[field * SUB + c] = value
                    if field:
                        hats[2 * SUB + c] = -value

    def channel(c, carry):
        def pair(p, totals):
            i = pairs[c, 2 * p]
            j = pairs[c, 2 * p + 1] + jnp.where(signs[c, p] < 0, 2 * SUB, SUB)
            a_re, a_im = hats[i, 0:size, :], hats[i, size:both, :]
            b_re, b_im = hats[j, 0:size, :], hats[j, size:both, :]
            return (
                totals[0] + (a_re * b_re + a_im * b_im),
                totals[1] + (a_im * b_re - a_re * b_im),
            )

        zero = jnp.zeros((size, LANES), jnp.float32)
        real, imag = lax.fori_loop(0, count, pair, (zero, zero), unroll=2)
        mixed[c, 0:size, :] = real
        mixed[c, size:both, :] = imag
        return carry

    lax.fori_loop(0, channels, channel, 0)
    if narrow:
        tiles = []
        for c in range(0, channels, 2):
            other = pltpu.roll(mixed[c + 1], LANES // 2, axis=1)
            tiles.append(jnp.where(lane_index(other.shape) < LANES // 2, mixed[c], other))
    else:
        tiles = [mixed[c] for c in range(channels)]
    result = left_dot(table_i[...], jnp.concatenate(tiles, axis=1))
    each_site = 2 * len(tiles)
    for t in range(len(tiles)):
        for part in range(2):
            value = result[part * size : (part + 1) * size, t * LANES : (t + 1) * LANES]
            first = 2 * t + part if narrow else part * channels + t
            rows[pl.ds(first, size, stride=each_site), :] = value
    for s in range(devices):
        out[s, 0] = rows[s * sites * each_site : (s + 1) * sites * each_site, :]


def middle(pieces, pairs, signs, table_f, table_i, sites, channels, narrow):
    size = table_f.shape[0] // 2
    devices = size // sites
    steps = pieces[0].shape[1]
    smem = pl.BlockSpec(memory_space=pltpu.SMEM)
    whole = lambda value: pl.BlockSpec(value.shape, lambda r: (0,) * value.ndim)
    third = lambda value: pl.BlockSpec(
        value.shape[:1] + (1,) + value.shape[2:], lambda r: (0, r) + (0,) * (value.ndim - 2)
    )
    rows = sites * (channels if narrow else 2 * channels)
    groups = 1 if narrow else 2
    return pl.pallas_call(
        functools.partial(middle_kernel, narrow, len(pieces), devices, sites, channels, signs.shape[1]),
        grid=(steps,),
        in_specs=[smem, smem] + [third(v) for v in pieces] + [whole(table_f), whole(table_i)],
        out_specs=pl.BlockSpec((devices, 1, rows, LANES), lambda r: (0, r, 0, 0)),
        out_shape=jax.ShapeDtypeStruct((devices, steps, rows, LANES), jnp.float32),
        scratch_shapes=[
            pltpu.VMEM((groups, SUB * 2 * size, LANES), jnp.float32),
            pltpu.VMEM((3 * SUB, 2 * size, LANES), jnp.float32),
            pltpu.VMEM((channels, 2 * size, LANES), jnp.float32),
            pltpu.VMEM((devices * rows, LANES), jnp.float32),
        ],
        compiler_params=pltpu.CompilerParams(vmem_limit_bytes=GRANT),
        cost_estimate=pl.CostEstimate(flops=4 * 10**9, bytes_accessed=10 * 10**6, transcendentals=0),
        name="middle_narrow" if narrow else "middle_wide",
    )(pairs, signs, *pieces, table_f, table_i)


def inverse_kernel(narrow, arrays, devices, channels, pairs_y, *refs):
    pieces, refs = each(refs[:arrays]), refs[arrays:]
    if narrow:
        table, depth, out, lines = refs
        staged = out.at[0]
    else:
        partial, table, depth, out, lines, staged = refs
    x = pl.program_id(0)
    thirds = pieces[0].shape[0]
    size = thirds * devices

    @pl.when(x == 0)
    def _():
        for s in range(devices):
            for r in range(thirds):
                for v in range(pieces[s].shape[1] // SUB):
                    start = v * SUB * size + r * devices + s
                    lines[pl.ds(start, SUB, stride=size), :] = pieces[s][r, v * SUB : (v + 1) * SUB, :]

    def tile(*spots):
        return jnp.concatenate([lines[pl.ds(pl.multiple_of(k * size, SUB), size), :] for k in spots], axis=0)

    if narrow:
        tiles = [tile(x * channels + 2 * c, x * channels + 2 * c + 1) for c in range(channels // 2)]
        width, sets = LANES // 4, [range(parity, channels, 2) for parity in range(2)]
    else:
        big = 2 * x * channels
        tiles = [tile(big + c, big + channels + c) for c in range(channels)]
        width, sets = LANES // 2, [range(channels)]
    result = left_dot(table[...], jnp.concatenate(tiles, axis=1))
    half = result.shape[0] // 2
    first, second = result[:half], result[half:]
    high, low = split(jnp.where(lane_index(first.shape) & width == 0, first, second))

    def rows_of(value, e, c):
        spot = c // 2 if narrow else c
        return jnp.concatenate(
            [
                value[(2 * part + e) * pairs_y : (2 * part + e + 1) * pairs_y, spot * LANES : (spot + 1) * LANES]
                for part in range(2)
            ],
            axis=1,
        )

    for k, members in enumerate(sets):
        products = []
        for e in range(2):
            left = [jnp.concatenate([rows_of(value, e, c) for c in members], axis=0) for value in (high, low)]
            products.append(dot(jnp.concatenate([left[0], left[1], left[0]], axis=1), depth[k, e]))
        for i, c in enumerate(members):
            rows = slice(i * pairs_y, (i + 1) * pairs_y)
            zero, one = products[0][rows], products[1][rows]
            for q, value in enumerate((zero[:, :LANES], zero[:, LANES:] + one[:, :LANES], one[:, LANES:])):
                staged[q, pl.ds(c, pairs_y, stride=channels), :] = value
    if not narrow:
        for p in range(pairs_y):
            rows = slice(p * channels, (p + 1) * channels)
            for q in range(3):
                lanes = slice((3 * p + q) * LANES, (3 * p + q + 1) * LANES)
                out[0, 0, :, lanes] = staged[q, rows, :] + partial[0, q, rows, :]


def inverse(pieces, partial, table, depth, sites, channels, flat):
    narrow = partial is None
    size = table.shape[1] // 6
    devices = size // pieces[0].shape[1]
    whole = lambda value: pl.BlockSpec(value.shape, lambda x: (0,) * value.ndim)
    tiles = (3, size * channels, LANES)
    lines = pltpu.VMEM((sites * pieces[0].shape[2] // sites * size, LANES), jnp.float32)
    kept = pl.BlockSpec((1,) + tiles, lambda x: (x, 0, 0, 0))
    return pl.pallas_call(
        functools.partial(inverse_kernel, narrow, len(pieces), devices, channels, size),
        grid=(sites,),
        in_specs=[whole(v) for v in pieces] + ([] if narrow else [kept]) + [whole(table), whole(depth)],
        out_specs=kept if narrow else pl.BlockSpec((1, 1, channels, flat), lambda x: (0, x, 0, 0)),
        out_shape=jax.ShapeDtypeStruct((sites,) + tiles if narrow else (1, sites, channels, flat), jnp.float32),
        scratch_shapes=[lines] if narrow else [lines, pltpu.VMEM(tiles, jnp.float32)],
        compiler_params=pltpu.CompilerParams(vmem_limit_bytes=GRANT),
        cost_estimate=pl.CostEstimate(flops=4 * 10**9, bytes_accessed=6 * 10**6, transcendentals=0),
        name="inverse_narrow" if narrow else "inverse_wide",
    )(*pieces, *([] if narrow else [partial]), table, depth)


AT_ONCE = dict(sent_narrow=True, sent_wide=True, back_narrow=True, back_wide=True)


def exchange(packed, at_once):
    if at_once:
        return [lax.all_to_all(packed, "space", 0, 0, tiled=True)]
    devices = packed.shape[0]
    order = sorted(range(1, devices), key=lambda s: (s % 4, -(s // 8), s))
    got = [packed[:1]] + [None] * (devices - 1)
    for s in order:
        got[s] = lax.ppermute(packed[s : s + 1], "space", [(i, i ^ s) for i in range(devices)])
    return got


def fast_slice(field_a, field_b, pairs, signs, tables):
    _, sites, components, flat = field_a.shape
    devices = lax.axis_size("space")
    channels = pairs.shape[0]
    me = lax.axis_index("space")
    mine = [lax.dynamic_index_in_dim(jnp.asarray(t), me, 0, False) for t in tables[:4]]
    fixed = [jnp.asarray(t[0]) for t in tables[:4]]

    def table(which, name):
        return (fixed if AT_ONCE[name] else mine)[which]

    depth_n, depth_w, depth_in, depth_iw = (jnp.asarray(t) for t in tables[4:])
    thirds = tables[0].shape[1] // 4 // devices
    flat_pairs = pairs.reshape(channels, -1)
    sent = {}
    token = signs
    for narrow, depth in ((True, depth_n), (False, depth_w)):
        name = "sent_narrow" if narrow else "sent_wide"
        groups = 1 if narrow else 2
        packed = forward(field_a, field_b, depth, table(0, name), narrow, token)
        token = packed[:SUB]
        packed = packed.reshape(devices, thirds, 2, groups, sites * SUB, LANES)
        sent[narrow] = exchange(packed, AT_ONCE[name])
    result = None
    for narrow, depth in ((True, depth_in), (False, depth_iw)):
        come, go = ("sent_narrow", "back_narrow") if narrow else ("sent_wide", "back_wide")
        mixed = middle(sent[narrow], flat_pairs, signs, table(2, come), table(3, go), sites, channels, narrow)
        back = exchange(mixed, AT_ONCE[go])
        result = inverse(back, result, table(1, go), depth, sites, channels, flat)
    return result


def neighbours(value):
    devices, length = lax.axis_size("tm"), value.shape[0]
    up = [(i, (i + 1) % devices) for i in range(devices)]
    down = [(j, i) for i, j in up]
    after = lax.ppermute(value[:1], "tm", down)
    before = after if devices == 2 and length == 1 else lax.ppermute(value[-1:], "tm", up)
    later = jnp.concatenate([value[1:], after], axis=0)
    earlier = jnp.concatenate([before, value[:-1]], axis=0)
    return later, earlier


def differences(correlator):
    later, earlier = neighbours(correlator)
    return correlator, later - correlator, later - 2.0 * correlator + earlier


def fast_device(tables, field_a, field_b, pairs, signs):
    field_a, field_b = field_a.swapaxes(1, 2), field_b.swapaxes(1, 2)
    parts = [
        fast_slice(field_a[t : t + 1], field_b[t : t + 1], pairs, signs, tables)
        for t in range(field_a.shape[0])
    ]
    return tuple(out.swapaxes(1, 2) for out in differences(jnp.concatenate(parts, axis=0)))


def dft_tables(length):
    cos, sin = unitary(length)
    return jnp.asarray(cos, jnp.float32), jnp.asarray(sin, jnp.float32)


def swap_parts(values):
    half = values.shape[-1] // 2
    return jnp.concatenate([values[..., half:], -values[..., :half]], axis=-1)


def along_depth(values, inverse):
    cosines, sines = dft_tables(values.shape[-1] // 2)
    matrix = jnp.block([[cosines, -sines], [sines, cosines]])
    if inverse:
        return jnp.einsum("tcxyr,kr->tcxyk", values, matrix, precision=highest)
    return jnp.einsum("tcxyr,rk->tcxyk", values, matrix, precision=highest)


def along(values, sign, axis):
    cosines, sines = dft_tables(values.shape[axis])
    table = jnp.concatenate([cosines, sign * sines], axis=1)
    stacked = jnp.concatenate([values, swap_parts(values)], axis=axis)
    spec = "ky,tcxyr->tcxkr" if axis == 3 else "kx,tcxyr->tckyr"
    return jnp.einsum(spec, table, stacked, precision=highest)


def contract(weights, hat_a, hat_b):
    depth = hat_a.shape[-1] // 2
    outputs = []
    for channel in range(weights.shape[0]):
        mixed_b = jnp.einsum("ij,tjxyk->tixyk", weights[channel], hat_b, precision=highest)
        direct = jnp.sum(hat_a * mixed_b, axis=1)
        crossed = jnp.sum(hat_a * swap_parts(mixed_b), axis=1)
        real_part = direct[..., :depth] + direct[..., depth:]
        imag_part = -(crossed[..., :depth] + crossed[..., depth:])
        outputs.append(jnp.concatenate([real_part, imag_part], axis=-1))
    return jnp.stack(outputs, axis=1)


def any_device(depth, field_a, field_b, pairs, signs):
    as_five = lambda v: v.reshape(v.shape[:3] + (-1, 2 * depth))
    as_four = lambda v: v.reshape(v.shape[:3] + (-1,))
    indices = jnp.arange(field_a.shape[1], dtype=jnp.int32)
    first = (pairs[:, :, 0][:, :, None] == indices).astype(jnp.float32)
    second = (pairs[:, :, 1][:, :, None] == indices).astype(jnp.float32)
    weights = jnp.einsum("cp,cpi,cpj->cij", signs.astype(jnp.float32), first, second, precision=highest)
    hats = []
    for field in (field_a, field_b):
        partial = as_four(along(along_depth(as_five(field), False), 1.0, 3))
        lines = lax.all_to_all(partial, "space", split_axis=3, concat_axis=2, tiled=True)
        hats.append(along(as_five(lines), 1.0, 2))
    returned = as_four(along(contract(weights, *hats), -1.0, 2))
    sites = lax.all_to_all(returned, "space", split_axis=2, concat_axis=3, tiled=True)
    return differences(as_four(along_depth(along(as_five(sites), -1.0, 3), True)))


def solution(mesh):
    devices = mesh.shape["space"]
    times = mesh.shape["tm"]

    def program(field_a, field_b, pairs, signs):
        _, components, size, flat = field_a.shape
        depth = flat // size // 2
        wide = LANES // 2
        fits = (
            depth == size
            and 2 * depth == 3 * wide
            and components == SUB
            and pairs.shape[0] == 4
            and size % (2 * devices) == 0
            and devices & (devices - 1) == 0
            and (size // devices) * 4 % SUB == 0
            and size % (2 * SUB) == 0
        )
        if fits:
            tables = (
                rows_forward(devices, size),
                rows_inverse(devices, size),
                columns_forward(devices, size),
                columns_inverse(devices, size),
                depth_forward(depth, wide, depth - wide),
                depth_forward(depth, 0, wide),
                depth_inverse(depth, wide, depth - wide, 2),
                depth_inverse(depth, 0, wide, 1),
            )
            per_device = functools.partial(fast_device, tables)
        else:
            per_device = functools.partial(any_device, depth)
        spec = P("tm", None, "space", None)
        return jax.shard_map(
            per_device,
            mesh=mesh,
            in_specs=(spec, spec, P(), P()),
            out_specs=(spec, spec, spec),
            check_vma=False,
        )(field_a, field_b, pairs, signs)

    return program
```

```python
import functools
import math

import jax
import jax.numpy as jnp
import ml_dtypes
import numpy as np
from jax import lax
from jax.experimental import pallas as pl
from jax.experimental.pallas import tpu as pltpu
from jax.sharding import PartitionSpec as P

highest = lax.Precision.HIGHEST
LANES = 128
SUB = 8
GRANT = 56 << 20
SMALL_GRANT = 24 << 20


def unitary(length):
    index = np.arange(length)
    angle = (index[:, None] * index[None, :] % length) * (2.0 * np.pi / length)
    return np.cos(angle) / math.sqrt(length), np.sin(angle) / math.sqrt(length)


def halves(table):
    high = table.astype(np.float32).astype(ml_dtypes.bfloat16)
    low = (table - high.astype(np.float64)).astype(np.float32).astype(ml_dtypes.bfloat16)
    return high, low


def left_table(table):
    high, low = halves(table)
    return np.concatenate([high, high, low], axis=1)


def right_table(table):
    high, low = halves(table)
    return np.concatenate([high, high, low], axis=0)


def owned(devices, length):
    each = length // devices
    me = np.arange(devices)
    return ((me[:, None] ^ me[None, :]) * each)[:, :, None] + np.arange(each)


def rows_forward(devices, length):
    cos, sin = unitary(length)
    out = []
    for spots in owned(devices, length):
        k = spots.reshape(devices, -1, 2).transpose(2, 0, 1).reshape(-1)
        y = np.arange(length).reshape(-1, 2).T.reshape(-1)
        c, s = cos[k][:, y], sin[k][:, y]
        out.append(left_table(np.block([[c, s], [-s, c]])))
    return np.stack(out)


def rows_inverse(devices, length):
    cos, sin = unitary(length)
    out = []
    for spots in owned(devices, length):
        y = np.arange(length).reshape(-1, 2).T.reshape(-1)
        blocks = []
        for e in range(2):
            k = spots.reshape(devices, -1, 2)[:, :, e].T.reshape(-1)
            c, s = cos[y][:, k], sin[y][:, k]
            blocks.append(np.block([[c, -s], [s, c]]))
        out.append(left_table(np.concatenate(blocks)))
    return np.stack(out)


def columns_forward(devices, length):
    cos, sin = unitary(length)
    out = []
    for spots in owned(devices, length):
        c, s = cos[:, spots.reshape(-1)], sin[:, spots.reshape(-1)]
        out.append(left_table(np.block([[c, s], [-s, c]])))
    return np.stack(out)


def columns_inverse(devices, length):
    cos, sin = unitary(length)
    out = []
    for spots in owned(devices, length):
        c, s = cos[spots.reshape(-1)], sin[spots.reshape(-1)]
        out.append(left_table(np.block([[c, -s], [s, c]])))
    return np.stack(out)


def depth_forward(length, first, count):
    cos, sin = unitary(length)
    k = np.tile(np.arange(first, first + count), LANES // count)
    matrix = np.block([[cos[:, k], -sin[:, k]], [sin[:, k], cos[:, k]]])
    gap = np.zeros((2 * LANES - 2 * length, 2 * LANES))
    both = np.stack([np.concatenate([matrix, gap]), np.concatenate([gap, matrix])])
    return np.stack([right_table(b) for b in both])


def depth_inverse(length, first, count, halves_of):
    cos, sin = unitary(length)
    k = np.tile(np.arange(first, first + count), LANES // count)
    out = []
    for half in range(halves_of):
        keep = (np.arange(LANES) * halves_of // LANES == half)[:, None] * 1.0
        matrix = np.block([[cos[k] * keep, sin[k] * keep], [-sin[k] * keep, cos[k] * keep]])
        gap = np.zeros((matrix.shape[0], 2 * LANES - 2 * length))
        both = (np.concatenate([matrix, gap], axis=1), np.concatenate([gap, matrix], axis=1))
        out.append(np.stack([right_table(b) for b in both]))
    return np.stack(out)


def split(value):
    high = value.astype(jnp.bfloat16)
    return high, (value - high.astype(jnp.float32)).astype(jnp.bfloat16)


def dot(left, right):
    return jnp.dot(left, right, preferred_element_type=jnp.float32)


def left_dot(table, value):
    high, low = split(value)
    return dot(table, jnp.concatenate([high, low, high], axis=0))


def lane_index(shape):
    return lax.broadcasted_iota(jnp.int32, shape, len(shape) - 1)


def forward_kernel(narrow, sites, pairs_y, field_a, field_b, depth, table, token, out, packed, *spectra):
    for site in range(field_a.shape[1]):
        spaces = spectra[2 * site], spectra[2 * site + 1]
        forward_site(narrow, pairs_y, field_a.at[0, site], field_b.at[0, site], depth, table, packed.at[site], spaces)
        for block in range(out.shape[0]):
            out[block, site] = packed[site, block * SUB : (block + 1) * SUB, :]


def forward_site(narrow, pairs_y, field_a, field_b, depth, table, packed, spectra):
    groups = 1 if narrow else 2
    width = LANES // 4 if narrow else LANES // 2
    block = 2 * groups * SUB
    slots = []
    for group, field in enumerate((field_a, field_b)):
        tiles = [
            jnp.concatenate(
                [field[:, (3 * p + q) * LANES : (3 * p + q + 1) * LANES] for p in range(pairs_y)], axis=0
            )
            for q in range(3)
        ]
        tiles = [split(tile) for tile in tiles]
        for e in range(2):
            left = [tiles[e + k][part] for part in (0, 1, 0) for k in range(2)]
            result = dot(jnp.concatenate(left, axis=1), depth[e])
            for part in range(2):
                spectra[group][part * 2 + e] = result[:, part * LANES : (part + 1) * LANES]

        def rows_of(c, group=group):
            return jnp.concatenate(
                [spectra[group][k, pl.ds(c, pairs_y, stride=SUB), :] for k in range(4)], axis=0
            )

        if narrow:
            for c in range(SUB // 2):
                first, second = rows_of(c), rows_of(c + SUB // 2)
                pick = lane_index(first.shape) < LANES // 2
                slots.append((0, group * 4 + c, jnp.where(pick, first, second)))
        else:
            slots += [(group, c, rows_of(c)) for c in range(SUB)]

    for first in range(0, len(slots), SUB):
        batch = slots[first : first + SUB]
        result = left_dot(table[...], jnp.concatenate([value for _, _, value in batch], axis=1))
        half = result.shape[0] // 4
        for part in range(2):
            even = result[2 * part * half : (2 * part + 1) * half]
            odd = result[(2 * part + 1) * half : (2 * part + 2) * half]
            merged = jnp.where(lane_index(even.shape) // width % 2 == 0, even, odd)
            for i, (group, slot, _) in enumerate(batch):
                start = (part * groups + group) * SUB + slot
                packed[pl.ds(start, half, stride=block), :] = merged[:, i * LANES : (i + 1) * LANES]


def forward(field_a, field_b, depth, table, narrow, token):
    _, sites, components, flat = field_a.shape
    groups = 1 if narrow else 2
    size = table.shape[0] // 2
    pairs_y = size // 2
    lines = size // 2
    blocks = lines * 2 * groups
    step = 1
    spot = pl.BlockSpec((1, step, components, flat), lambda x: (0, x, 0, 0))
    whole = lambda value: pl.BlockSpec(value.shape, lambda x: (0,) * value.ndim)
    return pl.pallas_call(
        functools.partial(forward_kernel, narrow, sites, pairs_y),
        grid=(sites // step,),
        in_specs=[spot, spot, whole(depth), whole(table), pl.BlockSpec(memory_space=pl.ANY)],
        out_specs=pl.BlockSpec((blocks, step, SUB, LANES), lambda x: (0, x, 0, 0)),
        out_shape=jax.ShapeDtypeStruct((blocks, sites, SUB, LANES), jnp.float32),
        scratch_shapes=[pltpu.VMEM((step, blocks * SUB, LANES), jnp.float32)]
        + [pltpu.VMEM((4, pairs_y * SUB, LANES), jnp.float32)] * (2 * step),
        compiler_params=pltpu.CompilerParams(vmem_limit_bytes=GRANT),
        cost_estimate=pl.CostEstimate(flops=8 * 10**9, bytes_accessed=12 * 10**6, transcendentals=0),
        name="forward_narrow" if narrow else "forward_wide",
    )(field_a, field_b, depth, table, token)


def placed(space, *values):
    return [pltpu.with_memory_space_constraint(value, space) for value in values]


def each(refs):
    return [ref.at[i] for ref in refs for i in range(ref.shape[0])]


def middle_kernel(narrow, arrays, devices, sites, channels, count, pairs, signs, *refs):
    pieces, refs = each(refs[:arrays]), refs[arrays:]
    table_f, table_i, out, lines, hats, mixed, rows = refs
    groups = 1 if narrow else 2
    size = devices * sites
    both = 2 * size
    for s, piece in enumerate(pieces):
        for part in range(2):
            for g in range(groups):
                for x in range(sites):
                    at = part * size + s * sites + x
                    lines[g, pl.ds(at, SUB, stride=both), :] = piece[0, part, g, x * SUB : (x + 1) * SUB, :]
    for g in range(groups):
        for quad in range(2):
            tiles = [lines[g, (quad * 4 + j) * both : (quad * 4 + j + 1) * both, :] for j in range(4)]
            result = left_dot(table_f[...], jnp.concatenate(tiles, axis=1))
            for j in range(4):
                hat = result[:, j * LANES : (j + 1) * LANES]
                if narrow:
                    turned = pltpu.roll(hat, LANES // 2, axis=1)
                    places = ((quad, j, hat), (quad, j + SUB // 2, turned))
                else:
                    places = ((g, quad * 4 + j, hat),)
                for field, c, value in places:
                    hats[field * SUB + c] = value
                    if field:
                        hats[2 * SUB + c] = -value

    def channel(c, carry):
        def pair(p, totals):
            i = pairs[c, 2 * p]
            j = pairs[c, 2 * p + 1] + jnp.where(signs[c, p] < 0, 2 * SUB, SUB)
            a_re, a_im = hats[i, 0:size, :], hats[i, size:both, :]
            b_re, b_im = hats[j, 0:size, :], hats[j, size:both, :]
            return (
                totals[0] + (a_re * b_re + a_im * b_im),
                totals[1] + (a_im * b_re - a_re * b_im),
            )

        zero = jnp.zeros((size, LANES), jnp.float32)
        real, imag = lax.fori_loop(0, count, pair, (zero, zero), unroll=4)
        mixed[c, 0:size, :] = real
        mixed[c, size:both, :] = imag
        return carry

    lax.fori_loop(0, channels, channel, 0)
    if narrow:
        tiles = []
        for c in range(0, channels, 2):
            other = pltpu.roll(mixed[c + 1], LANES // 2, axis=1)
            tiles.append(jnp.where(lane_index(other.shape) < LANES // 2, mixed[c], other))
    else:
        tiles = [mixed[c] for c in range(channels)]
    result = left_dot(table_i[...], jnp.concatenate(tiles, axis=1))
    each_site = 2 * len(tiles)
    for t in range(len(tiles)):
        for part in range(2):
            value = result[part * size : (part + 1) * size, t * LANES : (t + 1) * LANES]
            first = 2 * t + part if narrow else part * channels + t
            rows[pl.ds(first, size, stride=each_site), :] = value
    for s in range(devices):
        out[s, 0] = rows[s * sites * each_site : (s + 1) * sites * each_site, :]


def middle(pieces, pairs, signs, table_f, table_i, sites, channels, narrow):
    size = table_f.shape[0] // 2
    devices = size // sites
    steps = pieces[0].shape[1]
    smem = pl.BlockSpec(memory_space=pltpu.SMEM)
    whole = lambda value: pl.BlockSpec(value.shape, lambda r: (0,) * value.ndim)
    third = lambda value: pl.BlockSpec(
        value.shape[:1] + (1,) + value.shape[2:], lambda r: (0, r) + (0,) * (value.ndim - 2)
    )
    rows = sites * (channels if narrow else 2 * channels)
    groups = 1 if narrow else 2
    return pl.pallas_call(
        functools.partial(middle_kernel, narrow, len(pieces), devices, sites, channels, signs.shape[1]),
        grid=(steps,),
        in_specs=[smem, smem] + [third(v) for v in pieces] + [whole(table_f), whole(table_i)],
        out_specs=pl.BlockSpec((devices, 1, rows, LANES), lambda r: (0, r, 0, 0)),
        out_shape=jax.ShapeDtypeStruct((devices, steps, rows, LANES), jnp.float32),
        scratch_shapes=[
            pltpu.VMEM((groups, SUB * 2 * size, LANES), jnp.float32),
            pltpu.VMEM((3 * SUB, 2 * size, LANES), jnp.float32),
            pltpu.VMEM((channels, 2 * size, LANES), jnp.float32),
            pltpu.VMEM((devices * rows, LANES), jnp.float32),
        ],
        compiler_params=pltpu.CompilerParams(vmem_limit_bytes=SMALL_GRANT),
        cost_estimate=pl.CostEstimate(flops=4 * 10**9, bytes_accessed=10 * 10**6, transcendentals=0),
        name="middle_narrow" if narrow else "middle_wide",
    )(pairs, signs, *placed(pltpu.VMEM if narrow else pltpu.HBM, *pieces), *placed(pltpu.HBM, table_f, table_i))


def inverse_kernel(narrow, arrays, devices, channels, pairs_y, *refs):
    pieces, refs = each(refs[:arrays]), refs[arrays:]
    if narrow:
        table, depth, out, lines = refs
        staged = partial = out
    else:
        partial, table, depth, out, lines, staged = refs
    thirds = pieces[0].shape[0]
    size = thirds * devices

    @pl.when(pl.program_id(0) == 0)
    def _():
        for s in range(devices):
            for r in range(thirds):
                for v in range(pieces[s].shape[1] // SUB):
                    start = v * SUB * size + r * devices + s
                    lines[pl.ds(start, SUB, stride=size), :] = pieces[s][r, v * SUB : (v + 1) * SUB, :]

    step = partial.shape[0]
    for site in range(step):
        x = pl.program_id(0) * step + site
        place = None if narrow else out.at[0, site]
        inverse_site(narrow, channels, pairs_y, size, x, lines, table, depth, staged.at[site], partial.at[site], place)


def inverse_site(narrow, channels, pairs_y, size, x, lines, table, depth, staged, partial, out):
    def tile(*spots):
        return jnp.concatenate([lines[pl.ds(pl.multiple_of(k * size, SUB), size), :] for k in spots], axis=0)

    if narrow:
        tiles = [tile(x * channels + 2 * c, x * channels + 2 * c + 1) for c in range(channels // 2)]
        width, sets = LANES // 4, [range(parity, channels, 2) for parity in range(2)]
    else:
        big = 2 * x * channels
        tiles = [tile(big + c, big + channels + c) for c in range(channels)]
        width, sets = LANES // 2, [range(channels)]
    result = left_dot(table[...], jnp.concatenate(tiles, axis=1))
    half = result.shape[0] // 2
    first, second = result[:half], result[half:]
    high, low = split(jnp.where(lane_index(first.shape) & width == 0, first, second))

    def rows_of(value, e, c):
        spot = c // 2 if narrow else c
        return jnp.concatenate(
            [
                value[(2 * part + e) * pairs_y : (2 * part + e + 1) * pairs_y, spot * LANES : (spot + 1) * LANES]
                for part in range(2)
            ],
            axis=1,
        )

    for k, members in enumerate(sets):
        products = []
        for e in range(2):
            left = [jnp.concatenate([rows_of(value, e, c) for c in members], axis=0) for value in (high, low)]
            products.append(dot(jnp.concatenate([left[0], left[1], left[0]], axis=1), depth[k, e]))
        for i, c in enumerate(members):
            rows = slice(i * pairs_y, (i + 1) * pairs_y)
            zero, one = products[0][rows], products[1][rows]
            for q, value in enumerate((zero[:, :LANES], zero[:, LANES:] + one[:, :LANES], one[:, LANES:])):
                staged[q, pl.ds(c, pairs_y, stride=channels), :] = value
    if not narrow:
        for p in range(pairs_y):
            rows = slice(p * channels, (p + 1) * channels)
            for q in range(3):
                lanes = slice((3 * p + q) * LANES, (3 * p + q + 1) * LANES)
                out[:, lanes] = staged[q, rows, :] + partial[q, rows, :]


def inverse(pieces, partial, table, depth, sites, channels, flat):
    narrow = partial is None
    size = table.shape[1] // 6
    devices = size // pieces[0].shape[1]
    whole = lambda value: pl.BlockSpec(value.shape, lambda x: (0,) * value.ndim)
    tiles = (3, size * channels, LANES)
    lines = pltpu.VMEM((sites * pieces[0].shape[2] // sites * size, LANES), jnp.float32)
    step = 3 if sites % 3 == 0 else 1
    kept = pl.BlockSpec((step,) + tiles, lambda x: (x, 0, 0, 0))
    return pl.pallas_call(
        functools.partial(inverse_kernel, narrow, len(pieces), devices, channels, size),
        grid=(sites // step,),
        in_specs=[whole(v) for v in pieces] + ([] if narrow else [kept]) + [whole(table), whole(depth)],
        out_specs=kept if narrow else pl.BlockSpec((1, step, channels, flat), lambda x: (0, x, 0, 0)),
        out_shape=jax.ShapeDtypeStruct((sites,) + tiles if narrow else (1, sites, channels, flat), jnp.float32),
        scratch_shapes=[lines] if narrow else [lines, pltpu.VMEM((step,) + tiles, jnp.float32)],
        compiler_params=pltpu.CompilerParams(vmem_limit_bytes=SMALL_GRANT),
        cost_estimate=pl.CostEstimate(flops=4 * 10**9, bytes_accessed=6 * 10**6, transcendentals=0),
        name="inverse_narrow" if narrow else "inverse_wide",
    )(*placed(pltpu.VMEM, *pieces), *([] if narrow else placed(pltpu.HBM, partial)), *placed(pltpu.HBM, table, depth))


AT_ONCE = dict(sent_narrow=True, sent_wide=True, back_narrow=True, back_wide=True)


def exchange(packed, at_once):
    if at_once:
        return [lax.all_to_all(packed, "space", 0, 0, tiled=True)]
    devices = packed.shape[0]
    order = sorted(range(1, devices), key=lambda s: (s % 4, -(s // 8), s))
    got = [packed[:1]] + [None] * (devices - 1)
    for s in order:
        got[s] = lax.ppermute(packed[s : s + 1], "space", [(i, i ^ s) for i in range(devices)])
    return got


def fast_slice(field_a, field_b, pairs, signs, tables):
    _, sites, components, flat = field_a.shape
    devices = lax.axis_size("space")
    channels = pairs.shape[0]
    me = lax.axis_index("space")
    mine = [lax.dynamic_index_in_dim(jnp.asarray(t), me, 0, False) for t in tables[:4]]
    fixed = [jnp.asarray(t[0]) for t in tables[:4]]

    def table(which, name):
        return (fixed if AT_ONCE[name] else mine)[which]

    depth_n, depth_w, depth_in, depth_iw = (jnp.asarray(t) for t in tables[4:])
    thirds = tables[0].shape[1] // 4 // devices
    flat_pairs = pairs.reshape(channels, -1)
    sent = {}
    token = signs
    for narrow, depth in ((True, depth_n), (False, depth_w)):
        name = "sent_narrow" if narrow else "sent_wide"
        groups = 1 if narrow else 2
        packed = forward(field_a, field_b, depth, table(0, name), narrow, token)
        token = packed[0, 0]
        packed = packed.reshape(devices, thirds, 2, groups, sites * SUB, LANES)
        sent[narrow] = exchange(packed, AT_ONCE[name])
    result = None
    for narrow, depth in ((True, depth_in), (False, depth_iw)):
        come, go = ("sent_narrow", "back_narrow") if narrow else ("sent_wide", "back_wide")
        mixed = middle(sent[narrow], flat_pairs, signs, table(2, come), table(3, go), sites, channels, narrow)
        back = exchange(mixed, AT_ONCE[go])
        result = inverse(back, result, table(1, go), depth, sites, channels, flat)
    return result


def neighbours(value):
    devices, length = lax.axis_size("tm"), value.shape[0]
    up = [(i, (i + 1) % devices) for i in range(devices)]
    down = [(j, i) for i, j in up]
    after = lax.ppermute(value[:1], "tm", down)
    before = after if devices == 2 and length == 1 else lax.ppermute(value[-1:], "tm", up)
    later = jnp.concatenate([value[1:], after], axis=0)
    earlier = jnp.concatenate([before, value[:-1]], axis=0)
    return later, earlier


def differences(correlator):
    later, earlier = neighbours(correlator)
    return correlator, later - correlator, later - 2.0 * correlator + earlier


def fast_device(tables, field_a, field_b, pairs, signs):
    field_a, field_b = field_a.swapaxes(1, 2), field_b.swapaxes(1, 2)
    parts = [
        fast_slice(field_a[t : t + 1], field_b[t : t + 1], pairs, signs, tables)
        for t in range(field_a.shape[0])
    ]
    return tuple(out.swapaxes(1, 2) for out in differences(jnp.concatenate(parts, axis=0)))


def dft_tables(length):
    cos, sin = unitary(length)
    return jnp.asarray(cos, jnp.float32), jnp.asarray(sin, jnp.float32)


def swap_parts(values):
    half = values.shape[-1] // 2
    return jnp.concatenate([values[..., half:], -values[..., :half]], axis=-1)


def along_depth(values, inverse):
    cosines, sines = dft_tables(values.shape[-1] // 2)
    matrix = jnp.block([[cosines, -sines], [sines, cosines]])
    if inverse:
        return jnp.einsum("tcxyr,kr->tcxyk", values, matrix, precision=highest)
    return jnp.einsum("tcxyr,rk->tcxyk", values, matrix, precision=highest)


def along(values, sign, axis):
    cosines, sines = dft_tables(values.shape[axis])
    table = jnp.concatenate([cosines, sign * sines], axis=1)
    stacked = jnp.concatenate([values, swap_parts(values)], axis=axis)
    spec = "ky,tcxyr->tcxkr" if axis == 3 else "kx,tcxyr->tckyr"
    return jnp.einsum(spec, table, stacked, precision=highest)


def contract(weights, hat_a, hat_b):
    depth = hat_a.shape[-1] // 2
    outputs = []
    for channel in range(weights.shape[0]):
        mixed_b = jnp.einsum("ij,tjxyk->tixyk", weights[channel], hat_b, precision=highest)
        direct = jnp.sum(hat_a * mixed_b, axis=1)
        crossed = jnp.sum(hat_a * swap_parts(mixed_b), axis=1)
        real_part = direct[..., :depth] + direct[..., depth:]
        imag_part = -(crossed[..., :depth] + crossed[..., depth:])
        outputs.append(jnp.concatenate([real_part, imag_part], axis=-1))
    return jnp.stack(outputs, axis=1)


def any_device(depth, field_a, field_b, pairs, signs):
    as_five = lambda v: v.reshape(v.shape[:3] + (-1, 2 * depth))
    as_four = lambda v: v.reshape(v.shape[:3] + (-1,))
    indices = jnp.arange(field_a.shape[1], dtype=jnp.int32)
    first = (pairs[:, :, 0][:, :, None] == indices).astype(jnp.float32)
    second = (pairs[:, :, 1][:, :, None] == indices).astype(jnp.float32)
    weights = jnp.einsum("cp,cpi,cpj->cij", signs.astype(jnp.float32), first, second, precision=highest)
    hats = []
    for field in (field_a, field_b):
        partial = as_four(along(along_depth(as_five(field), False), 1.0, 3))
        lines = lax.all_to_all(partial, "space", split_axis=3, concat_axis=2, tiled=True)
        hats.append(along(as_five(lines), 1.0, 2))
    returned = as_four(along(contract(weights, *hats), -1.0, 2))
    sites = lax.all_to_all(returned, "space", split_axis=2, concat_axis=3, tiled=True)
    return differences(as_four(along_depth(along(as_five(sites), -1.0, 3), True)))


def solution(mesh):
    devices = mesh.shape["space"]
    times = mesh.shape["tm"]

    def program(field_a, field_b, pairs, signs):
        _, components, size, flat = field_a.shape
        depth = flat // size // 2
        wide = LANES // 2
        fits = (
            depth == size
            and 2 * depth == 3 * wide
            and components == SUB
            and pairs.shape[0] == 4
            and size % (2 * devices) == 0
            and devices & (devices - 1) == 0
            and (size // devices) * 4 % SUB == 0
            and size % (2 * SUB) == 0
        )
        if fits:
            tables = (
                rows_forward(devices, size),
                rows_inverse(devices, size),
                columns_forward(devices, size),
                columns_inverse(devices, size),
                depth_forward(depth, wide, depth - wide),
                depth_forward(depth, 0, wide),
                depth_inverse(depth, wide, depth - wide, 2),
                depth_inverse(depth, 0, wide, 1),
            )
            per_device = functools.partial(fast_device, tables)
        else:
            per_device = functools.partial(any_device, depth)
        spec = P("tm", None, "space", None)
        return jax.shard_map(
            per_device,
            mesh=mesh,
            in_specs=(spec, spec, P(), P()),
            out_specs=(spec, spec, spec),
            check_vma=False,
        )(field_a, field_b, pairs, signs)

    return program
```

```python
import functools
import math

import jax
import jax.numpy as jnp
import ml_dtypes
import numpy as np
from jax import lax
from jax.experimental import pallas as pl
from jax.experimental.pallas import tpu as pltpu
from jax.sharding import PartitionSpec as P

highest = lax.Precision.HIGHEST
LANES = 128
SUB = 8
GRANT = 56 << 20
SMALL_GRANT = 24 << 20


def unitary(length):
    index = np.arange(length)
    angle = (index[:, None] * index[None, :] % length) * (2.0 * np.pi / length)
    return np.cos(angle) / math.sqrt(length), np.sin(angle) / math.sqrt(length)


def halves(table):
    high = table.astype(np.float32).astype(ml_dtypes.bfloat16)
    low = (table - high.astype(np.float64)).astype(np.float32).astype(ml_dtypes.bfloat16)
    return high, low


def left_table(table):
    high, low = halves(table)
    return np.concatenate([high, high, low], axis=1)


def right_table(table):
    high, low = halves(table)
    return np.concatenate([high, high, low], axis=0)


def owned(devices, length):
    each = length // devices
    me = np.arange(devices)
    return ((me[:, None] ^ me[None, :]) * each)[:, :, None] + np.arange(each)


def rows_forward(devices, length):
    cos, sin = unitary(length)
    out = []
    for spots in owned(devices, length):
        k = spots.reshape(devices, -1, 2).transpose(2, 0, 1).reshape(-1)
        y = np.arange(length).reshape(-1, 2).T.reshape(-1)
        c, s = cos[k][:, y], sin[k][:, y]
        out.append(left_table(np.block([[c, s], [-s, c]])))
    return np.stack(out)


def rows_inverse(devices, length):
    cos, sin = unitary(length)
    out = []
    for spots in owned(devices, length):
        y = np.arange(length).reshape(-1, 2).T.reshape(-1)
        blocks = []
        for e in range(2):
            k = spots.reshape(devices, -1, 2)[:, :, e].T.reshape(-1)
            c, s = cos[y][:, k], sin[y][:, k]
            blocks.append(np.block([[c, -s], [s, c]]))
        out.append(left_table(np.concatenate(blocks)))
    return np.stack(out)


def columns_forward(devices, length):
    cos, sin = unitary(length)
    out = []
    for spots in owned(devices, length):
        c, s = cos[:, spots.reshape(-1)], sin[:, spots.reshape(-1)]
        out.append(left_table(np.block([[c, s], [-s, c]])))
    return np.stack(out)


def columns_inverse(devices, length):
    cos, sin = unitary(length)
    out = []
    for spots in owned(devices, length):
        c, s = cos[spots.reshape(-1)], sin[spots.reshape(-1)]
        out.append(left_table(np.block([[c, -s], [s, c]])))
    return np.stack(out)


def depth_forward(length, first, count):
    cos, sin = unitary(length)
    k = np.tile(np.arange(first, first + count), LANES // count)
    matrix = np.block([[cos[:, k], -sin[:, k]], [sin[:, k], cos[:, k]]])
    gap = np.zeros((2 * LANES - 2 * length, 2 * LANES))
    both = np.stack([np.concatenate([matrix, gap]), np.concatenate([gap, matrix])])
    return np.stack([right_table(b) for b in both])


def depth_inverse(length, first, count, halves_of):
    cos, sin = unitary(length)
    k = np.tile(np.arange(first, first + count), LANES // count)
    out = []
    for half in range(halves_of):
        keep = (np.arange(LANES) * halves_of // LANES == half)[:, None] * 1.0
        matrix = np.block([[cos[k] * keep, sin[k] * keep], [-sin[k] * keep, cos[k] * keep]])
        gap = np.zeros((matrix.shape[0], 2 * LANES - 2 * length))
        both = (np.concatenate([matrix, gap], axis=1), np.concatenate([gap, matrix], axis=1))
        out.append(np.stack([right_table(b) for b in both]))
    return np.stack(out)


def split(value):
    high = value.astype(jnp.bfloat16)
    return high, (value - high.astype(jnp.float32)).astype(jnp.bfloat16)


def dot(left, right):
    return jnp.dot(left, right, preferred_element_type=jnp.float32)


def left_dot(table, value):
    high, low = split(value)
    return dot(table, jnp.concatenate([high, low, high], axis=0))


def lane_index(shape):
    return lax.broadcasted_iota(jnp.int32, shape, len(shape) - 1)


def forward_kernel(narrow, sites, pairs_y, field_a, field_b, depth, table, token, out, packed, *spectra):
    for site in range(field_a.shape[1]):
        spaces = spectra[2 * site], spectra[2 * site + 1]
        forward_site(narrow, pairs_y, field_a.at[0, site], field_b.at[0, site], depth, table, packed.at[site], spaces)
        for block in range(out.shape[0]):
            out[block, site] = packed[site, block * SUB : (block + 1) * SUB, :]


def forward_site(narrow, pairs_y, field_a, field_b, depth, table, packed, spectra):
    groups = 1 if narrow else 2
    width = LANES // 4 if narrow else LANES // 2
    block = 2 * groups * SUB
    slots = []
    for group, field in enumerate((field_a, field_b)):
        tiles = [
            jnp.concatenate(
                [field[:, (3 * p + q) * LANES : (3 * p + q + 1) * LANES] for p in range(pairs_y)], axis=0
            )
            for q in range(3)
        ]
        tiles = [split(tile) for tile in tiles]
        for e in range(2):
            left = [tiles[e + k][part] for part in (0, 1, 0) for k in range(2)]
            result = dot(jnp.concatenate(left, axis=1), depth[e])
            for part in range(2):
                spectra[group][part * 2 + e] = result[:, part * LANES : (part + 1) * LANES]

        def rows_of(c, group=group):
            return jnp.concatenate(
                [spectra[group][k, pl.ds(c, pairs_y, stride=SUB), :] for k in range(4)], axis=0
            )

        if narrow:
            for c in range(SUB // 2):
                first, second = rows_of(c), rows_of(c + SUB // 2)
                pick = lane_index(first.shape) < LANES // 2
                slots.append((0, group * 4 + c, jnp.where(pick, first, second)))
        else:
            slots += [(group, c, rows_of(c)) for c in range(SUB)]

    for first in range(0, len(slots), SUB):
        batch = slots[first : first + SUB]
        result = left_dot(table[...], jnp.concatenate([value for _, _, value in batch], axis=1))
        half = result.shape[0] // 4
        for part in range(2):
            even = result[2 * part * half : (2 * part + 1) * half]
            odd = result[(2 * part + 1) * half : (2 * part + 2) * half]
            merged = jnp.where(lane_index(even.shape) // width % 2 == 0, even, odd)
            for i, (group, slot, _) in enumerate(batch):
                start = (part * groups + group) * SUB + slot
                packed[pl.ds(start, half, stride=block), :] = merged[:, i * LANES : (i + 1) * LANES]


def forward(field_a, field_b, depth, table, narrow, token):
    _, sites, components, flat = field_a.shape
    groups = 1 if narrow else 2
    size = table.shape[0] // 2
    pairs_y = size // 2
    lines = size // 2
    blocks = lines * 2 * groups
    step = 1
    spot = pl.BlockSpec((1, step, components, flat), lambda x: (0, x, 0, 0))
    whole = lambda value: pl.BlockSpec(value.shape, lambda x: (0,) * value.ndim)
    return pl.pallas_call(
        functools.partial(forward_kernel, narrow, sites, pairs_y),
        grid=(sites // step,),
        in_specs=[spot, spot, whole(depth), whole(table), pl.BlockSpec(memory_space=pl.ANY)],
        out_specs=pl.BlockSpec((blocks, step, SUB, LANES), lambda x: (0, x, 0, 0)),
        out_shape=jax.ShapeDtypeStruct((blocks, sites, SUB, LANES), jnp.float32),
        scratch_shapes=[pltpu.VMEM((step, blocks * SUB, LANES), jnp.float32)]
        + [pltpu.VMEM((4, pairs_y * SUB, LANES), jnp.float32)] * (2 * step),
        compiler_params=pltpu.CompilerParams(vmem_limit_bytes=GRANT),
        cost_estimate=pl.CostEstimate(flops=8 * 10**9, bytes_accessed=12 * 10**6, transcendentals=0),
        name="forward_narrow" if narrow else "forward_wide",
    )(field_a, field_b, depth, table, token)


def placed(space, *values):
    return [pltpu.with_memory_space_constraint(value, space) for value in values]


def each(refs):
    return [ref.at[i] for ref in refs for i in range(ref.shape[0])]


def middle_kernel(narrow, arrays, devices, sites, channels, count, pairs, signs, *refs):
    pieces, refs = each(refs[:arrays]), refs[arrays:]
    table_f, table_i, out, lines, hats, mixed, rows = refs
    groups = 1 if narrow else 2
    size = devices * sites
    both = 2 * size
    for s, piece in enumerate(pieces):
        for part in range(2):
            for g in range(groups):
                for x in range(sites):
                    at = part * size + s * sites + x
                    lines[g, pl.ds(at, SUB, stride=both), :] = piece[0, part, g, x * SUB : (x + 1) * SUB, :]
    for g in range(groups):
        for quad in range(2):
            tiles = [lines[g, (quad * 4 + j) * both : (quad * 4 + j + 1) * both, :] for j in range(4)]
            result = left_dot(table_f[...], jnp.concatenate(tiles, axis=1))
            for j in range(4):
                hat = result[:, j * LANES : (j + 1) * LANES]
                if narrow:
                    turned = pltpu.roll(hat, LANES // 2, axis=1)
                    places = ((quad, j, hat), (quad, j + SUB // 2, turned))
                else:
                    places = ((g, quad * 4 + j, hat),)
                for field, c, value in places:
                    hats[field * SUB + c] = value
                    if field:
                        hats[2 * SUB + c] = -value

    def channel(c, carry):
        def pair(p, totals):
            i = pairs[c, 2 * p]
            j = pairs[c, 2 * p + 1] + jnp.where(signs[c, p] < 0, 2 * SUB, SUB)
            a_re, a_im = hats[i, 0:size, :], hats[i, size:both, :]
            b_re, b_im = hats[j, 0:size, :], hats[j, size:both, :]
            return (
                totals[0] + (a_re * b_re + a_im * b_im),
                totals[1] + (a_im * b_re - a_re * b_im),
            )

        zero = jnp.zeros((size, LANES), jnp.float32)
        real, imag = lax.fori_loop(0, count, pair, (zero, zero), unroll=4)
        mixed[c, 0:size, :] = real
        mixed[c, size:both, :] = imag
        return carry

    lax.fori_loop(0, channels, channel, 0)
    if narrow:
        tiles = []
        for c in range(0, channels, 2):
            other = pltpu.roll(mixed[c + 1], LANES // 2, axis=1)
            tiles.append(jnp.where(lane_index(other.shape) < LANES // 2, mixed[c], other))
    else:
        tiles = [mixed[c] for c in range(channels)]
    result = left_dot(table_i[...], jnp.concatenate(tiles, axis=1))
    each_site = 2 * len(tiles)
    for t in range(len(tiles)):
        for part in range(2):
            value = result[part * size : (part + 1) * size, t * LANES : (t + 1) * LANES]
            first = 2 * t + part if narrow else part * channels + t
            rows[pl.ds(first, size, stride=each_site), :] = value
    for s in range(devices):
        out[s, 0] = rows[s * sites * each_site : (s + 1) * sites * each_site, :]


def middle(pieces, pairs, signs, table_f, table_i, sites, channels, narrow):
    size = table_f.shape[0] // 2
    devices = size // sites
    steps = pieces[0].shape[1]
    smem = pl.BlockSpec(memory_space=pltpu.SMEM)
    whole = lambda value: pl.BlockSpec(value.shape, lambda r: (0,) * value.ndim)
    third = lambda value: pl.BlockSpec(
        value.shape[:1] + (1,) + value.shape[2:], lambda r: (0, r) + (0,) * (value.ndim - 2)
    )
    rows = sites * (channels if narrow else 2 * channels)
    groups = 1 if narrow else 2
    return pl.pallas_call(
        functools.partial(middle_kernel, narrow, len(pieces), devices, sites, channels, signs.shape[1]),
        grid=(steps,),
        in_specs=[smem, smem] + [third(v) for v in pieces] + [whole(table_f), whole(table_i)],
        out_specs=pl.BlockSpec((devices, 1, rows, LANES), lambda r: (0, r, 0, 0)),
        out_shape=jax.ShapeDtypeStruct((devices, steps, rows, LANES), jnp.float32),
        scratch_shapes=[
            pltpu.VMEM((groups, SUB * 2 * size, LANES), jnp.float32),
            pltpu.VMEM((3 * SUB, 2 * size, LANES), jnp.float32),
            pltpu.VMEM((channels, 2 * size, LANES), jnp.float32),
            pltpu.VMEM((devices * rows, LANES), jnp.float32),
        ],
        compiler_params=pltpu.CompilerParams(vmem_limit_bytes=SMALL_GRANT),
        cost_estimate=pl.CostEstimate(flops=4 * 10**9, bytes_accessed=10 * 10**6, transcendentals=0),
        name="middle_narrow" if narrow else "middle_wide",
    )(pairs, signs, *placed(pltpu.VMEM if narrow else pltpu.HBM, *pieces), *placed(pltpu.HBM, table_f, table_i))


def inverse_kernel(narrow, arrays, devices, channels, pairs_y, *refs):
    pieces, refs = each(refs[:arrays]), refs[arrays:]
    if narrow:
        table, depth, out, lines = refs
        staged = partial = out
    else:
        partial, table, depth, out, lines, staged = refs
    thirds = pieces[0].shape[0]
    size = thirds * devices

    @pl.when(pl.program_id(0) == 0)
    def _():
        for s in range(devices):
            for r in range(thirds):
                for v in range(pieces[s].shape[1] // SUB):
                    start = v * SUB * size + r * devices + s
                    lines[pl.ds(start, SUB, stride=size), :] = pieces[s][r, v * SUB : (v + 1) * SUB, :]

    step = partial.shape[0]
    for site in range(step):
        x = pl.program_id(0) * step + site
        place = None if narrow else out.at[0, site]
        inverse_site(narrow, channels, pairs_y, size, x, lines, table, depth, staged.at[site], partial.at[site], place)


def inverse_site(narrow, channels, pairs_y, size, x, lines, table, depth, staged, partial, out):
    def tile(*spots):
        return jnp.concatenate([lines[pl.ds(pl.multiple_of(k * size, SUB), size), :] for k in spots], axis=0)

    if narrow:
        tiles = [tile(x * channels + 2 * c, x * channels + 2 * c + 1) for c in range(channels // 2)]
        width, sets = LANES // 4, [range(parity, channels, 2) for parity in range(2)]
    else:
        big = 2 * x * channels
        tiles = [tile(big + c, big + channels + c) for c in range(channels)]
        width, sets = LANES // 2, [range(channels)]
    result = left_dot(table[...], jnp.concatenate(tiles, axis=1))
    half = result.shape[0] // 2
    first, second = result[:half], result[half:]
    high, low = split(jnp.where(lane_index(first.shape) & width == 0, first, second))

    def rows_of(value, e, c):
        spot = c // 2 if narrow else c
        return jnp.concatenate(
            [
                value[(2 * part + e) * pairs_y : (2 * part + e + 1) * pairs_y, spot * LANES : (spot + 1) * LANES]
                for part in range(2)
            ],
            axis=1,
        )

    for k, members in enumerate(sets):
        products = []
        for e in range(2):
            left = [jnp.concatenate([rows_of(value, e, c) for c in members], axis=0) for value in (high, low)]
            products.append(dot(jnp.concatenate([left[0], left[1], left[0]], axis=1), depth[k, e]))
        for i, c in enumerate(members):
            rows = slice(i * pairs_y, (i + 1) * pairs_y)
            zero, one = products[0][rows], products[1][rows]
            for q, value in enumerate((zero[:, :LANES], zero[:, LANES:] + one[:, :LANES], one[:, LANES:])):
                staged[q, pl.ds(c, pairs_y, stride=channels), :] = value
    if not narrow:
        for p in range(pairs_y):
            rows = slice(p * channels, (p + 1) * channels)
            for q in range(3):
                lanes = slice((3 * p + q) * LANES, (3 * p + q + 1) * LANES)
                out[:, lanes] = staged[q, rows, :] + partial[q, rows, :]


def inverse(pieces, partial, table, depth, sites, channels, flat, share=0, shares=1):
    narrow = partial is None
    size = table.shape[1] // 6
    devices = size // pieces[0].shape[1]
    whole = lambda value: pl.BlockSpec(value.shape, lambda x: (0,) * value.ndim)
    tiles = (3, size * channels, LANES)
    rows = pieces[0].shape[2] // shares
    sites = sites // shares
    lines = pltpu.VMEM((rows * size, LANES), jnp.float32)
    part = lambda value: pl.BlockSpec(value.shape[:2] + (rows, LANES), lambda x: (0, 0, share, 0))
    step = 3 if sites % 3 == 0 else 1
    kept = pl.BlockSpec((step,) + tiles, lambda x: (x + share * sites // step, 0, 0, 0))
    return pl.pallas_call(
        functools.partial(inverse_kernel, narrow, len(pieces), devices, channels, size),
        grid=(sites // step,),
        in_specs=[part(v) for v in pieces] + ([] if narrow else [kept]) + [whole(table), whole(depth)],
        out_specs=kept if narrow else pl.BlockSpec((1, step, channels, flat), lambda x: (0, x, 0, 0)),
        out_shape=jax.ShapeDtypeStruct((sites,) + tiles if narrow else (1, sites, channels, flat), jnp.float32),
        scratch_shapes=[lines] if narrow else [lines, pltpu.VMEM((step,) + tiles, jnp.float32)],
        compiler_params=pltpu.CompilerParams(vmem_limit_bytes=SMALL_GRANT),
        cost_estimate=pl.CostEstimate(flops=4 * 10**9, bytes_accessed=6 * 10**6, transcendentals=0),
        name="inverse_narrow" if narrow else "inverse_wide",
    )(*placed(pltpu.VMEM, *pieces), *([] if narrow else placed(pltpu.HBM, partial)), *placed(pltpu.HBM, table, depth))


AT_ONCE = dict(sent_narrow=True, sent_wide=True, back_narrow=True, back_wide=True)


def exchange(packed, at_once):
    if at_once:
        return [lax.all_to_all(packed, "space", 0, 0, tiled=True)]
    devices = packed.shape[0]
    order = sorted(range(1, devices), key=lambda s: (s % 4, -(s // 8), s))
    got = [packed[:1]] + [None] * (devices - 1)
    for s in order:
        got[s] = lax.ppermute(packed[s : s + 1], "space", [(i, i ^ s) for i in range(devices)])
    return got


def fast_slice(field_a, field_b, pairs, signs, tables):
    _, sites, components, flat = field_a.shape
    devices = lax.axis_size("space")
    channels = pairs.shape[0]
    me = lax.axis_index("space")
    mine = [lax.dynamic_index_in_dim(jnp.asarray(t), me, 0, False) for t in tables[:4]]
    fixed = [jnp.asarray(t[0]) for t in tables[:4]]

    def table(which, name):
        return (fixed if AT_ONCE[name] else mine)[which]

    depth_n, depth_w, depth_in, depth_iw = (jnp.asarray(t) for t in tables[4:])
    thirds = tables[0].shape[1] // 4 // devices
    flat_pairs = pairs.reshape(channels, -1)
    sent = {}
    token = signs
    for narrow, depth in ((True, depth_n), (False, depth_w)):
        name = "sent_narrow" if narrow else "sent_wide"
        groups = 1 if narrow else 2
        packed = forward(field_a, field_b, depth, table(0, name), narrow, token)
        token = packed[0, 0]
        packed = packed.reshape(devices, thirds, 2, groups, sites * SUB, LANES)
        sent[narrow] = exchange(packed, AT_ONCE[name])
    partial = None
    shares = 2 if sites % 2 == 0 and sites // 2 * 2 * channels % SUB == 0 else 1
    for narrow, depth in ((True, depth_in), (False, depth_iw)):
        come, go = ("sent_narrow", "back_narrow") if narrow else ("sent_wide", "back_wide")
        mixed = middle(sent[narrow], flat_pairs, signs, table(2, come), table(3, go), sites, channels, narrow)
        back = exchange(mixed, AT_ONCE[go])
        shared = functools.partial(inverse, back, partial, table(1, go), depth, sites, channels, flat)
        if narrow:
            partial = shared()
    return [shared(share, shares) for share in range(shares)]


def neighbours(value):
    devices, length = lax.axis_size("tm"), value.shape[0]
    up = [(i, (i + 1) % devices) for i in range(devices)]
    down = [(j, i) for i, j in up]
    after = lax.ppermute(value[:1], "tm", down)
    before = after if devices == 2 and length == 1 else lax.ppermute(value[-1:], "tm", up)
    later = jnp.concatenate([value[1:], after], axis=0)
    earlier = jnp.concatenate([before, value[:-1]], axis=0)
    return later, earlier


def differences(correlator):
    later, earlier = neighbours(correlator)
    return correlator, later - correlator, later - 2.0 * correlator + earlier


def differences_kernel(count, own, *refs):
    later, earlier = refs[0], refs[count - 1]
    outs = refs[-3:]
    outs[0][...] = own[...]
    outs[1][...] = later[...] - own[...]
    outs[2][...] = later[...] - 2.0 * own[...] + earlier[...]


def write_differences(own, others, share, shares, written):
    _, sites, channels, flat = own.shape
    block = (1, 1, channels, flat)
    mine = pl.BlockSpec(block, lambda x: (0, x, 0, 0))
    shape = jax.ShapeDtypeStruct((1, sites * shares, channels, flat), jnp.float32)
    count = len(others)
    return pl.pallas_call(
        functools.partial(differences_kernel, count),
        grid=(sites,),
        in_specs=[mine] * (1 + count) + [pl.BlockSpec(memory_space=pl.ANY)] * len(written),
        out_specs=[pl.BlockSpec(block, lambda x: (0, x + share * sites, 0, 0))] * 3,
        out_shape=[shape] * 3,
        input_output_aliases={1 + count + k: k for k in range(len(written))},
        compiler_params=pltpu.CompilerParams(vmem_limit_bytes=SMALL_GRANT),
        cost_estimate=pl.CostEstimate(flops=10**6, bytes_accessed=5 * own.size * 4, transcendentals=0),
        name="differences",
    )(own, *others, *written)


def one_time(tables, field_a, field_b, pairs, signs):
    devices = lax.axis_size("tm")
    up = [(i, (i + 1) % devices) for i in range(devices)]
    shares = fast_slice(field_a, field_b, pairs, signs, tables)
    written = []
    for share, own in enumerate(shares):
        others = [lax.ppermute(own, "tm", [(j, i) for i, j in up])]
        if devices != 2:
            others.append(lax.ppermute(own, "tm", up))
        written = write_differences(own, others, share, len(shares), written)
    return written


def fast_device(tables, field_a, field_b, pairs, signs):
    field_a, field_b = field_a.swapaxes(1, 2), field_b.swapaxes(1, 2)
    if field_a.shape[0] == 1:
        outs = one_time(tables, field_a, field_b, pairs, signs)
    else:
        parts = [
            jnp.concatenate(fast_slice(field_a[t : t + 1], field_b[t : t + 1], pairs, signs, tables), axis=1)
            for t in range(field_a.shape[0])
        ]
        outs = differences(jnp.concatenate(parts, axis=0))
    return tuple(out.swapaxes(1, 2) for out in outs)


def dft_tables(length):
    cos, sin = unitary(length)
    return jnp.asarray(cos, jnp.float32), jnp.asarray(sin, jnp.float32)


def swap_parts(values):
    half = values.shape[-1] // 2
    return jnp.concatenate([values[..., half:], -values[..., :half]], axis=-1)


def along_depth(values, inverse):
    cosines, sines = dft_tables(values.shape[-1] // 2)
    matrix = jnp.block([[cosines, -sines], [sines, cosines]])
    if inverse:
        return jnp.einsum("tcxyr,kr->tcxyk", values, matrix, precision=highest)
    return jnp.einsum("tcxyr,rk->tcxyk", values, matrix, precision=highest)


def along(values, sign, axis):
    cosines, sines = dft_tables(values.shape[axis])
    table = jnp.concatenate([cosines, sign * sines], axis=1)
    stacked = jnp.concatenate([values, swap_parts(values)], axis=axis)
    spec = "ky,tcxyr->tcxkr" if axis == 3 else "kx,tcxyr->tckyr"
    return jnp.einsum(spec, table, stacked, precision=highest)


def contract(weights, hat_a, hat_b):
    depth = hat_a.shape[-1] // 2
    outputs = []
    for channel in range(weights.shape[0]):
        mixed_b = jnp.einsum("ij,tjxyk->tixyk", weights[channel], hat_b, precision=highest)
        direct = jnp.sum(hat_a * mixed_b, axis=1)
        crossed = jnp.sum(hat_a * swap_parts(mixed_b), axis=1)
        real_part = direct[..., :depth] + direct[..., depth:]
        imag_part = -(crossed[..., :depth] + crossed[..., depth:])
        outputs.append(jnp.concatenate([real_part, imag_part], axis=-1))
    return jnp.stack(outputs, axis=1)


def any_device(depth, field_a, field_b, pairs, signs):
    as_five = lambda v: v.reshape(v.shape[:3] + (-1, 2 * depth))
    as_four = lambda v: v.reshape(v.shape[:3] + (-1,))
    indices = jnp.arange(field_a.shape[1], dtype=jnp.int32)
    first = (pairs[:, :, 0][:, :, None] == indices).astype(jnp.float32)
    second = (pairs[:, :, 1][:, :, None] == indices).astype(jnp.float32)
    weights = jnp.einsum("cp,cpi,cpj->cij", signs.astype(jnp.float32), first, second, precision=highest)
    hats = []
    for field in (field_a, field_b):
        partial = as_four(along(along_depth(as_five(field), False), 1.0, 3))
        lines = lax.all_to_all(partial, "space", split_axis=3, concat_axis=2, tiled=True)
        hats.append(along(as_five(lines), 1.0, 2))
    returned = as_four(along(contract(weights, *hats), -1.0, 2))
    sites = lax.all_to_all(returned, "space", split_axis=2, concat_axis=3, tiled=True)
    return differences(as_four(along_depth(along(as_five(sites), -1.0, 3), True)))


def solution(mesh):
    devices = mesh.shape["space"]
    times = mesh.shape["tm"]

    def program(field_a, field_b, pairs, signs):
        _, components, size, flat = field_a.shape
        depth = flat // size // 2
        wide = LANES // 2
        fits = (
            depth == size
            and 2 * depth == 3 * wide
            and components == SUB
            and pairs.shape[0] == 4
            and size % (2 * devices) == 0
            and devices & (devices - 1) == 0
            and (size // devices) * 4 % SUB == 0
            and size % (2 * SUB) == 0
        )
        if fits:
            tables = (
                rows_forward(devices, size),
                rows_inverse(devices, size),
                columns_forward(devices, size),
                columns_inverse(devices, size),
                depth_forward(depth, wide, depth - wide),
                depth_forward(depth, 0, wide),
                depth_inverse(depth, wide, depth - wide, 2),
                depth_inverse(depth, 0, wide, 1),
            )
            per_device = functools.partial(fast_device, tables)
        else:
            per_device = functools.partial(any_device, depth)
        spec = P("tm", None, "space", None)
        return jax.shard_map(
            per_device,
            mesh=mesh,
            in_specs=(spec, spec, P(), P()),
            out_specs=(spec, spec, spec),
            check_vma=False,
        )(field_a, field_b, pairs, signs)

    return program
```

```python
import functools
import math

import jax
import jax.numpy as jnp
import ml_dtypes
import numpy as np
from jax import lax
from jax.experimental import pallas as pl
from jax.experimental.pallas import tpu as pltpu
from jax.sharding import PartitionSpec as P

highest = lax.Precision.HIGHEST
LANES = 128
SUB = 8
GRANT = 56 << 20
SMALL_GRANT = 24 << 20


def unitary(length):
    index = np.arange(length)
    angle = (index[:, None] * index[None, :] % length) * (2.0 * np.pi / length)
    return np.cos(angle) / math.sqrt(length), np.sin(angle) / math.sqrt(length)


def halves(table):
    high = table.astype(np.float32).astype(ml_dtypes.bfloat16)
    low = (table - high.astype(np.float64)).astype(np.float32).astype(ml_dtypes.bfloat16)
    return high, low


def left_table(table):
    high, low = halves(table)
    return np.concatenate([high, high, low], axis=1)


def right_table(table):
    high, low = halves(table)
    return np.concatenate([high, high, low], axis=0)


def owned(devices, length):
    each = length // devices
    me = np.arange(devices)
    return ((me[:, None] ^ me[None, :]) * each)[:, :, None] + np.arange(each)


def rows_forward(devices, length):
    cos, sin = unitary(length)
    out = []
    for spots in owned(devices, length):
        k = spots.reshape(devices, -1, 2).transpose(2, 0, 1).reshape(-1)
        y = np.arange(length).reshape(-1, 2).T.reshape(-1)
        c, s = cos[k][:, y], sin[k][:, y]
        out.append(left_table(np.block([[c, s], [-s, c]])))
    return np.stack(out)


def rows_inverse(devices, length):
    cos, sin = unitary(length)
    out = []
    for spots in owned(devices, length):
        y = np.arange(length).reshape(-1, 2).T.reshape(-1)
        blocks = []
        for e in range(2):
            k = spots.reshape(devices, -1, 2)[:, :, e].T.reshape(-1)
            c, s = cos[y][:, k], sin[y][:, k]
            blocks.append(np.block([[c, -s], [s, c]]))
        out.append(left_table(np.concatenate(blocks)))
    return np.stack(out)


def columns_forward(devices, length):
    cos, sin = unitary(length)
    out = []
    for spots in owned(devices, length):
        c, s = cos[:, spots.reshape(-1)], sin[:, spots.reshape(-1)]
        out.append(left_table(np.block([[c, s], [-s, c]])))
    return np.stack(out)


def columns_inverse(devices, length):
    cos, sin = unitary(length)
    out = []
    for spots in owned(devices, length):
        c, s = cos[spots.reshape(-1)], sin[spots.reshape(-1)]
        out.append(left_table(np.block([[c, -s], [s, c]])))
    return np.stack(out)


def depth_forward(length, first, count):
    cos, sin = unitary(length)
    k = np.tile(np.arange(first, first + count), LANES // count)
    matrix = np.block([[cos[:, k], -sin[:, k]], [sin[:, k], cos[:, k]]])
    gap = np.zeros((2 * LANES - 2 * length, 2 * LANES))
    both = np.stack([np.concatenate([matrix, gap]), np.concatenate([gap, matrix])])
    return np.stack([right_table(b) for b in both])


def depth_inverse(length, first, count, halves_of):
    cos, sin = unitary(length)
    k = np.tile(np.arange(first, first + count), LANES // count)
    out = []
    for half in range(halves_of):
        keep = (np.arange(LANES) * halves_of // LANES == half)[:, None] * 1.0
        matrix = np.block([[cos[k] * keep, sin[k] * keep], [-sin[k] * keep, cos[k] * keep]])
        gap = np.zeros((matrix.shape[0], 2 * LANES - 2 * length))
        both = (np.concatenate([matrix, gap], axis=1), np.concatenate([gap, matrix], axis=1))
        out.append(np.stack([right_table(b) for b in both]))
    return np.stack(out)


def split(value):
    high = value.astype(jnp.bfloat16)
    return high, (value - high.astype(jnp.float32)).astype(jnp.bfloat16)


def dot(left, right):
    return jnp.dot(left, right, preferred_element_type=jnp.float32)


def left_dot(table, value):
    high, low = split(value)
    return dot(table, jnp.concatenate([high, low, high], axis=0))


def lane_index(shape):
    return lax.broadcasted_iota(jnp.int32, shape, len(shape) - 1)


def forward_kernel(narrow, sites, pairs_y, field_a, field_b, depth, table, token, out, packed, *spectra):
    for site in range(field_a.shape[1]):
        spaces = spectra[2 * site], spectra[2 * site + 1]
        forward_site(narrow, pairs_y, field_a.at[0, site], field_b.at[0, site], depth, table, packed.at[site], spaces)
        for block in range(out.shape[0]):
            out[block, site] = packed[site, block * SUB : (block + 1) * SUB, :]


def forward_site(narrow, pairs_y, field_a, field_b, depth, table, packed, spectra):
    groups = 1 if narrow else 2
    width = LANES // 4 if narrow else LANES // 2
    block = 2 * groups * SUB
    slots = []
    for group, field in enumerate((field_a, field_b)):
        tiles = [
            jnp.concatenate(
                [field[:, (3 * p + q) * LANES : (3 * p + q + 1) * LANES] for p in range(pairs_y)], axis=0
            )
            for q in range(3)
        ]
        tiles = [split(tile) for tile in tiles]
        for e in range(2):
            left = [tiles[e + k][part] for part in (0, 1, 0) for k in range(2)]
            result = dot(jnp.concatenate(left, axis=1), depth[e])
            for part in range(2):
                spectra[group][part * 2 + e, : result.shape[0]] = result[:, part * LANES : (part + 1) * LANES]

        def rows_of(c, group=group):
            return jnp.concatenate(
                [spectra[group][k, pl.ds(c, pairs_y, stride=SUB), :] for k in range(4)], axis=0
            )

        if narrow:
            for c in range(SUB // 2):
                first, second = rows_of(c), rows_of(c + SUB // 2)
                pick = lane_index(first.shape) < LANES // 2
                slots.append((0, group * 4 + c, jnp.where(pick, first, second)))
        else:
            slots += [(group, c, rows_of(c)) for c in range(SUB)]

    for first in range(0, len(slots), SUB):
        batch = slots[first : first + SUB]
        result = left_dot(table[...], jnp.concatenate([value for _, _, value in batch], axis=1))
        half = result.shape[0] // 4
        for part in range(2):
            even = result[2 * part * half : (2 * part + 1) * half]
            odd = result[(2 * part + 1) * half : (2 * part + 2) * half]
            merged = jnp.where(lane_index(even.shape) // width % 2 == 0, even, odd)
            for i, (group, slot, _) in enumerate(batch):
                start = (part * groups + group) * SUB + slot
                packed[pl.ds(start, half, stride=block), :] = merged[:, i * LANES : (i + 1) * LANES]


def forward(field_a, field_b, depth, table, narrow, token):
    _, sites, components, flat = field_a.shape
    groups = 1 if narrow else 2
    size = table.shape[0] // 2
    pairs_y = size // 2
    lines = size // 2
    blocks = lines * 2 * groups
    step = 1
    spot = pl.BlockSpec((1, step, components, flat), lambda x: (0, x, 0, 0))
    whole = lambda value: pl.BlockSpec(value.shape, lambda x: (0,) * value.ndim)
    return pl.pallas_call(
        functools.partial(forward_kernel, narrow, sites, pairs_y),
        grid=(sites // step,),
        in_specs=[spot, spot, whole(depth), whole(table), pl.BlockSpec(memory_space=pl.ANY)],
        out_specs=pl.BlockSpec((blocks, step, SUB, LANES), lambda x: (0, x, 0, 0)),
        out_shape=jax.ShapeDtypeStruct((blocks, sites, SUB, LANES), jnp.float32),
        scratch_shapes=[pltpu.VMEM((step, (blocks + 2 * groups) * SUB, LANES), jnp.float32)]
        + [pltpu.VMEM((4, (pairs_y + 1) * SUB, LANES), jnp.float32)] * (2 * step),
        compiler_params=pltpu.CompilerParams(vmem_limit_bytes=GRANT),
        cost_estimate=pl.CostEstimate(flops=8 * 10**9, bytes_accessed=12 * 10**6, transcendentals=0),
        name="forward_narrow" if narrow else "forward_wide",
    )(field_a, field_b, depth, table, token)


def placed(space, *values):
    return [pltpu.with_memory_space_constraint(value, space) for value in values]


def each(refs):
    return [ref.at[i] for ref in refs for i in range(ref.shape[0])]


def middle_kernel(narrow, arrays, devices, sites, channels, count, pairs, signs, *refs):
    pieces, refs = each(refs[:arrays]), refs[arrays:]
    table_f, table_i, out, lines, hats, mixed, rows = refs
    groups = 1 if narrow else 2
    size = devices * sites
    both = 2 * size
    for s, piece in enumerate(pieces):
        for part in range(2):
            for g in range(groups):
                for x in range(sites):
                    at = part * size + s * sites + x
                    lines[g, pl.ds(at, SUB, stride=both), :] = piece[0, part, g, x * SUB : (x + 1) * SUB, :]
    for g in range(groups):
        for quad in range(2):
            tiles = [lines[g, (quad * 4 + j) * both : (quad * 4 + j + 1) * both, :] for j in range(4)]
            result = left_dot(table_f[...], jnp.concatenate(tiles, axis=1))
            for j in range(4):
                hat = result[:, j * LANES : (j + 1) * LANES]
                if narrow:
                    turned = pltpu.roll(hat, LANES // 2, axis=1)
                    places = ((quad, j, hat), (quad, j + SUB // 2, turned))
                else:
                    places = ((g, quad * 4 + j, hat),)
                for field, c, value in places:
                    hats[field * SUB + c] = value
                    if field:
                        hats[2 * SUB + c] = -value

    def channel(c, carry):
        def pair(p, totals):
            i = pairs[c, 2 * p]
            j = pairs[c, 2 * p + 1] + jnp.where(signs[c, p] < 0, 2 * SUB, SUB)
            a_re, a_im = hats[i, 0:size, :], hats[i, size:both, :]
            b_re, b_im = hats[j, 0:size, :], hats[j, size:both, :]
            return (
                totals[0] + (a_re * b_re + a_im * b_im),
                totals[1] + (a_im * b_re - a_re * b_im),
            )

        zero = jnp.zeros((size, LANES), jnp.float32)
        real, imag = lax.fori_loop(0, count, pair, (zero, zero), unroll=4)
        mixed[c, 0:size, :] = real
        mixed[c, size:both, :] = imag
        return carry

    lax.fori_loop(0, channels, channel, 0)
    if narrow:
        tiles = []
        for c in range(0, channels, 2):
            other = pltpu.roll(mixed[c + 1], LANES // 2, axis=1)
            tiles.append(jnp.where(lane_index(other.shape) < LANES // 2, mixed[c], other))
    else:
        tiles = [mixed[c] for c in range(channels)]
    result = left_dot(table_i[...], jnp.concatenate(tiles, axis=1))
    each_site = 2 * len(tiles)
    for t in range(len(tiles)):
        for part in range(2):
            value = result[part * size : (part + 1) * size, t * LANES : (t + 1) * LANES]
            first = 2 * t + part if narrow else part * channels + t
            rows[pl.ds(first, size, stride=each_site), :] = value
    for s in range(devices):
        out[s, 0] = rows[s * sites * each_site : (s + 1) * sites * each_site, :]


def middle(pieces, pairs, signs, table_f, table_i, sites, channels, narrow):
    size = table_f.shape[0] // 2
    devices = size // sites
    steps = pieces[0].shape[1]
    smem = pl.BlockSpec(memory_space=pltpu.SMEM)
    whole = lambda value: pl.BlockSpec(value.shape, lambda r: (0,) * value.ndim)
    third = lambda value: pl.BlockSpec(
        value.shape[:1] + (1,) + value.shape[2:], lambda r: (0, r) + (0,) * (value.ndim - 2)
    )
    rows = sites * (channels if narrow else 2 * channels)
    groups = 1 if narrow else 2
    return pl.pallas_call(
        functools.partial(middle_kernel, narrow, len(pieces), devices, sites, channels, signs.shape[1]),
        grid=(steps,),
        in_specs=[smem, smem] + [third(v) for v in pieces] + [whole(table_f), whole(table_i)],
        out_specs=pl.BlockSpec((devices, 1, rows, LANES), lambda r: (0, r, 0, 0)),
        out_shape=jax.ShapeDtypeStruct((devices, steps, rows, LANES), jnp.float32),
        scratch_shapes=[
            pltpu.VMEM((groups, (SUB + 1) * 2 * size, LANES), jnp.float32),
            pltpu.VMEM((3 * SUB, 2 * size, LANES), jnp.float32),
            pltpu.VMEM((channels, 2 * size, LANES), jnp.float32),
            pltpu.VMEM((devices * rows + SUB, LANES), jnp.float32),
        ],
        compiler_params=pltpu.CompilerParams(vmem_limit_bytes=SMALL_GRANT),
        cost_estimate=pl.CostEstimate(flops=4 * 10**9, bytes_accessed=10 * 10**6, transcendentals=0),
        name="middle_narrow" if narrow else "middle_wide",
    )(pairs, signs, *placed(pltpu.VMEM if narrow else pltpu.HBM, *pieces), *placed(pltpu.HBM, table_f, table_i))


def inverse_kernel(narrow, arrays, devices, channels, pairs_y, *refs):
    pieces, refs = each(refs[:arrays]), refs[arrays:]
    if narrow:
        table, depth, out, lines, staged = refs
        partial = out
    else:
        partial, table, depth, out, lines, staged = refs
    thirds = pieces[0].shape[0]
    size = thirds * devices

    @pl.when(pl.program_id(0) == 0)
    def _():
        for s in range(devices):
            for r in range(thirds):
                for v in range(pieces[s].shape[1] // SUB):
                    start = v * SUB * size + r * devices + s
                    lines[pl.ds(start, SUB, stride=size), :] = pieces[s][r, v * SUB : (v + 1) * SUB, :]

    step = partial.shape[0]
    for site in range(step):
        x = pl.program_id(0) * step + site
        place = None if narrow else out.at[0, site]
        inverse_site(narrow, channels, pairs_y, size, x, lines, table, depth, staged.at[site], partial.at[site], place)


def inverse_site(narrow, channels, pairs_y, size, x, lines, table, depth, staged, partial, out):
    def tile(*spots):
        return jnp.concatenate([lines[pl.ds(pl.multiple_of(k * size, SUB), size), :] for k in spots], axis=0)

    if narrow:
        tiles = [tile(x * channels + 2 * c, x * channels + 2 * c + 1) for c in range(channels // 2)]
        width, sets = LANES // 4, [range(parity, channels, 2) for parity in range(2)]
    else:
        big = 2 * x * channels
        tiles = [tile(big + c, big + channels + c) for c in range(channels)]
        width, sets = LANES // 2, [range(channels)]
    result = left_dot(table[...], jnp.concatenate(tiles, axis=1))
    half = result.shape[0] // 2
    first, second = result[:half], result[half:]
    high, low = split(jnp.where(lane_index(first.shape) & width == 0, first, second))

    def rows_of(value, e, c):
        spot = c // 2 if narrow else c
        return jnp.concatenate(
            [
                value[(2 * part + e) * pairs_y : (2 * part + e + 1) * pairs_y, spot * LANES : (spot + 1) * LANES]
                for part in range(2)
            ],
            axis=1,
        )

    for k, members in enumerate(sets):
        products = []
        for e in range(2):
            left = [jnp.concatenate([rows_of(value, e, c) for c in members], axis=0) for value in (high, low)]
            products.append(dot(jnp.concatenate([left[0], left[1], left[0]], axis=1), depth[k, e]))
        for i, c in enumerate(members):
            rows = slice(i * pairs_y, (i + 1) * pairs_y)
            zero, one = products[0][rows], products[1][rows]
            for q, value in enumerate((zero[:, :LANES], zero[:, LANES:] + one[:, :LANES], one[:, LANES:])):
                staged[q, pl.ds(c, pairs_y, stride=channels), :] = value
    if narrow:
        partial[...] = staged[:, : partial.shape[1], :]
    else:
        for p in range(pairs_y):
            rows = slice(p * channels, (p + 1) * channels)
            for q in range(3):
                lanes = slice((3 * p + q) * LANES, (3 * p + q + 1) * LANES)
                out[:, lanes] = staged[q, rows, :] + partial[q, rows, :]


def inverse(pieces, partial, table, depth, sites, channels, flat, share=0, shares=1):
    narrow = partial is None
    size = table.shape[1] // 6
    devices = size // pieces[0].shape[1]
    whole = lambda value: pl.BlockSpec(value.shape, lambda x: (0,) * value.ndim)
    tiles = (3, size * channels, LANES)
    rows = pieces[0].shape[2] // shares
    sites = sites // shares
    lines = pltpu.VMEM(((rows + 1) * size, LANES), jnp.float32)
    part = lambda value: pl.BlockSpec(value.shape[:2] + (rows, LANES), lambda x: (0, 0, share, 0))
    step = 3 if sites % 3 == 0 else 1
    kept = pl.BlockSpec((step,) + tiles, lambda x: (x + share * sites // step, 0, 0, 0))
    return pl.pallas_call(
        functools.partial(inverse_kernel, narrow, len(pieces), devices, channels, size),
        grid=(sites // step,),
        in_specs=[part(v) for v in pieces] + ([] if narrow else [kept]) + [whole(table), whole(depth)],
        out_specs=kept if narrow else pl.BlockSpec((1, step, channels, flat), lambda x: (0, x, 0, 0)),
        out_shape=jax.ShapeDtypeStruct((sites,) + tiles if narrow else (1, sites, channels, flat), jnp.float32),
        scratch_shapes=[lines, pltpu.VMEM((step, 3, size * channels + SUB, LANES), jnp.float32)],
        compiler_params=pltpu.CompilerParams(vmem_limit_bytes=SMALL_GRANT),
        cost_estimate=pl.CostEstimate(flops=4 * 10**9, bytes_accessed=6 * 10**6, transcendentals=0),
        name="inverse_narrow" if narrow else "inverse_wide",
    )(*placed(pltpu.VMEM, *pieces), *([] if narrow else placed(pltpu.HBM, partial)), *placed(pltpu.HBM, table, depth))


AT_ONCE = dict(sent_narrow=True, sent_wide=True, back_narrow=True, back_wide=True)


def exchange(packed, at_once):
    if at_once:
        return [lax.all_to_all(packed, "space", 0, 0, tiled=True)]
    devices = packed.shape[0]
    order = sorted(range(1, devices), key=lambda s: (s % 4, -(s // 8), s))
    got = [packed[:1]] + [None] * (devices - 1)
    for s in order:
        got[s] = lax.ppermute(packed[s : s + 1], "space", [(i, i ^ s) for i in range(devices)])
    return got


def fast_slice(field_a, field_b, pairs, signs, tables):
    _, sites, components, flat = field_a.shape
    devices = lax.axis_size("space")
    channels = pairs.shape[0]
    me = lax.axis_index("space")
    mine = [lax.dynamic_index_in_dim(jnp.asarray(t), me, 0, False) for t in tables[:4]]
    fixed = [jnp.asarray(t[0]) for t in tables[:4]]

    def table(which, name):
        return (fixed if AT_ONCE[name] else mine)[which]

    depth_n, depth_w, depth_in, depth_iw = (jnp.asarray(t) for t in tables[4:])
    thirds = tables[0].shape[1] // 4 // devices
    flat_pairs = pairs.reshape(channels, -1)
    sent = {}
    token = signs
    for narrow, depth in ((True, depth_n), (False, depth_w)):
        name = "sent_narrow" if narrow else "sent_wide"
        groups = 1 if narrow else 2
        packed = forward(field_a, field_b, depth, table(0, name), narrow, token)
        token = packed[0, 0]
        packed = packed.reshape(devices, thirds, 2, groups, sites * SUB, LANES)
        sent[narrow] = exchange(packed, AT_ONCE[name])
    partial = None
    shares = 2 if sites % 2 == 0 and sites // 2 * 2 * channels % SUB == 0 else 1
    for narrow, depth in ((True, depth_in), (False, depth_iw)):
        come, go = ("sent_narrow", "back_narrow") if narrow else ("sent_wide", "back_wide")
        mixed = middle(sent[narrow], flat_pairs, signs, table(2, come), table(3, go), sites, channels, narrow)
        back = exchange(mixed, AT_ONCE[go])
        shared = functools.partial(inverse, back, partial, table(1, go), depth, sites, channels, flat)
        if narrow:
            partial = shared()
    return [shared(share, shares) for share in range(shares)]


def neighbours(value):
    devices, length = lax.axis_size("tm"), value.shape[0]
    up = [(i, (i + 1) % devices) for i in range(devices)]
    down = [(j, i) for i, j in up]
    after = lax.ppermute(value[:1], "tm", down)
    before = after if devices == 2 and length == 1 else lax.ppermute(value[-1:], "tm", up)
    later = jnp.concatenate([value[1:], after], axis=0)
    earlier = jnp.concatenate([before, value[:-1]], axis=0)
    return later, earlier


def differences(correlator):
    later, earlier = neighbours(correlator)
    return correlator, later - correlator, later - 2.0 * correlator + earlier


def differences_kernel(count, own, *refs):
    later, earlier = refs[0], refs[count - 1]
    outs = refs[-3:]
    outs[0][...] = own[...]
    outs[1][...] = later[...] - own[...]
    outs[2][...] = later[...] - 2.0 * own[...] + earlier[...]


def write_differences(own, others, share, shares, written):
    _, sites, channels, flat = own.shape
    block = (1, 1, channels, flat)
    mine = pl.BlockSpec(block, lambda x: (0, x, 0, 0))
    shape = jax.ShapeDtypeStruct((1, sites * shares, channels, flat), jnp.float32)
    count = len(others)
    return pl.pallas_call(
        functools.partial(differences_kernel, count),
        grid=(sites,),
        in_specs=[mine] * (1 + count) + [pl.BlockSpec(memory_space=pl.ANY)] * len(written),
        out_specs=[pl.BlockSpec(block, lambda x: (0, x + share * sites, 0, 0))] * 3,
        out_shape=[shape] * 3,
        input_output_aliases={1 + count + k: k for k in range(len(written))},
        compiler_params=pltpu.CompilerParams(vmem_limit_bytes=SMALL_GRANT),
        cost_estimate=pl.CostEstimate(flops=10**6, bytes_accessed=5 * own.size * 4, transcendentals=0),
        name="differences",
    )(own, *others, *written)


def one_time(tables, field_a, field_b, pairs, signs):
    devices = lax.axis_size("tm")
    up = [(i, (i + 1) % devices) for i in range(devices)]
    shares = fast_slice(field_a, field_b, pairs, signs, tables)
    written = []
    for share, own in enumerate(shares):
        others = [lax.ppermute(own, "tm", [(j, i) for i, j in up])]
        if devices != 2:
            others.append(lax.ppermute(own, "tm", up))
        written = write_differences(own, others, share, len(shares), written)
    return written


def fast_device(tables, field_a, field_b, pairs, signs):
    field_a, field_b = field_a.swapaxes(1, 2), field_b.swapaxes(1, 2)
    if field_a.shape[0] == 1:
        outs = one_time(tables, field_a, field_b, pairs, signs)
    else:
        parts = [
            jnp.concatenate(fast_slice(field_a[t : t + 1], field_b[t : t + 1], pairs, signs, tables), axis=1)
            for t in range(field_a.shape[0])
        ]
        outs = differences(jnp.concatenate(parts, axis=0))
    return tuple(out.swapaxes(1, 2) for out in outs)


def dft_tables(length):
    cos, sin = unitary(length)
    return jnp.asarray(cos, jnp.float32), jnp.asarray(sin, jnp.float32)


def swap_parts(values):
    half = values.shape[-1] // 2
    return jnp.concatenate([values[..., half:], -values[..., :half]], axis=-1)


def along_depth(values, inverse):
    cosines, sines = dft_tables(values.shape[-1] // 2)
    matrix = jnp.block([[cosines, -sines], [sines, cosines]])
    if inverse:
        return jnp.einsum("tcxyr,kr->tcxyk", values, matrix, precision=highest)
    return jnp.einsum("tcxyr,rk->tcxyk", values, matrix, precision=highest)


def along(values, sign, axis):
    cosines, sines = dft_tables(values.shape[axis])
    table = jnp.concatenate([cosines, sign * sines], axis=1)
    stacked = jnp.concatenate([values, swap_parts(values)], axis=axis)
    spec = "ky,tcxyr->tcxkr" if axis == 3 else "kx,tcxyr->tckyr"
    return jnp.einsum(spec, table, stacked, precision=highest)


def contract(weights, hat_a, hat_b):
    depth = hat_a.shape[-1] // 2
    outputs = []
    for channel in range(weights.shape[0]):
        mixed_b = jnp.einsum("ij,tjxyk->tixyk", weights[channel], hat_b, precision=highest)
        direct = jnp.sum(hat_a * mixed_b, axis=1)
        crossed = jnp.sum(hat_a * swap_parts(mixed_b), axis=1)
        real_part = direct[..., :depth] + direct[..., depth:]
        imag_part = -(crossed[..., :depth] + crossed[..., depth:])
        outputs.append(jnp.concatenate([real_part, imag_part], axis=-1))
    return jnp.stack(outputs, axis=1)


def any_device(depth, field_a, field_b, pairs, signs):
    as_five = lambda v: v.reshape(v.shape[:3] + (-1, 2 * depth))
    as_four = lambda v: v.reshape(v.shape[:3] + (-1,))
    indices = jnp.arange(field_a.shape[1], dtype=jnp.int32)
    first = (pairs[:, :, 0][:, :, None] == indices).astype(jnp.float32)
    second = (pairs[:, :, 1][:, :, None] == indices).astype(jnp.float32)
    weights = jnp.einsum("cp,cpi,cpj->cij", signs.astype(jnp.float32), first, second, precision=highest)
    hats = []
    for field in (field_a, field_b):
        partial = as_four(along(along_depth(as_five(field), False), 1.0, 3))
        lines = lax.all_to_all(partial, "space", split_axis=3, concat_axis=2, tiled=True)
        hats.append(along(as_five(lines), 1.0, 2))
    returned = as_four(along(contract(weights, *hats), -1.0, 2))
    sites = lax.all_to_all(returned, "space", split_axis=2, concat_axis=3, tiled=True)
    return differences(as_four(along_depth(along(as_five(sites), -1.0, 3), True)))


def solution(mesh):
    devices = mesh.shape["space"]
    times = mesh.shape["tm"]

    def program(field_a, field_b, pairs, signs):
        _, components, size, flat = field_a.shape
        depth = flat // size // 2
        wide = LANES // 2
        fits = (
            depth == size
            and 2 * depth == 3 * wide
            and components == SUB
            and pairs.shape[0] == 4
            and size % (2 * devices) == 0
            and devices & (devices - 1) == 0
            and (size // devices) * 4 % SUB == 0
            and size % (2 * SUB) == 0
        )
        if fits:
            tables = (
                rows_forward(devices, size),
                rows_inverse(devices, size),
                columns_forward(devices, size),
                columns_inverse(devices, size),
                depth_forward(depth, wide, depth - wide),
                depth_forward(depth, 0, wide),
                depth_inverse(depth, wide, depth - wide, 2),
                depth_inverse(depth, 0, wide, 1),
            )
            per_device = functools.partial(fast_device, tables)
        else:
            per_device = functools.partial(any_device, depth)
        spec = P("tm", None, "space", None)
        return jax.shard_map(
            per_device,
            mesh=mesh,
            in_specs=(spec, spec, P(), P()),
            out_specs=(spec, spec, spec),
            check_vma=False,
        )(field_a, field_b, pairs, signs)

    return program
```

```python
import functools
import math

import jax
import jax.numpy as jnp
import ml_dtypes
import numpy as np
from jax import lax
from jax.experimental import pallas as pl
from jax.experimental.pallas import tpu as pltpu
from jax.sharding import PartitionSpec as P

highest = lax.Precision.HIGHEST
LANES = 128
SUB = 8
GRANT = 56 << 20
SMALL_GRANT = 24 << 20


def unitary(length):
    index = np.arange(length)
    angle = (index[:, None] * index[None, :] % length) * (2.0 * np.pi / length)
    return np.cos(angle) / math.sqrt(length), np.sin(angle) / math.sqrt(length)


def halves(table):
    high = table.astype(np.float32).astype(ml_dtypes.bfloat16)
    low = (table - high.astype(np.float64)).astype(np.float32).astype(ml_dtypes.bfloat16)
    return high, low


def left_table(table):
    high, low = halves(table)
    return np.concatenate([high, high, low], axis=1)


def right_table(table):
    high, low = halves(table)
    return np.concatenate([high, high, low], axis=0)


def owned(devices, length):
    each = length // devices
    me = np.arange(devices)
    return ((me[:, None] ^ me[None, :]) * each)[:, :, None] + np.arange(each)


def rows_forward(devices, length):
    cos, sin = unitary(length)
    out = []
    for spots in owned(devices, length):
        k = spots.reshape(devices, -1, 2).transpose(2, 0, 1).reshape(-1)
        y = np.arange(length).reshape(-1, 2).T.reshape(-1)
        c, s = cos[k][:, y], sin[k][:, y]
        out.append(left_table(np.block([[c, s], [-s, c]])))
    return np.stack(out)


def rows_inverse(devices, length):
    cos, sin = unitary(length)
    out = []
    for spots in owned(devices, length):
        y = np.arange(length).reshape(-1, 2).T.reshape(-1)
        blocks = []
        for e in range(2):
            k = spots.reshape(devices, -1, 2)[:, :, e].T.reshape(-1)
            c, s = cos[y][:, k], sin[y][:, k]
            blocks.append(np.block([[c, -s], [s, c]]))
        out.append(left_table(np.concatenate(blocks)))
    return np.stack(out)


def columns_forward(devices, length):
    cos, sin = unitary(length)
    out = []
    for spots in owned(devices, length):
        c, s = cos[:, spots.reshape(-1)], sin[:, spots.reshape(-1)]
        out.append(left_table(np.block([[c, s], [-s, c]])))
    return np.stack(out)


def columns_inverse(devices, length):
    cos, sin = unitary(length)
    out = []
    for spots in owned(devices, length):
        c, s = cos[spots.reshape(-1)], sin[spots.reshape(-1)]
        out.append(left_table(np.block([[c, -s], [s, c]])))
    return np.stack(out)


def depth_forward(length, first, count):
    cos, sin = unitary(length)
    k = np.tile(np.arange(first, first + count), LANES // count)
    matrix = np.block([[cos[:, k], -sin[:, k]], [sin[:, k], cos[:, k]]])
    gap = np.zeros((2 * LANES - 2 * length, 2 * LANES))
    both = np.stack([np.concatenate([matrix, gap]), np.concatenate([gap, matrix])])
    return np.stack([right_table(b) for b in both])


def depth_inverse(length, first, count, halves_of):
    cos, sin = unitary(length)
    k = np.tile(np.arange(first, first + count), LANES // count)
    out = []
    for half in range(halves_of):
        keep = (np.arange(LANES) * halves_of // LANES == half)[:, None] * 1.0
        matrix = np.block([[cos[k] * keep, sin[k] * keep], [-sin[k] * keep, cos[k] * keep]])
        gap = np.zeros((matrix.shape[0], 2 * LANES - 2 * length))
        both = (np.concatenate([matrix, gap], axis=1), np.concatenate([gap, matrix], axis=1))
        out.append(np.stack([right_table(b) for b in both]))
    return np.stack(out)


def split(value):
    high = value.astype(jnp.bfloat16)
    return high, (value - high.astype(jnp.float32)).astype(jnp.bfloat16)


def dot(left, right):
    return jnp.dot(left, right, preferred_element_type=jnp.float32)


def left_dot(table, value):
    high, low = split(value)
    return dot(table, jnp.concatenate([high, low, high], axis=0))


def lane_index(shape):
    return lax.broadcasted_iota(jnp.int32, shape, len(shape) - 1)


def forward_kernel(narrow, sites, pairs_y, field_a, field_b, depth, table, token, out, packed, *spectra):
    for site in range(field_a.shape[1]):
        spaces = spectra[2 * site], spectra[2 * site + 1]
        forward_site(narrow, pairs_y, field_a.at[0, site], field_b.at[0, site], depth, table, packed.at[site], spaces)
        for block in range(out.shape[0]):
            out[block, site] = packed[site, block * SUB : (block + 1) * SUB, :]


def forward_site(narrow, pairs_y, field_a, field_b, depth, table, packed, spectra):
    groups = 1 if narrow else 2
    width = LANES // 4 if narrow else LANES // 2
    block = 2 * groups * SUB
    slots = []
    for group, field in enumerate((field_a, field_b)):
        tiles = [
            jnp.concatenate(
                [field[:, (3 * p + q) * LANES : (3 * p + q + 1) * LANES] for p in range(pairs_y)], axis=0
            )
            for q in range(3)
        ]
        tiles = [split(tile) for tile in tiles]
        for e in range(2):
            left = [tiles[e + k][part] for part in (0, 1, 0) for k in range(2)]
            result = dot(jnp.concatenate(left, axis=1), depth[e])
            for part in range(2):
                spectra[group][part * 2 + e, : result.shape[0]] = result[:, part * LANES : (part + 1) * LANES]

        def rows_of(c, group=group):
            return jnp.concatenate(
                [spectra[group][k, pl.ds(c, pairs_y, stride=SUB), :] for k in range(4)], axis=0
            )

        if narrow:
            for c in range(SUB // 2):
                first, second = rows_of(c), rows_of(c + SUB // 2)
                pick = lane_index(first.shape) < LANES // 2
                slots.append((0, group * 4 + c, jnp.where(pick, first, second)))
        else:
            slots += [(group, c, rows_of(c)) for c in range(SUB)]

    for first in range(0, len(slots), SUB):
        batch = slots[first : first + SUB]
        result = left_dot(table[...], jnp.concatenate([value for _, _, value in batch], axis=1))
        half = result.shape[0] // 4
        for part in range(2):
            even = result[2 * part * half : (2 * part + 1) * half]
            odd = result[(2 * part + 1) * half : (2 * part + 2) * half]
            merged = jnp.where(lane_index(even.shape) // width % 2 == 0, even, odd)
            for i, (group, slot, _) in enumerate(batch):
                start = (part * groups + group) * SUB + slot
                packed[pl.ds(start, half, stride=block), :] = merged[:, i * LANES : (i + 1) * LANES]


def forward(field_a, field_b, depth, table, narrow, token):
    _, sites, components, flat = field_a.shape
    groups = 1 if narrow else 2
    size = table.shape[0] // 2
    pairs_y = size // 2
    lines = size // 2
    blocks = lines * 2 * groups
    step = 1
    spot = pl.BlockSpec((1, step, components, flat), lambda x: (0, x, 0, 0))
    whole = lambda value: pl.BlockSpec(value.shape, lambda x: (0,) * value.ndim)
    return pl.pallas_call(
        functools.partial(forward_kernel, narrow, sites, pairs_y),
        grid=(sites // step,),
        in_specs=[spot, spot, whole(depth), whole(table), pl.BlockSpec(memory_space=pl.ANY)],
        out_specs=pl.BlockSpec((blocks, step, SUB, LANES), lambda x: (0, x, 0, 0)),
        out_shape=jax.ShapeDtypeStruct((blocks, sites, SUB, LANES), jnp.float32),
        scratch_shapes=[pltpu.VMEM((step, (blocks + 2 * groups) * SUB, LANES), jnp.float32)]
        + [pltpu.VMEM((4, (pairs_y + 1) * SUB, LANES), jnp.float32)] * (2 * step),
        compiler_params=pltpu.CompilerParams(vmem_limit_bytes=GRANT),
        cost_estimate=pl.CostEstimate(flops=8 * 10**9, bytes_accessed=12 * 10**6, transcendentals=0),
        name="forward_narrow" if narrow else "forward_wide",
    )(field_a, field_b, depth, table, token)


def placed(space, *values):
    return [pltpu.with_memory_space_constraint(value, space) for value in values]


def each(refs):
    return [ref.at[i] for ref in refs for i in range(ref.shape[0])]


def middle_kernel(narrow, arrays, devices, sites, channels, count, pairs, signs, *refs):
    pieces, refs = each(refs[:arrays]), refs[arrays:]
    table_f, table_i, out, lines, hats, mixed, rows = refs
    groups = 1 if narrow else 2
    size = devices * sites
    both = 2 * size
    for s, piece in enumerate(pieces):
        for part in range(2):
            for g in range(groups):
                for x in range(sites):
                    at = part * size + s * sites + x
                    lines[g, pl.ds(at, SUB, stride=both), :] = piece[0, part, g, x * SUB : (x + 1) * SUB, :]
    for g in range(groups):
        for quad in range(2):
            tiles = [lines[g, (quad * 4 + j) * both : (quad * 4 + j + 1) * both, :] for j in range(4)]
            result = left_dot(table_f[...], jnp.concatenate(tiles, axis=1))
            for j in range(4):
                hat = result[:, j * LANES : (j + 1) * LANES]
                if narrow:
                    turned = pltpu.roll(hat, LANES // 2, axis=1)
                    places = ((quad, j, hat), (quad, j + SUB // 2, turned))
                else:
                    places = ((g, quad * 4 + j, hat),)
                for field, c, value in places:
                    hats[field * SUB + c] = value
                    if field:
                        hats[2 * SUB + c] = -value

    def channel(c, carry):
        def pair(p, totals):
            i = pairs[c, 2 * p]
            j = pairs[c, 2 * p + 1] + jnp.where(signs[c, p] < 0, 2 * SUB, SUB)
            a_re, a_im = hats[i, 0:size, :], hats[i, size:both, :]
            b_re, b_im = hats[j, 0:size, :], hats[j, size:both, :]
            return (
                totals[0] + (a_re * b_re + a_im * b_im),
                totals[1] + (a_im * b_re - a_re * b_im),
            )

        zero = jnp.zeros((size, LANES), jnp.float32)
        real, imag = lax.fori_loop(0, count, pair, (zero, zero), unroll=4)
        mixed[c, 0:size, :] = real
        mixed[c, size:both, :] = imag
        return carry

    lax.fori_loop(0, channels, channel, 0)
    if narrow:
        tiles = []
        for c in range(0, channels, 2):
            other = pltpu.roll(mixed[c + 1], LANES // 2, axis=1)
            tiles.append(jnp.where(lane_index(other.shape) < LANES // 2, mixed[c], other))
    else:
        tiles = [mixed[c] for c in range(channels)]
    result = left_dot(table_i[...], jnp.concatenate(tiles, axis=1))
    each_site = 2 * len(tiles)
    for t in range(len(tiles)):
        for part in range(2):
            value = result[part * size : (part + 1) * size, t * LANES : (t + 1) * LANES]
            first = 2 * t + part if narrow else part * channels + t
            rows[pl.ds(first, size, stride=each_site), :] = value
    for s in range(devices):
        out[s, 0] = rows[s * sites * each_site : (s + 1) * sites * each_site, :]


def middle(pieces, pairs, signs, table_f, table_i, sites, channels, narrow):
    size = table_f.shape[0] // 2
    devices = size // sites
    steps = pieces[0].shape[1]
    smem = pl.BlockSpec(memory_space=pltpu.SMEM)
    whole = lambda value: pl.BlockSpec(value.shape, lambda r: (0,) * value.ndim)
    third = lambda value: pl.BlockSpec(
        value.shape[:1] + (1,) + value.shape[2:], lambda r: (0, r) + (0,) * (value.ndim - 2)
    )
    rows = sites * (channels if narrow else 2 * channels)
    groups = 1 if narrow else 2
    return pl.pallas_call(
        functools.partial(middle_kernel, narrow, len(pieces), devices, sites, channels, signs.shape[1]),
        grid=(steps,),
        in_specs=[smem, smem] + [third(v) for v in pieces] + [whole(table_f), whole(table_i)],
        out_specs=pl.BlockSpec((devices, 1, rows, LANES), lambda r: (0, r, 0, 0)),
        out_shape=jax.ShapeDtypeStruct((devices, steps, rows, LANES), jnp.float32),
        scratch_shapes=[
            pltpu.VMEM((groups, (SUB + 1) * 2 * size, LANES), jnp.float32),
            pltpu.VMEM((3 * SUB, 2 * size, LANES), jnp.float32),
            pltpu.VMEM((channels, 2 * size, LANES), jnp.float32),
            pltpu.VMEM((devices * rows + SUB, LANES), jnp.float32),
        ],
        compiler_params=pltpu.CompilerParams(vmem_limit_bytes=SMALL_GRANT),
        cost_estimate=pl.CostEstimate(flops=4 * 10**9, bytes_accessed=10 * 10**6, transcendentals=0),
        name="middle_narrow" if narrow else "middle_wide",
    )(pairs, signs, *placed(pltpu.VMEM if narrow else pltpu.HBM, *pieces), *placed(pltpu.HBM, table_f, table_i))


def inverse_kernel(narrow, arrays, devices, channels, pairs_y, *refs):
    pieces, refs = each(refs[:arrays]), refs[arrays:]
    if narrow:
        table, depth, out, lines, staged = refs
        partial = out
    else:
        partial, table, depth, out, lines, staged = refs
    thirds = pieces[0].shape[0]
    size = thirds * devices

    @pl.when(pl.program_id(0) == 0)
    def _():
        for s in range(devices):
            for r in range(thirds):
                for v in range(pieces[s].shape[1] // SUB):
                    start = v * SUB * size + r * devices + s
                    lines[pl.ds(start, SUB, stride=size), :] = pieces[s][r, v * SUB : (v + 1) * SUB, :]

    step = partial.shape[0]
    for site in range(step):
        x = pl.program_id(0) * step + site
        place = None if narrow else out.at[0, site]
        inverse_site(narrow, channels, pairs_y, size, x, lines, table, depth, staged.at[site], partial.at[site], place)


def inverse_site(narrow, channels, pairs_y, size, x, lines, table, depth, staged, partial, out):
    def tile(*spots):
        return jnp.concatenate([lines[pl.ds(pl.multiple_of(k * size, SUB), size), :] for k in spots], axis=0)

    if narrow:
        tiles = [tile(x * channels + 2 * c, x * channels + 2 * c + 1) for c in range(channels // 2)]
        width, sets = LANES // 4, [range(parity, channels, 2) for parity in range(2)]
    else:
        big = 2 * x * channels
        tiles = [tile(big + c, big + channels + c) for c in range(channels)]
        width, sets = LANES // 2, [range(channels)]
    result = left_dot(table[...], jnp.concatenate(tiles, axis=1))
    half = result.shape[0] // 2
    first, second = result[:half], result[half:]
    high, low = split(jnp.where(lane_index(first.shape) & width == 0, first, second))

    def rows_of(value, e, c):
        spot = c // 2 if narrow else c
        return jnp.concatenate(
            [
                value[(2 * part + e) * pairs_y : (2 * part + e + 1) * pairs_y, spot * LANES : (spot + 1) * LANES]
                for part in range(2)
            ],
            axis=1,
        )

    for k, members in enumerate(sets):
        products = []
        for e in range(2):
            left = [jnp.concatenate([rows_of(value, e, c) for c in members], axis=0) for value in (high, low)]
            products.append(dot(jnp.concatenate([left[0], left[1], left[0]], axis=1), depth[k, e]))
        for i, c in enumerate(members):
            rows = slice(i * pairs_y, (i + 1) * pairs_y)
            zero, one = products[0][rows], products[1][rows]
            for q, value in enumerate((zero[:, :LANES], zero[:, LANES:] + one[:, :LANES], one[:, LANES:])):
                staged[q, pl.ds(c, pairs_y, stride=channels), :] = value
    if narrow:
        partial[...] = staged[:, : partial.shape[1], :]
    else:
        for p in range(pairs_y):
            rows = slice(p * channels, (p + 1) * channels)
            for q in range(3):
                lanes = slice((3 * p + q) * LANES, (3 * p + q + 1) * LANES)
                out[:, lanes] = staged[q, rows, :] + partial[q, rows, :]


def inverse(pieces, partial, table, depth, sites, channels, flat, share=0, shares=1):
    narrow = partial is None
    size = table.shape[1] // 6
    devices = size // pieces[0].shape[1]
    whole = lambda value: pl.BlockSpec(value.shape, lambda x: (0,) * value.ndim)
    tiles = (3, size * channels, LANES)
    rows = pieces[0].shape[2] // shares
    sites = sites // shares
    lines = pltpu.VMEM(((rows + 1) * size, LANES), jnp.float32)
    part = lambda value: pl.BlockSpec(value.shape[:2] + (rows, LANES), lambda x: (0, 0, share, 0))
    step = 3 if sites % 3 == 0 else 1
    kept = pl.BlockSpec((step,) + tiles, lambda x: (x + share * sites // step, 0, 0, 0))
    return pl.pallas_call(
        functools.partial(inverse_kernel, narrow, len(pieces), devices, channels, size),
        grid=(sites // step,),
        in_specs=[part(v) for v in pieces] + ([] if narrow else [kept]) + [whole(table), whole(depth)],
        out_specs=kept if narrow else pl.BlockSpec((1, step, channels, flat), lambda x: (0, x, 0, 0)),
        out_shape=jax.ShapeDtypeStruct((sites,) + tiles if narrow else (1, sites, channels, flat), jnp.float32),
        scratch_shapes=[lines, pltpu.VMEM((step, 3, size * channels + SUB, LANES), jnp.float32)],
        compiler_params=pltpu.CompilerParams(vmem_limit_bytes=SMALL_GRANT),
        cost_estimate=pl.CostEstimate(flops=4 * 10**9, bytes_accessed=6 * 10**6, transcendentals=0),
        name="inverse_narrow" if narrow else "inverse_wide",
    )(*placed(pltpu.VMEM, *pieces), *([] if narrow else placed(pltpu.VMEM, partial)), *placed(pltpu.HBM if narrow else pltpu.VMEM, table, depth))


AT_ONCE = dict(sent_narrow=True, sent_wide=True, back_narrow=True, back_wide=True)


def exchange(packed, at_once):
    if at_once:
        return [lax.all_to_all(packed, "space", 0, 0, tiled=True)]
    devices = packed.shape[0]
    order = sorted(range(1, devices), key=lambda s: (s % 4, -(s // 8), s))
    got = [packed[:1]] + [None] * (devices - 1)
    for s in order:
        got[s] = lax.ppermute(packed[s : s + 1], "space", [(i, i ^ s) for i in range(devices)])
    return got


def fast_slice(field_a, field_b, pairs, signs, tables):
    _, sites, components, flat = field_a.shape
    devices = lax.axis_size("space")
    channels = pairs.shape[0]
    me = lax.axis_index("space")
    mine = [lax.dynamic_index_in_dim(jnp.asarray(t), me, 0, False) for t in tables[:4]]
    fixed = [jnp.asarray(t[0]) for t in tables[:4]]

    def table(which, name):
        return (fixed if AT_ONCE[name] else mine)[which]

    depth_n, depth_w, depth_in, depth_iw = (jnp.asarray(t) for t in tables[4:])
    thirds = tables[0].shape[1] // 4 // devices
    flat_pairs = pairs.reshape(channels, -1)
    sent = {}
    token = signs
    for narrow, depth in ((True, depth_n), (False, depth_w)):
        name = "sent_narrow" if narrow else "sent_wide"
        groups = 1 if narrow else 2
        packed = forward(field_a, field_b, depth, table(0, name), narrow, token)
        token = packed[0, 0]
        packed = packed.reshape(devices, thirds, 2, groups, sites * SUB, LANES)
        sent[narrow] = exchange(packed, AT_ONCE[name])
    partial = None
    shares = 2 if sites % 2 == 0 and sites // 2 * 2 * channels % SUB == 0 else 1
    for narrow, depth in ((True, depth_in), (False, depth_iw)):
        come, go = ("sent_narrow", "back_narrow") if narrow else ("sent_wide", "back_wide")
        mixed = middle(sent[narrow], flat_pairs, signs, table(2, come), table(3, go), sites, channels, narrow)
        back = exchange(mixed, AT_ONCE[go])
        shared = functools.partial(inverse, back, partial, table(1, go), depth, sites, channels, flat)
        if narrow:
            partial = shared()
    return [shared(share, shares) for share in range(shares)]


def neighbours(value):
    devices, length = lax.axis_size("tm"), value.shape[0]
    up = [(i, (i + 1) % devices) for i in range(devices)]
    down = [(j, i) for i, j in up]
    after = lax.ppermute(value[:1], "tm", down)
    before = after if devices == 2 and length == 1 else lax.ppermute(value[-1:], "tm", up)
    later = jnp.concatenate([value[1:], after], axis=0)
    earlier = jnp.concatenate([before, value[:-1]], axis=0)
    return later, earlier


def differences(correlator):
    later, earlier = neighbours(correlator)
    return correlator, later - correlator, later - 2.0 * correlator + earlier


def differences_kernel(count, own, *refs):
    later, earlier = refs[0], refs[count - 1]
    outs = refs[-3:]
    outs[0][...] = own[...]
    outs[1][...] = later[...] - own[...]
    outs[2][...] = later[...] - 2.0 * own[...] + earlier[...]


def write_differences(own, others, share, shares, written):
    _, sites, channels, flat = own.shape
    block = (1, 1, channels, flat)
    mine = pl.BlockSpec(block, lambda x: (0, x, 0, 0))
    shape = jax.ShapeDtypeStruct((1, sites * shares, channels, flat), jnp.float32)
    count = len(others)
    return pl.pallas_call(
        functools.partial(differences_kernel, count),
        grid=(sites,),
        in_specs=[mine] * (1 + count) + [pl.BlockSpec(memory_space=pl.ANY)] * len(written),
        out_specs=[pl.BlockSpec(block, lambda x: (0, x + share * sites, 0, 0))] * 3,
        out_shape=[shape] * 3,
        input_output_aliases={1 + count + k: k for k in range(len(written))},
        compiler_params=pltpu.CompilerParams(vmem_limit_bytes=SMALL_GRANT),
        cost_estimate=pl.CostEstimate(flops=10**6, bytes_accessed=5 * own.size * 4, transcendentals=0),
        name="differences",
    )(own, *others, *written)


def one_time(tables, field_a, field_b, pairs, signs):
    devices = lax.axis_size("tm")
    up = [(i, (i + 1) % devices) for i in range(devices)]
    shares = fast_slice(field_a, field_b, pairs, signs, tables)
    written = []
    for share, own in enumerate(shares):
        others = [lax.ppermute(own, "tm", [(j, i) for i, j in up])]
        if devices != 2:
            others.append(lax.ppermute(own, "tm", up))
        written = write_differences(own, others, share, len(shares), written)
    return written


def fast_device(tables, field_a, field_b, pairs, signs):
    field_a, field_b = field_a.swapaxes(1, 2), field_b.swapaxes(1, 2)
    if field_a.shape[0] == 1:
        outs = one_time(tables, field_a, field_b, pairs, signs)
    else:
        parts = [
            jnp.concatenate(fast_slice(field_a[t : t + 1], field_b[t : t + 1], pairs, signs, tables), axis=1)
            for t in range(field_a.shape[0])
        ]
        outs = differences(jnp.concatenate(parts, axis=0))
    return tuple(out.swapaxes(1, 2) for out in outs)


def dft_tables(length):
    cos, sin = unitary(length)
    return jnp.asarray(cos, jnp.float32), jnp.asarray(sin, jnp.float32)


def swap_parts(values):
    half = values.shape[-1] // 2
    return jnp.concatenate([values[..., half:], -values[..., :half]], axis=-1)


def along_depth(values, inverse):
    cosines, sines = dft_tables(values.shape[-1] // 2)
    matrix = jnp.block([[cosines, -sines], [sines, cosines]])
    if inverse:
        return jnp.einsum("tcxyr,kr->tcxyk", values, matrix, precision=highest)
    return jnp.einsum("tcxyr,rk->tcxyk", values, matrix, precision=highest)


def along(values, sign, axis):
    cosines, sines = dft_tables(values.shape[axis])
    table = jnp.concatenate([cosines, sign * sines], axis=1)
    stacked = jnp.concatenate([values, swap_parts(values)], axis=axis)
    spec = "ky,tcxyr->tcxkr" if axis == 3 else "kx,tcxyr->tckyr"
    return jnp.einsum(spec, table, stacked, precision=highest)


def contract(weights, hat_a, hat_b):
    depth = hat_a.shape[-1] // 2
    outputs = []
    for channel in range(weights.shape[0]):
        mixed_b = jnp.einsum("ij,tjxyk->tixyk", weights[channel], hat_b, precision=highest)
        direct = jnp.sum(hat_a * mixed_b, axis=1)
        crossed = jnp.sum(hat_a * swap_parts(mixed_b), axis=1)
        real_part = direct[..., :depth] + direct[..., depth:]
        imag_part = -(crossed[..., :depth] + crossed[..., depth:])
        outputs.append(jnp.concatenate([real_part, imag_part], axis=-1))
    return jnp.stack(outputs, axis=1)


def any_device(depth, field_a, field_b, pairs, signs):
    as_five = lambda v: v.reshape(v.shape[:3] + (-1, 2 * depth))
    as_four = lambda v: v.reshape(v.shape[:3] + (-1,))
    indices = jnp.arange(field_a.shape[1], dtype=jnp.int32)
    first = (pairs[:, :, 0][:, :, None] == indices).astype(jnp.float32)
    second = (pairs[:, :, 1][:, :, None] == indices).astype(jnp.float32)
    weights = jnp.einsum("cp,cpi,cpj->cij", signs.astype(jnp.float32), first, second, precision=highest)
    hats = []
    for field in (field_a, field_b):
        partial = as_four(along(along_depth(as_five(field), False), 1.0, 3))
        lines = lax.all_to_all(partial, "space", split_axis=3, concat_axis=2, tiled=True)
        hats.append(along(as_five(lines), 1.0, 2))
    returned = as_four(along(contract(weights, *hats), -1.0, 2))
    sites = lax.all_to_all(returned, "space", split_axis=2, concat_axis=3, tiled=True)
    return differences(as_four(along_depth(along(as_five(sites), -1.0, 3), True)))


def solution(mesh):
    devices = mesh.shape["space"]
    times = mesh.shape["tm"]

    def program(field_a, field_b, pairs, signs):
        _, components, size, flat = field_a.shape
        depth = flat // size // 2
        wide = LANES // 2
        fits = (
            depth == size
            and 2 * depth == 3 * wide
            and components == SUB
            and pairs.shape[0] == 4
            and size % (2 * devices) == 0
            and devices & (devices - 1) == 0
            and (size // devices) * 4 % SUB == 0
            and size % (2 * SUB) == 0
        )
        if fits:
            tables = (
                rows_forward(devices, size),
                rows_inverse(devices, size),
                columns_forward(devices, size),
                columns_inverse(devices, size),
                depth_forward(depth, wide, depth - wide),
                depth_forward(depth, 0, wide),
                depth_inverse(depth, wide, depth - wide, 2),
                depth_inverse(depth, 0, wide, 1),
            )
            per_device = functools.partial(fast_device, tables)
        else:
            per_device = functools.partial(any_device, depth)
        spec = P("tm", None, "space", None)
        return jax.shard_map(
            per_device,
            mesh=mesh,
            in_specs=(spec, spec, P(), P()),
            out_specs=(spec, spec, spec),
            check_vma=False,
        )(field_a, field_b, pairs, signs)

    return program
```

```python
import functools
import math

import jax
import jax.numpy as jnp
import ml_dtypes
import numpy as np
from jax import lax
from jax.experimental import pallas as pl
from jax.experimental.pallas import tpu as pltpu
from jax.sharding import PartitionSpec as P

highest = lax.Precision.HIGHEST
LANES = 128
SUB = 8
GRANT = 56 << 20
SMALL_GRANT = 24 << 20


def unitary(length):
    index = np.arange(length)
    angle = (index[:, None] * index[None, :] % length) * (2.0 * np.pi / length)
    return np.cos(angle) / math.sqrt(length), np.sin(angle) / math.sqrt(length)


def halves(table):
    high = table.astype(np.float32).astype(ml_dtypes.bfloat16)
    low = (table - high.astype(np.float64)).astype(np.float32).astype(ml_dtypes.bfloat16)
    return high, low


def left_table(table):
    high, low = halves(table)
    return np.concatenate([high, high, low], axis=1)


def right_table(table):
    high, low = halves(table)
    return np.concatenate([high, high, low], axis=0)


def owned(devices, length):
    each = length // devices
    me = np.arange(devices)
    return ((me[:, None] ^ me[None, :]) * each)[:, :, None] + np.arange(each)


def rows_forward(devices, length):
    cos, sin = unitary(length)
    out = []
    for spots in owned(devices, length):
        k = spots.reshape(devices, -1, 2).transpose(2, 0, 1).reshape(-1)
        y = np.arange(length).reshape(-1, 2).T.reshape(-1)
        c, s = cos[k][:, y], sin[k][:, y]
        out.append(left_table(np.block([[c, s], [-s, c]])))
    return np.stack(out)


def rows_inverse(devices, length):
    cos, sin = unitary(length)
    out = []
    for spots in owned(devices, length):
        y = np.arange(length).reshape(-1, 2).T.reshape(-1)
        blocks = []
        for e in range(2):
            k = spots.reshape(devices, -1, 2)[:, :, e].T.reshape(-1)
            c, s = cos[y][:, k], sin[y][:, k]
            blocks.append(np.block([[c, -s], [s, c]]))
        out.append(left_table(np.concatenate(blocks)))
    return np.stack(out)


def columns_forward(devices, length):
    cos, sin = unitary(length)
    out = []
    for spots in owned(devices, length):
        c, s = cos[:, spots.reshape(-1)], sin[:, spots.reshape(-1)]
        out.append(left_table(np.block([[c, s], [-s, c]])))
    return np.stack(out)


def columns_inverse(devices, length):
    cos, sin = unitary(length)
    out = []
    for spots in owned(devices, length):
        c, s = cos[spots.reshape(-1)], sin[spots.reshape(-1)]
        out.append(left_table(np.block([[c, -s], [s, c]])))
    return np.stack(out)


def depth_forward(length, first, count):
    cos, sin = unitary(length)
    k = np.tile(np.arange(first, first + count), LANES // count)
    matrix = np.block([[cos[:, k], -sin[:, k]], [sin[:, k], cos[:, k]]])
    gap = np.zeros((2 * LANES - 2 * length, 2 * LANES))
    both = np.stack([np.concatenate([matrix, gap]), np.concatenate([gap, matrix])])
    return np.stack([right_table(b) for b in both])


def depth_inverse(length, first, count, halves_of):
    cos, sin = unitary(length)
    k = np.tile(np.arange(first, first + count), LANES // count)
    out = []
    for half in range(halves_of):
        keep = (np.arange(LANES) * halves_of // LANES == half)[:, None] * 1.0
        matrix = np.block([[cos[k] * keep, sin[k] * keep], [-sin[k] * keep, cos[k] * keep]])
        gap = np.zeros((matrix.shape[0], 2 * LANES - 2 * length))
        both = (np.concatenate([matrix, gap], axis=1), np.concatenate([gap, matrix], axis=1))
        out.append(np.stack([np.concatenate(halves(b)) for b in both]))
    return np.stack(out)


def split(value):
    high = value.astype(jnp.bfloat16)
    return high, (value - high.astype(jnp.float32)).astype(jnp.bfloat16)


def dot(left, right):
    return jnp.dot(left, right, preferred_element_type=jnp.float32)


def left_dot(table, value):
    high, low = split(value)
    return dot(table, jnp.concatenate([high, low, high], axis=0))


def lane_index(shape):
    return lax.broadcasted_iota(jnp.int32, shape, len(shape) - 1)


def forward_kernel(narrow, sites, pairs_y, field_a, field_b, depth, table, token, out, packed, *spectra):
    for site in range(field_a.shape[1]):
        spaces = spectra[2 * site], spectra[2 * site + 1]
        forward_site(narrow, pairs_y, field_a.at[0, site], field_b.at[0, site], depth, table, packed.at[site], spaces)
        for block in range(out.shape[0]):
            out[block, site] = packed[site, block * SUB : (block + 1) * SUB, :]


def forward_site(narrow, pairs_y, field_a, field_b, depth, table, packed, spectra):
    groups = 1 if narrow else 2
    width = LANES // 4 if narrow else LANES // 2
    block = 2 * groups * SUB
    slots = []
    for group, field in enumerate((field_a, field_b)):
        tiles = [
            jnp.concatenate(
                [field[:, (3 * p + q) * LANES : (3 * p + q + 1) * LANES] for p in range(pairs_y)], axis=0
            )
            for q in range(3)
        ]
        tiles = [split(tile) for tile in tiles]
        for e in range(2):
            left = [tiles[e + k][part] for part in (0, 1, 0) for k in range(2)]
            result = dot(jnp.concatenate(left, axis=1), depth[e])
            for part in range(2):
                spectra[group][part * 2 + e, : result.shape[0]] = result[:, part * LANES : (part + 1) * LANES]

        def rows_of(c, group=group):
            return jnp.concatenate(
                [spectra[group][k, pl.ds(c, pairs_y, stride=SUB), :] for k in range(4)], axis=0
            )

        if narrow:
            for c in range(SUB // 2):
                first, second = rows_of(c), rows_of(c + SUB // 2)
                pick = lane_index(first.shape) < LANES // 2
                slots.append((0, group * 4 + c, jnp.where(pick, first, second)))
        else:
            slots += [(group, c, rows_of(c)) for c in range(SUB)]

    for first in range(0, len(slots), SUB):
        batch = slots[first : first + SUB]
        result = left_dot(table[...], jnp.concatenate([value for _, _, value in batch], axis=1))
        half = result.shape[0] // 4
        for part in range(2):
            even = result[2 * part * half : (2 * part + 1) * half]
            odd = result[(2 * part + 1) * half : (2 * part + 2) * half]
            merged = jnp.where(lane_index(even.shape) // width % 2 == 0, even, odd)
            for i, (group, slot, _) in enumerate(batch):
                start = (part * groups + group) * SUB + slot
                packed[pl.ds(start, half, stride=block), :] = merged[:, i * LANES : (i + 1) * LANES]


def forward(field_a, field_b, depth, table, narrow, token):
    _, sites, components, flat = field_a.shape
    groups = 1 if narrow else 2
    size = table.shape[0] // 2
    pairs_y = size // 2
    lines = size // 2
    blocks = lines * 2 * groups
    step = 1
    spot = pl.BlockSpec((1, step, components, flat), lambda x: (0, x, 0, 0))
    whole = lambda value: pl.BlockSpec(value.shape, lambda x: (0,) * value.ndim)
    return pl.pallas_call(
        functools.partial(forward_kernel, narrow, sites, pairs_y),
        grid=(sites // step,),
        in_specs=[spot, spot, whole(depth), whole(table), pl.BlockSpec(memory_space=pl.ANY)],
        out_specs=pl.BlockSpec((blocks, step, SUB, LANES), lambda x: (0, x, 0, 0)),
        out_shape=jax.ShapeDtypeStruct((blocks, sites, SUB, LANES), jnp.float32),
        scratch_shapes=[pltpu.VMEM((step, (blocks + 2 * groups) * SUB, LANES), jnp.float32)]
        + [pltpu.VMEM((4, (pairs_y + 1) * SUB, LANES), jnp.float32)] * (2 * step),
        compiler_params=pltpu.CompilerParams(vmem_limit_bytes=GRANT),
        cost_estimate=pl.CostEstimate(flops=8 * 10**9, bytes_accessed=12 * 10**6, transcendentals=0),
        name="forward_narrow" if narrow else "forward_wide",
    )(field_a, field_b, depth, table, token)


def placed(space, *values):
    return [pltpu.with_memory_space_constraint(value, space) for value in values]


def each(refs):
    return [ref.at[i] for ref in refs for i in range(ref.shape[0])]


def middle_kernel(narrow, arrays, devices, sites, channels, count, pairs, signs, *refs):
    pieces, refs = each(refs[:arrays]), refs[arrays:]
    table_f, table_i, out, lines, hats, mixed, rows = refs
    groups = 1 if narrow else 2
    size = devices * sites
    both = 2 * size
    for s, piece in enumerate(pieces):
        for part in range(2):
            for g in range(groups):
                for x in range(sites):
                    at = part * size + s * sites + x
                    lines[g, pl.ds(at, SUB, stride=both), :] = piece[0, part, g, x * SUB : (x + 1) * SUB, :]
    for g in range(groups):
        for quad in range(2):
            tiles = [lines[g, (quad * 4 + j) * both : (quad * 4 + j + 1) * both, :] for j in range(4)]
            result = left_dot(table_f[...], jnp.concatenate(tiles, axis=1))
            for j in range(4):
                hat = result[:, j * LANES : (j + 1) * LANES]
                if narrow:
                    turned = pltpu.roll(hat, LANES // 2, axis=1)
                    places = ((quad, j, hat), (quad, j + SUB // 2, turned))
                else:
                    places = ((g, quad * 4 + j, hat),)
                for field, c, value in places:
                    hats[field * SUB + c] = value
                    if field:
                        hats[2 * SUB + c] = -value

    def channel(c, carry):
        def pair(p, totals):
            i = pairs[c, 2 * p]
            j = pairs[c, 2 * p + 1] + jnp.where(signs[c, p] < 0, 2 * SUB, SUB)
            a_re, a_im = hats[i, 0:size, :], hats[i, size:both, :]
            b_re, b_im = hats[j, 0:size, :], hats[j, size:both, :]
            return (
                totals[0] + (a_re * b_re + a_im * b_im),
                totals[1] + (a_im * b_re - a_re * b_im),
            )

        zero = jnp.zeros((size, LANES), jnp.float32)
        real, imag = lax.fori_loop(0, count, pair, (zero, zero), unroll=4)
        mixed[c, 0:size, :] = real
        mixed[c, size:both, :] = imag
        return carry

    lax.fori_loop(0, channels, channel, 0)
    if narrow:
        tiles = []
        for c in range(0, channels, 2):
            other = pltpu.roll(mixed[c + 1], LANES // 2, axis=1)
            tiles.append(jnp.where(lane_index(other.shape) < LANES // 2, mixed[c], other))
    else:
        tiles = [mixed[c] for c in range(channels)]
    result = left_dot(table_i[...], jnp.concatenate(tiles, axis=1))
    each_site = 2 * len(tiles)
    for t in range(len(tiles)):
        for part in range(2):
            value = result[part * size : (part + 1) * size, t * LANES : (t + 1) * LANES]
            first = 2 * t + part if narrow else part * channels + t
            rows[pl.ds(first, size, stride=each_site), :] = value
    for s in range(devices):
        out[s, 0] = rows[s * sites * each_site : (s + 1) * sites * each_site, :]


def middle(pieces, pairs, signs, table_f, table_i, sites, channels, narrow):
    size = table_f.shape[0] // 2
    devices = size // sites
    steps = pieces[0].shape[1]
    smem = pl.BlockSpec(memory_space=pltpu.SMEM)
    whole = lambda value: pl.BlockSpec(value.shape, lambda r: (0,) * value.ndim)
    third = lambda value: pl.BlockSpec(
        value.shape[:1] + (1,) + value.shape[2:], lambda r: (0, r) + (0,) * (value.ndim - 2)
    )
    rows = sites * (channels if narrow else 2 * channels)
    groups = 1 if narrow else 2
    return pl.pallas_call(
        functools.partial(middle_kernel, narrow, len(pieces), devices, sites, channels, signs.shape[1]),
        grid=(steps,),
        in_specs=[smem, smem] + [third(v) for v in pieces] + [whole(table_f), whole(table_i)],
        out_specs=pl.BlockSpec((devices, 1, rows, LANES), lambda r: (0, r, 0, 0)),
        out_shape=jax.ShapeDtypeStruct((devices, steps, rows, LANES), jnp.float32),
        scratch_shapes=[
            pltpu.VMEM((groups, (SUB + 1) * 2 * size, LANES), jnp.float32),
            pltpu.VMEM((3 * SUB, 2 * size, LANES), jnp.float32),
            pltpu.VMEM((channels, 2 * size, LANES), jnp.float32),
            pltpu.VMEM((devices * rows + SUB, LANES), jnp.float32),
        ],
        compiler_params=pltpu.CompilerParams(vmem_limit_bytes=SMALL_GRANT),
        cost_estimate=pl.CostEstimate(flops=4 * 10**9, bytes_accessed=10 * 10**6, transcendentals=0),
        name="middle_narrow" if narrow else "middle_wide",
    )(pairs, signs, *placed(pltpu.VMEM if narrow else pltpu.HBM, *pieces), *placed(pltpu.HBM, table_f, table_i))


def inverse_kernel(narrow, arrays, devices, channels, pairs_y, *refs):
    pieces, refs = each(refs[:arrays]), refs[arrays:]
    if narrow:
        table, depth, out, lines, staged = refs
        partial = out
    else:
        partial, table, depth, out, lines, staged = refs
    thirds = pieces[0].shape[0]
    size = thirds * devices

    @pl.when(pl.program_id(0) == 0)
    def _():
        for s in range(devices):
            for r in range(thirds):
                for v in range(pieces[s].shape[1] // SUB):
                    start = v * SUB * size + r * devices + s
                    lines[pl.ds(start, SUB, stride=size), :] = pieces[s][r, v * SUB : (v + 1) * SUB, :]

    step = partial.shape[0]
    for site in range(step):
        x = pl.program_id(0) * step + site
        place = None if narrow else out.at[0, site]
        inverse_site(narrow, channels, pairs_y, size, x, lines, table, depth, staged.at[site], partial.at[site], place)


def inverse_site(narrow, channels, pairs_y, size, x, lines, table, depth, staged, partial, out):
    def tile(*spots):
        return jnp.concatenate([lines[pl.ds(pl.multiple_of(k * size, SUB), size), :] for k in spots], axis=0)

    if narrow:
        tiles = [tile(x * channels + 2 * c, x * channels + 2 * c + 1) for c in range(channels // 2)]
        width, sets = LANES // 4, [range(parity, channels, 2) for parity in range(2)]
    else:
        big = 2 * x * channels
        tiles = [tile(big + c, big + channels + c) for c in range(channels)]
        width, sets = LANES // 2, [range(channels)]
    result = left_dot(table[...], jnp.concatenate(tiles, axis=1))
    half = result.shape[0] // 2
    first, second = result[:half], result[half:]
    high, low = split(jnp.where(lane_index(first.shape) & width == 0, first, second))

    def rows_of(value, e, c):
        spot = c // 2 if narrow else c
        return jnp.concatenate(
            [
                value[(2 * part + e) * pairs_y : (2 * part + e + 1) * pairs_y, spot * LANES : (spot + 1) * LANES]
                for part in range(2)
            ],
            axis=1,
        )

    for k, members in enumerate(sets):
        products = []
        for e in range(2):
            left = [jnp.concatenate([rows_of(value, e, c) for c in members], axis=0) for value in (high, low)]
            high_rows, low_rows = depth[k, e, : 2 * LANES], depth[k, e, 2 * LANES :]
            right = jnp.concatenate([high_rows, high_rows, low_rows], axis=0)
            products.append(dot(jnp.concatenate([left[0], left[1], left[0]], axis=1), right))
        for i, c in enumerate(members):
            rows = slice(i * pairs_y, (i + 1) * pairs_y)
            zero, one = products[0][rows], products[1][rows]
            for q, value in enumerate((zero[:, :LANES], zero[:, LANES:] + one[:, :LANES], one[:, LANES:])):
                staged[q, pl.ds(c, pairs_y, stride=channels), :] = value
    if narrow:
        partial[...] = staged[:, : partial.shape[1], :]
    else:
        for p in range(pairs_y):
            rows = slice(p * channels, (p + 1) * channels)
            for q in range(3):
                lanes = slice((3 * p + q) * LANES, (3 * p + q + 1) * LANES)
                out[:, lanes] = staged[q, rows, :] + partial[q, rows, :]


def inverse(pieces, partial, table, depth, sites, channels, flat, share=0, shares=1):
    narrow = partial is None
    size = table.shape[1] // 6
    devices = size // pieces[0].shape[1]
    whole = lambda value: pl.BlockSpec(value.shape, lambda x: (0,) * value.ndim)
    tiles = (3, size * channels, LANES)
    rows = pieces[0].shape[2] // shares
    sites = sites // shares
    lines = pltpu.VMEM(((rows + 1) * size, LANES), jnp.float32)
    part = lambda value: pl.BlockSpec(value.shape[:2] + (rows, LANES), lambda x: (0, 0, share, 0))
    step = 3 if sites % 3 == 0 else 1
    kept = pl.BlockSpec((step,) + tiles, lambda x: (x + share * sites // step, 0, 0, 0))
    return pl.pallas_call(
        functools.partial(inverse_kernel, narrow, len(pieces), devices, channels, size),
        grid=(sites // step,),
        in_specs=[part(v) for v in pieces] + ([] if narrow else [kept]) + [whole(table), whole(depth)],
        out_specs=kept if narrow else pl.BlockSpec((1, step, channels, flat), lambda x: (0, x, 0, 0)),
        out_shape=jax.ShapeDtypeStruct((sites,) + tiles if narrow else (1, sites, channels, flat), jnp.float32),
        scratch_shapes=[lines, pltpu.VMEM((step, 3, size * channels + SUB, LANES), jnp.float32)],
        compiler_params=pltpu.CompilerParams(vmem_limit_bytes=SMALL_GRANT),
        cost_estimate=pl.CostEstimate(flops=4 * 10**9, bytes_accessed=6 * 10**6, transcendentals=0),
        name="inverse_narrow" if narrow else "inverse_wide",
    )(*placed(pltpu.VMEM, *pieces), *([] if narrow else placed(pltpu.VMEM, partial)), *placed(pltpu.HBM if narrow else pltpu.VMEM, table, depth))


AT_ONCE = dict(sent_narrow=True, sent_wide=True, back_narrow=True, back_wide=True)


def exchange(packed, at_once):
    if at_once:
        return [lax.all_to_all(packed, "space", 0, 0, tiled=True)]
    devices = packed.shape[0]
    order = sorted(range(1, devices), key=lambda s: (s % 4, -(s // 8), s))
    got = [packed[:1]] + [None] * (devices - 1)
    for s in order:
        got[s] = lax.ppermute(packed[s : s + 1], "space", [(i, i ^ s) for i in range(devices)])
    return got


def fast_slice(field_a, field_b, pairs, signs, tables):
    _, sites, components, flat = field_a.shape
    devices = lax.axis_size("space")
    channels = pairs.shape[0]
    me = lax.axis_index("space")
    mine = [lax.dynamic_index_in_dim(jnp.asarray(t), me, 0, False) for t in tables[:4]]
    fixed = [jnp.asarray(t[0]) for t in tables[:4]]

    def table(which, name):
        return (fixed if AT_ONCE[name] else mine)[which]

    depth_n, depth_w, depth_in, depth_iw = (jnp.asarray(t) for t in tables[4:])
    thirds = tables[0].shape[1] // 4 // devices
    flat_pairs = pairs.reshape(channels, -1)
    sent = {}
    token = signs
    for narrow, depth in ((True, depth_n), (False, depth_w)):
        name = "sent_narrow" if narrow else "sent_wide"
        groups = 1 if narrow else 2
        packed = forward(field_a, field_b, depth, table(0, name), narrow, token)
        token = packed[0, 0]
        packed = packed.reshape(devices, thirds, 2, groups, sites * SUB, LANES)
        sent[narrow] = exchange(packed, AT_ONCE[name])
    partial = None
    shares = 2 if sites % 2 == 0 and sites // 2 * 2 * channels % SUB == 0 else 1
    for narrow, depth in ((True, depth_in), (False, depth_iw)):
        come, go = ("sent_narrow", "back_narrow") if narrow else ("sent_wide", "back_wide")
        mixed = middle(sent[narrow], flat_pairs, signs, table(2, come), table(3, go), sites, channels, narrow)
        back = exchange(mixed, AT_ONCE[go])
        shared = functools.partial(inverse, back, partial, table(1, go), depth, sites, channels, flat)
        if narrow:
            partial = shared()
    return [shared(share, shares) for share in range(shares)]


def neighbours(value):
    devices, length = lax.axis_size("tm"), value.shape[0]
    up = [(i, (i + 1) % devices) for i in range(devices)]
    down = [(j, i) for i, j in up]
    after = lax.ppermute(value[:1], "tm", down)
    before = after if devices == 2 and length == 1 else lax.ppermute(value[-1:], "tm", up)
    later = jnp.concatenate([value[1:], after], axis=0)
    earlier = jnp.concatenate([before, value[:-1]], axis=0)
    return later, earlier


def differences(correlator):
    later, earlier = neighbours(correlator)
    return correlator, later - correlator, later - 2.0 * correlator + earlier


def differences_kernel(count, own, *refs):
    later, earlier = refs[0], refs[count - 1]
    outs = refs[-3:]
    outs[0][...] = own[...]
    outs[1][...] = later[...] - own[...]
    outs[2][...] = later[...] - 2.0 * own[...] + earlier[...]


def write_differences(own, others, share, shares, written):
    _, sites, channels, flat = own.shape
    block = (1, 1, channels, flat)
    mine = pl.BlockSpec(block, lambda x: (0, x, 0, 0))
    shape = jax.ShapeDtypeStruct((1, sites * shares, channels, flat), jnp.float32)
    count = len(others)
    return pl.pallas_call(
        functools.partial(differences_kernel, count),
        grid=(sites,),
        in_specs=[mine] * (1 + count) + [pl.BlockSpec(memory_space=pl.ANY)] * len(written),
        out_specs=[pl.BlockSpec(block, lambda x: (0, x + share * sites, 0, 0))] * 3,
        out_shape=[shape] * 3,
        input_output_aliases={1 + count + k: k for k in range(len(written))},
        compiler_params=pltpu.CompilerParams(vmem_limit_bytes=SMALL_GRANT),
        cost_estimate=pl.CostEstimate(flops=10**6, bytes_accessed=5 * own.size * 4, transcendentals=0),
        name="differences",
    )(own, *others, *written)


def one_time(tables, field_a, field_b, pairs, signs):
    devices = lax.axis_size("tm")
    up = [(i, (i + 1) % devices) for i in range(devices)]
    shares = fast_slice(field_a, field_b, pairs, signs, tables)
    written = []
    for share, own in enumerate(shares):
        others = [lax.ppermute(own, "tm", [(j, i) for i, j in up])]
        if devices != 2:
            others.append(lax.ppermute(own, "tm", up))
        written = write_differences(own, others, share, len(shares), written)
    return written


def fast_device(tables, field_a, field_b, pairs, signs):
    field_a, field_b = field_a.swapaxes(1, 2), field_b.swapaxes(1, 2)
    if field_a.shape[0] == 1:
        outs = one_time(tables, field_a, field_b, pairs, signs)
    else:
        parts = [
            jnp.concatenate(fast_slice(field_a[t : t + 1], field_b[t : t + 1], pairs, signs, tables), axis=1)
            for t in range(field_a.shape[0])
        ]
        outs = differences(jnp.concatenate(parts, axis=0))
    return tuple(out.swapaxes(1, 2) for out in outs)


def dft_tables(length):
    cos, sin = unitary(length)
    return jnp.asarray(cos, jnp.float32), jnp.asarray(sin, jnp.float32)


def swap_parts(values):
    half = values.shape[-1] // 2
    return jnp.concatenate([values[..., half:], -values[..., :half]], axis=-1)


def along_depth(values, inverse):
    cosines, sines = dft_tables(values.shape[-1] // 2)
    matrix = jnp.block([[cosines, -sines], [sines, cosines]])
    if inverse:
        return jnp.einsum("tcxyr,kr->tcxyk", values, matrix, precision=highest)
    return jnp.einsum("tcxyr,rk->tcxyk", values, matrix, precision=highest)


def along(values, sign, axis):
    cosines, sines = dft_tables(values.shape[axis])
    table = jnp.concatenate([cosines, sign * sines], axis=1)
    stacked = jnp.concatenate([values, swap_parts(values)], axis=axis)
    spec = "ky,tcxyr->tcxkr" if axis == 3 else "kx,tcxyr->tckyr"
    return jnp.einsum(spec, table, stacked, precision=highest)


def contract(weights, hat_a, hat_b):
    depth = hat_a.shape[-1] // 2
    outputs = []
    for channel in range(weights.shape[0]):
        mixed_b = jnp.einsum("ij,tjxyk->tixyk", weights[channel], hat_b, precision=highest)
        direct = jnp.sum(hat_a * mixed_b, axis=1)
        crossed = jnp.sum(hat_a * swap_parts(mixed_b), axis=1)
        real_part = direct[..., :depth] + direct[..., depth:]
        imag_part = -(crossed[..., :depth] + crossed[..., depth:])
        outputs.append(jnp.concatenate([real_part, imag_part], axis=-1))
    return jnp.stack(outputs, axis=1)


def any_device(depth, field_a, field_b, pairs, signs):
    as_five = lambda v: v.reshape(v.shape[:3] + (-1, 2 * depth))
    as_four = lambda v: v.reshape(v.shape[:3] + (-1,))
    indices = jnp.arange(field_a.shape[1], dtype=jnp.int32)
    first = (pairs[:, :, 0][:, :, None] == indices).astype(jnp.float32)
    second = (pairs[:, :, 1][:, :, None] == indices).astype(jnp.float32)
    weights = jnp.einsum("cp,cpi,cpj->cij", signs.astype(jnp.float32), first, second, precision=highest)
    hats = []
    for field in (field_a, field_b):
        partial = as_four(along(along_depth(as_five(field), False), 1.0, 3))
        lines = lax.all_to_all(partial, "space", split_axis=3, concat_axis=2, tiled=True)
        hats.append(along(as_five(lines), 1.0, 2))
    returned = as_four(along(contract(weights, *hats), -1.0, 2))
    sites = lax.all_to_all(returned, "space", split_axis=2, concat_axis=3, tiled=True)
    return differences(as_four(along_depth(along(as_five(sites), -1.0, 3), True)))


def solution(mesh):
    devices = mesh.shape["space"]
    times = mesh.shape["tm"]

    def program(field_a, field_b, pairs, signs):
        _, components, size, flat = field_a.shape
        depth = flat // size // 2
        wide = LANES // 2
        fits = (
            depth == size
            and 2 * depth == 3 * wide
            and components == SUB
            and pairs.shape[0] == 4
            and size % (2 * devices) == 0
            and devices & (devices - 1) == 0
            and (size // devices) * 4 % SUB == 0
            and size % (2 * SUB) == 0
        )
        if fits:
            tables = (
                rows_forward(devices, size),
                rows_inverse(devices, size),
                columns_forward(devices, size),
                columns_inverse(devices, size),
                depth_forward(depth, wide, depth - wide),
                depth_forward(depth, 0, wide),
                depth_inverse(depth, wide, depth - wide, 2),
                depth_inverse(depth, 0, wide, 1),
            )
            per_device = functools.partial(fast_device, tables)
        else:
            per_device = functools.partial(any_device, depth)
        spec = P("tm", None, "space", None)
        return jax.shard_map(
            per_device,
            mesh=mesh,
            in_specs=(spec, spec, P(), P()),
            out_specs=(spec, spec, spec),
            check_vma=False,
        )(field_a, field_b, pairs, signs)

    return program
```

```python
import functools
import math

import jax
import jax.numpy as jnp
import ml_dtypes
import numpy as np
from jax import lax
from jax.experimental import pallas as pl
from jax.experimental.pallas import tpu as pltpu
from jax.sharding import PartitionSpec as P

highest = lax.Precision.HIGHEST
LANES = 128
SUB = 8
GRANT = 56 << 20
SMALL_GRANT = 24 << 20


def unitary(length):
    index = np.arange(length)
    angle = (index[:, None] * index[None, :] % length) * (2.0 * np.pi / length)
    return np.cos(angle) / math.sqrt(length), np.sin(angle) / math.sqrt(length)


def halves(table):
    high = table.astype(np.float32).astype(ml_dtypes.bfloat16)
    low = (table - high.astype(np.float64)).astype(np.float32).astype(ml_dtypes.bfloat16)
    return high, low


def left_table(table):
    high, low = halves(table)
    return np.concatenate([high, high, low], axis=1)


def right_table(table):
    high, low = halves(table)
    return np.concatenate([high, high, low], axis=0)


def owned(devices, length):
    each = length // devices
    me = np.arange(devices)
    return ((me[:, None] ^ me[None, :]) * each)[:, :, None] + np.arange(each)


def rows_forward(devices, length):
    cos, sin = unitary(length)
    out = []
    for spots in owned(devices, length):
        k = spots.reshape(devices, -1, 2).transpose(2, 0, 1).reshape(-1)
        y = np.arange(length).reshape(-1, 2).T.reshape(-1)
        c, s = cos[k][:, y], sin[k][:, y]
        out.append(left_table(np.block([[c, s], [-s, c]])))
    return np.stack(out)


def rows_inverse(devices, length):
    cos, sin = unitary(length)
    out = []
    for spots in owned(devices, length):
        y = np.arange(length).reshape(-1, 2).T.reshape(-1)
        blocks = []
        for e in range(2):
            k = spots.reshape(devices, -1, 2)[:, :, e].T.reshape(-1)
            c, s = cos[y][:, k], sin[y][:, k]
            blocks.append(np.block([[c, -s], [s, c]]))
        out.append(left_table(np.concatenate(blocks)))
    return np.stack(out)


def columns_forward(devices, length):
    cos, sin = unitary(length)
    out = []
    for spots in owned(devices, length):
        c, s = cos[:, spots.reshape(-1)], sin[:, spots.reshape(-1)]
        out.append(left_table(np.block([[c, s], [-s, c]])))
    return np.stack(out)


def columns_inverse(devices, length):
    cos, sin = unitary(length)
    out = []
    for spots in owned(devices, length):
        c, s = cos[spots.reshape(-1)], sin[spots.reshape(-1)]
        out.append(left_table(np.block([[c, -s], [s, c]])))
    return np.stack(out)


def depth_forward(length, first, count):
    cos, sin = unitary(length)
    k = np.tile(np.arange(first, first + count), LANES // count)
    matrix = np.block([[cos[:, k], -sin[:, k]], [sin[:, k], cos[:, k]]])
    gap = np.zeros((2 * LANES - 2 * length, 2 * LANES))
    both = np.stack([np.concatenate([matrix, gap]), np.concatenate([gap, matrix])])
    return np.stack([np.concatenate(halves(b)) for b in both])


def depth_inverse(length, first, count, halves_of):
    cos, sin = unitary(length)
    k = np.tile(np.arange(first, first + count), LANES // count)
    out = []
    for half in range(halves_of):
        keep = (np.arange(LANES) * halves_of // LANES == half)[:, None] * 1.0
        matrix = np.block([[cos[k] * keep, sin[k] * keep], [-sin[k] * keep, cos[k] * keep]])
        gap = np.zeros((matrix.shape[0], 2 * LANES - 2 * length))
        both = (np.concatenate([matrix, gap], axis=1), np.concatenate([gap, matrix], axis=1))
        out.append(np.stack([np.concatenate(halves(b)) for b in both]))
    return np.stack(out)


def split(value):
    high = value.astype(jnp.bfloat16)
    return high, (value - high.astype(jnp.float32)).astype(jnp.bfloat16)


def dot(left, right):
    return jnp.dot(left, right, preferred_element_type=jnp.float32)


def left_dot(table, value):
    high, low = split(value)
    return dot(table, jnp.concatenate([high, low, high], axis=0))


def lane_index(shape):
    return lax.broadcasted_iota(jnp.int32, shape, len(shape) - 1)


def forward_kernel(narrow, sites, pairs_y, field_a, field_b, depth, table, token, out, packed, *spectra):
    for site in range(field_a.shape[1]):
        spaces = spectra[2 * site], spectra[2 * site + 1]
        forward_site(narrow, pairs_y, field_a.at[0, site], field_b.at[0, site], depth, table, packed.at[site], spaces)
        for block in range(out.shape[0]):
            out[block, site] = packed[site, block * SUB : (block + 1) * SUB, :]


def forward_site(narrow, pairs_y, field_a, field_b, depth, table, packed, spectra):
    groups = 1 if narrow else 2
    width = LANES // 4 if narrow else LANES // 2
    block = 2 * groups * SUB
    slots = []
    for group, field in enumerate((field_a, field_b)):
        tiles = [
            jnp.concatenate(
                [field[:, (3 * p + q) * LANES : (3 * p + q + 1) * LANES] for p in range(pairs_y)], axis=0
            )
            for q in range(3)
        ]
        tiles = [split(tile) for tile in tiles]
        for e in range(2):
            left = [tiles[e + k][part] for part in (0, 1, 0) for k in range(2)]
            high_rows, low_rows = depth[e, : 2 * LANES], depth[e, 2 * LANES :]
            result = dot(jnp.concatenate(left, axis=1), jnp.concatenate([high_rows, high_rows, low_rows], axis=0))
            for part in range(2):
                spectra[group][part * 2 + e, : result.shape[0]] = result[:, part * LANES : (part + 1) * LANES]

        def rows_of(c, group=group):
            return jnp.concatenate(
                [spectra[group][k, pl.ds(c, pairs_y, stride=SUB), :] for k in range(4)], axis=0
            )

        if narrow:
            for c in range(SUB // 2):
                first, second = rows_of(c), rows_of(c + SUB // 2)
                pick = lane_index(first.shape) < LANES // 2
                slots.append((0, group * 4 + c, jnp.where(pick, first, second)))
        else:
            slots += [(group, c, rows_of(c)) for c in range(SUB)]

    for first in range(0, len(slots), SUB):
        batch = slots[first : first + SUB]
        result = left_dot(table[...], jnp.concatenate([value for _, _, value in batch], axis=1))
        half = result.shape[0] // 4
        for part in range(2):
            even = result[2 * part * half : (2 * part + 1) * half]
            odd = result[(2 * part + 1) * half : (2 * part + 2) * half]
            merged = jnp.where(lane_index(even.shape) // width % 2 == 0, even, odd)
            for i, (group, slot, _) in enumerate(batch):
                start = (part * groups + group) * SUB + slot
                packed[pl.ds(start, half, stride=block), :] = merged[:, i * LANES : (i + 1) * LANES]


def forward(field_a, field_b, depth, table, narrow, token):
    _, sites, components, flat = field_a.shape
    groups = 1 if narrow else 2
    size = table.shape[0] // 2
    pairs_y = size // 2
    lines = size // 2
    blocks = lines * 2 * groups
    step = 1
    spot = pl.BlockSpec((1, step, components, flat), lambda x: (0, x, 0, 0))
    whole = lambda value: pl.BlockSpec(value.shape, lambda x: (0,) * value.ndim)
    return pl.pallas_call(
        functools.partial(forward_kernel, narrow, sites, pairs_y),
        grid=(sites // step,),
        in_specs=[spot, spot, whole(depth), whole(table), pl.BlockSpec(memory_space=pl.ANY)],
        out_specs=pl.BlockSpec((blocks, step, SUB, LANES), lambda x: (0, x, 0, 0)),
        out_shape=jax.ShapeDtypeStruct((blocks, sites, SUB, LANES), jnp.float32),
        scratch_shapes=[pltpu.VMEM((step, (blocks + 2 * groups) * SUB, LANES), jnp.float32)]
        + [pltpu.VMEM((4, (pairs_y + 1) * SUB, LANES), jnp.float32)] * (2 * step),
        compiler_params=pltpu.CompilerParams(vmem_limit_bytes=GRANT),
        cost_estimate=pl.CostEstimate(flops=8 * 10**9, bytes_accessed=12 * 10**6, transcendentals=0),
        name="forward_narrow" if narrow else "forward_wide",
    )(field_a, field_b, depth, table, token)


def placed(space, *values):
    return [pltpu.with_memory_space_constraint(value, space) for value in values]


def each(refs):
    return [ref.at[i] for ref in refs for i in range(ref.shape[0])]


def middle_kernel(narrow, arrays, devices, sites, channels, count, pairs, signs, *refs):
    pieces, refs = each(refs[:arrays]), refs[arrays:]
    table_f, table_i, out, lines, hats, mixed, rows = refs
    groups = 1 if narrow else 2
    size = devices * sites
    both = 2 * size
    for s, piece in enumerate(pieces):
        for part in range(2):
            for g in range(groups):
                for x in range(sites):
                    at = part * size + s * sites + x
                    lines[g, pl.ds(at, SUB, stride=both), :] = piece[0, part, g, x * SUB : (x + 1) * SUB, :]
    for g in range(groups):
        for quad in range(2):
            tiles = [lines[g, (quad * 4 + j) * both : (quad * 4 + j + 1) * both, :] for j in range(4)]
            result = left_dot(table_f[...], jnp.concatenate(tiles, axis=1))
            for j in range(4):
                hat = result[:, j * LANES : (j + 1) * LANES]
                if narrow:
                    turned = pltpu.roll(hat, LANES // 2, axis=1)
                    places = ((quad, j, hat), (quad, j + SUB // 2, turned))
                else:
                    places = ((g, quad * 4 + j, hat),)
                for field, c, value in places:
                    hats[field * SUB + c] = value
                    if field:
                        hats[2 * SUB + c] = -value

    def channel(c, carry):
        def pair(p, totals):
            i = pairs[c, 2 * p]
            j = pairs[c, 2 * p + 1] + jnp.where(signs[c, p] < 0, 2 * SUB, SUB)
            a_re, a_im = hats[i, 0:size, :], hats[i, size:both, :]
            b_re, b_im = hats[j, 0:size, :], hats[j, size:both, :]
            return (
                totals[0] + (a_re * b_re + a_im * b_im),
                totals[1] + (a_im * b_re - a_re * b_im),
            )

        zero = jnp.zeros((size, LANES), jnp.float32)
        real, imag = lax.fori_loop(0, count, pair, (zero, zero), unroll=4)
        mixed[c, 0:size, :] = real
        mixed[c, size:both, :] = imag
        return carry

    lax.fori_loop(0, channels, channel, 0)
    if narrow:
        tiles = []
        for c in range(0, channels, 2):
            other = pltpu.roll(mixed[c + 1], LANES // 2, axis=1)
            tiles.append(jnp.where(lane_index(other.shape) < LANES // 2, mixed[c], other))
    else:
        tiles = [mixed[c] for c in range(channels)]
    result = left_dot(table_i[...], jnp.concatenate(tiles, axis=1))
    each_site = 2 * len(tiles)
    for t in range(len(tiles)):
        for part in range(2):
            value = result[part * size : (part + 1) * size, t * LANES : (t + 1) * LANES]
            first = 2 * t + part if narrow else part * channels + t
            rows[pl.ds(first, size, stride=each_site), :] = value
    for s in range(devices):
        out[s, 0] = rows[s * sites * each_site : (s + 1) * sites * each_site, :]


def middle(pieces, pairs, signs, table_f, table_i, sites, channels, narrow):
    size = table_f.shape[0] // 2
    devices = size // sites
    steps = pieces[0].shape[1]
    smem = pl.BlockSpec(memory_space=pltpu.SMEM)
    whole = lambda value: pl.BlockSpec(value.shape, lambda r: (0,) * value.ndim)
    third = lambda value: pl.BlockSpec(
        value.shape[:1] + (1,) + value.shape[2:], lambda r: (0, r) + (0,) * (value.ndim - 2)
    )
    rows = sites * (channels if narrow else 2 * channels)
    groups = 1 if narrow else 2
    return pl.pallas_call(
        functools.partial(middle_kernel, narrow, len(pieces), devices, sites, channels, signs.shape[1]),
        grid=(steps,),
        in_specs=[smem, smem] + [third(v) for v in pieces] + [whole(table_f), whole(table_i)],
        out_specs=pl.BlockSpec((devices, 1, rows, LANES), lambda r: (0, r, 0, 0)),
        out_shape=jax.ShapeDtypeStruct((devices, steps, rows, LANES), jnp.float32),
        scratch_shapes=[
            pltpu.VMEM((groups, (SUB + 1) * 2 * size, LANES), jnp.float32),
            pltpu.VMEM((3 * SUB, 2 * size, LANES), jnp.float32),
            pltpu.VMEM((channels, 2 * size, LANES), jnp.float32),
            pltpu.VMEM((devices * rows + SUB, LANES), jnp.float32),
        ],
        compiler_params=pltpu.CompilerParams(vmem_limit_bytes=SMALL_GRANT),
        cost_estimate=pl.CostEstimate(flops=4 * 10**9, bytes_accessed=10 * 10**6, transcendentals=0),
        name="middle_narrow" if narrow else "middle_wide",
    )(pairs, signs, *placed(pltpu.VMEM if narrow else pltpu.HBM, *pieces), *placed(pltpu.HBM, table_f, table_i))


def inverse_kernel(narrow, arrays, devices, channels, pairs_y, *refs):
    pieces, refs = each(refs[:arrays]), refs[arrays:]
    if narrow:
        table, depth, out, lines, staged = refs
        partial = out
    else:
        partial, table, depth, out, lines, staged = refs
    thirds = pieces[0].shape[0]
    size = thirds * devices

    @pl.when(pl.program_id(0) == 0)
    def _():
        for s in range(devices):
            for r in range(thirds):
                for v in range(pieces[s].shape[1] // SUB):
                    start = v * SUB * size + r * devices + s
                    lines[pl.ds(start, SUB, stride=size), :] = pieces[s][r, v * SUB : (v + 1) * SUB, :]

    step = partial.shape[0]
    for site in range(step):
        x = pl.program_id(0) * step + site
        place = None if narrow else out.at[0, site]
        inverse_site(narrow, channels, pairs_y, size, x, lines, table, depth, staged.at[site], partial.at[site], place)


def inverse_site(narrow, channels, pairs_y, size, x, lines, table, depth, staged, partial, out):
    def tile(*spots):
        return jnp.concatenate([lines[pl.ds(pl.multiple_of(k * size, SUB), size), :] for k in spots], axis=0)

    if narrow:
        tiles = [tile(x * channels + 2 * c, x * channels + 2 * c + 1) for c in range(channels // 2)]
        width, sets = LANES // 4, [range(parity, channels, 2) for parity in range(2)]
    else:
        big = 2 * x * channels
        tiles = [tile(big + c, big + channels + c) for c in range(channels)]
        width, sets = LANES // 2, [range(channels)]
    result = left_dot(table[...], jnp.concatenate(tiles, axis=1))
    half = result.shape[0] // 2
    first, second = result[:half], result[half:]
    high, low = split(jnp.where(lane_index(first.shape) & width == 0, first, second))

    def rows_of(value, e, c):
        spot = c // 2 if narrow else c
        return jnp.concatenate(
            [
                value[(2 * part + e) * pairs_y : (2 * part + e + 1) * pairs_y, spot * LANES : (spot + 1) * LANES]
                for part in range(2)
            ],
            axis=1,
        )

    for k, members in enumerate(sets):
        products = []
        for e in range(2):
            left = [jnp.concatenate([rows_of(value, e, c) for c in members], axis=0) for value in (high, low)]
            high_rows, low_rows = depth[k, e, : 2 * LANES], depth[k, e, 2 * LANES :]
            right = jnp.concatenate([high_rows, high_rows, low_rows], axis=0)
            products.append(dot(jnp.concatenate([left[0], left[1], left[0]], axis=1), right))
        for i, c in enumerate(members):
            rows = slice(i * pairs_y, (i + 1) * pairs_y)
            zero, one = products[0][rows], products[1][rows]
            for q, value in enumerate((zero[:, :LANES], zero[:, LANES:] + one[:, :LANES], one[:, LANES:])):
                staged[q, pl.ds(c, pairs_y, stride=channels), :] = value
    if narrow:
        partial[...] = staged[:, : partial.shape[1], :]
    else:
        for p in range(pairs_y):
            rows = slice(p * channels, (p + 1) * channels)
            for q in range(3):
                lanes = slice((3 * p + q) * LANES, (3 * p + q + 1) * LANES)
                out[:, lanes] = staged[q, rows, :] + partial[q, rows, :]


def inverse(pieces, partial, table, depth, sites, channels, flat, share=0, shares=1):
    narrow = partial is None
    size = table.shape[1] // 6
    devices = size // pieces[0].shape[1]
    whole = lambda value: pl.BlockSpec(value.shape, lambda x: (0,) * value.ndim)
    tiles = (3, size * channels, LANES)
    rows = pieces[0].shape[2] // shares
    sites = sites // shares
    lines = pltpu.VMEM(((rows + 1) * size, LANES), jnp.float32)
    part = lambda value: pl.BlockSpec(value.shape[:2] + (rows, LANES), lambda x: (0, 0, share, 0))
    step = 3 if sites % 3 == 0 else 1
    kept = pl.BlockSpec((step,) + tiles, lambda x: (x + share * sites // step, 0, 0, 0))
    return pl.pallas_call(
        functools.partial(inverse_kernel, narrow, len(pieces), devices, channels, size),
        grid=(sites // step,),
        in_specs=[part(v) for v in pieces] + ([] if narrow else [kept]) + [whole(table), whole(depth)],
        out_specs=kept if narrow else pl.BlockSpec((1, step, channels, flat), lambda x: (0, x, 0, 0)),
        out_shape=jax.ShapeDtypeStruct((sites,) + tiles if narrow else (1, sites, channels, flat), jnp.float32),
        scratch_shapes=[lines, pltpu.VMEM((step, 3, size * channels + SUB, LANES), jnp.float32)],
        compiler_params=pltpu.CompilerParams(vmem_limit_bytes=SMALL_GRANT),
        cost_estimate=pl.CostEstimate(flops=4 * 10**9, bytes_accessed=6 * 10**6, transcendentals=0),
        name="inverse_narrow" if narrow else "inverse_wide",
    )(*placed(pltpu.VMEM, *pieces), *([] if narrow else placed(pltpu.VMEM, partial)), *placed(pltpu.HBM if narrow else pltpu.VMEM, table, depth))


AT_ONCE = dict(sent_narrow=True, sent_wide=True, back_narrow=True, back_wide=True)


def exchange(packed, at_once):
    if at_once:
        return [lax.all_to_all(packed, "space", 0, 0, tiled=True)]
    devices = packed.shape[0]
    order = sorted(range(1, devices), key=lambda s: (s % 4, -(s // 8), s))
    got = [packed[:1]] + [None] * (devices - 1)
    for s in order:
        got[s] = lax.ppermute(packed[s : s + 1], "space", [(i, i ^ s) for i in range(devices)])
    return got


def fast_slice(field_a, field_b, pairs, signs, tables):
    _, sites, components, flat = field_a.shape
    devices = lax.axis_size("space")
    channels = pairs.shape[0]
    me = lax.axis_index("space")
    mine = [lax.dynamic_index_in_dim(jnp.asarray(t), me, 0, False) for t in tables[:4]]
    fixed = [jnp.asarray(t[0]) for t in tables[:4]]

    def table(which, name):
        return (fixed if AT_ONCE[name] else mine)[which]

    depth_n, depth_w, depth_in, depth_iw = (jnp.asarray(t) for t in tables[4:])
    thirds = tables[0].shape[1] // 4 // devices
    flat_pairs = pairs.reshape(channels, -1)
    sent = {}
    token = signs
    for narrow, depth in ((True, depth_n), (False, depth_w)):
        name = "sent_narrow" if narrow else "sent_wide"
        groups = 1 if narrow else 2
        packed = forward(field_a, field_b, depth, table(0, name), narrow, token)
        token = packed[0, 0]
        packed = packed.reshape(devices, thirds, 2, groups, sites * SUB, LANES)
        sent[narrow] = exchange(packed, AT_ONCE[name])
    partial = None
    shares = 2 if sites % 2 == 0 and sites // 2 * 2 * channels % SUB == 0 else 1
    for narrow, depth in ((True, depth_in), (False, depth_iw)):
        come, go = ("sent_narrow", "back_narrow") if narrow else ("sent_wide", "back_wide")
        mixed = middle(sent[narrow], flat_pairs, signs, table(2, come), table(3, go), sites, channels, narrow)
        back = exchange(mixed, AT_ONCE[go])
        shared = functools.partial(inverse, back, partial, table(1, go), depth, sites, channels, flat)
        if narrow:
            partial = shared()
    return [shared(share, shares) for share in range(shares)]


def neighbours(value):
    devices, length = lax.axis_size("tm"), value.shape[0]
    up = [(i, (i + 1) % devices) for i in range(devices)]
    down = [(j, i) for i, j in up]
    after = lax.ppermute(value[:1], "tm", down)
    before = after if devices == 2 and length == 1 else lax.ppermute(value[-1:], "tm", up)
    later = jnp.concatenate([value[1:], after], axis=0)
    earlier = jnp.concatenate([before, value[:-1]], axis=0)
    return later, earlier


def differences(correlator):
    later, earlier = neighbours(correlator)
    return correlator, later - correlator, later - 2.0 * correlator + earlier


def differences_kernel(count, own, *refs):
    later, earlier = refs[0], refs[count - 1]
    outs = refs[-3:]
    outs[0][...] = own[...]
    outs[1][...] = later[...] - own[...]
    outs[2][...] = later[...] - 2.0 * own[...] + earlier[...]


def write_differences(own, others, share, shares, written):
    _, sites, channels, flat = own.shape
    block = (1, 1, channels, flat)
    mine = pl.BlockSpec(block, lambda x: (0, x, 0, 0))
    shape = jax.ShapeDtypeStruct((1, sites * shares, channels, flat), jnp.float32)
    count = len(others)
    return pl.pallas_call(
        functools.partial(differences_kernel, count),
        grid=(sites,),
        in_specs=[mine] * (1 + count) + [pl.BlockSpec(memory_space=pl.ANY)] * len(written),
        out_specs=[pl.BlockSpec(block, lambda x: (0, x + share * sites, 0, 0))] * 3,
        out_shape=[shape] * 3,
        input_output_aliases={1 + count + k: k for k in range(len(written))},
        compiler_params=pltpu.CompilerParams(vmem_limit_bytes=SMALL_GRANT),
        cost_estimate=pl.CostEstimate(flops=10**6, bytes_accessed=5 * own.size * 4, transcendentals=0),
        name="differences",
    )(own, *others, *written)


def one_time(tables, field_a, field_b, pairs, signs):
    devices = lax.axis_size("tm")
    up = [(i, (i + 1) % devices) for i in range(devices)]
    shares = fast_slice(field_a, field_b, pairs, signs, tables)
    written = []
    for share, own in enumerate(shares):
        others = [lax.ppermute(own, "tm", [(j, i) for i, j in up])]
        if devices != 2:
            others.append(lax.ppermute(own, "tm", up))
        written = write_differences(own, others, share, len(shares), written)
    return written


def fast_device(tables, field_a, field_b, pairs, signs):
    field_a, field_b = field_a.swapaxes(1, 2), field_b.swapaxes(1, 2)
    if field_a.shape[0] == 1:
        outs = one_time(tables, field_a, field_b, pairs, signs)
    else:
        parts = [
            jnp.concatenate(fast_slice(field_a[t : t + 1], field_b[t : t + 1], pairs, signs, tables), axis=1)
            for t in range(field_a.shape[0])
        ]
        outs = differences(jnp.concatenate(parts, axis=0))
    return tuple(out.swapaxes(1, 2) for out in outs)


def dft_tables(length):
    cos, sin = unitary(length)
    return jnp.asarray(cos, jnp.float32), jnp.asarray(sin, jnp.float32)


def swap_parts(values):
    half = values.shape[-1] // 2
    return jnp.concatenate([values[..., half:], -values[..., :half]], axis=-1)


def along_depth(values, inverse):
    cosines, sines = dft_tables(values.shape[-1] // 2)
    matrix = jnp.block([[cosines, -sines], [sines, cosines]])
    if inverse:
        return jnp.einsum("tcxyr,kr->tcxyk", values, matrix, precision=highest)
    return jnp.einsum("tcxyr,rk->tcxyk", values, matrix, precision=highest)


def along(values, sign, axis):
    cosines, sines = dft_tables(values.shape[axis])
    table = jnp.concatenate([cosines, sign * sines], axis=1)
    stacked = jnp.concatenate([values, swap_parts(values)], axis=axis)
    spec = "ky,tcxyr->tcxkr" if axis == 3 else "kx,tcxyr->tckyr"
    return jnp.einsum(spec, table, stacked, precision=highest)


def contract(weights, hat_a, hat_b):
    depth = hat_a.shape[-1] // 2
    outputs = []
    for channel in range(weights.shape[0]):
        mixed_b = jnp.einsum("ij,tjxyk->tixyk", weights[channel], hat_b, precision=highest)
        direct = jnp.sum(hat_a * mixed_b, axis=1)
        crossed = jnp.sum(hat_a * swap_parts(mixed_b), axis=1)
        real_part = direct[..., :depth] + direct[..., depth:]
        imag_part = -(crossed[..., :depth] + crossed[..., depth:])
        outputs.append(jnp.concatenate([real_part, imag_part], axis=-1))
    return jnp.stack(outputs, axis=1)


def any_device(depth, field_a, field_b, pairs, signs):
    as_five = lambda v: v.reshape(v.shape[:3] + (-1, 2 * depth))
    as_four = lambda v: v.reshape(v.shape[:3] + (-1,))
    indices = jnp.arange(field_a.shape[1], dtype=jnp.int32)
    first = (pairs[:, :, 0][:, :, None] == indices).astype(jnp.float32)
    second = (pairs[:, :, 1][:, :, None] == indices).astype(jnp.float32)
    weights = jnp.einsum("cp,cpi,cpj->cij", signs.astype(jnp.float32), first, second, precision=highest)
    hats = []
    for field in (field_a, field_b):
        partial = as_four(along(along_depth(as_five(field), False), 1.0, 3))
        lines = lax.all_to_all(partial, "space", split_axis=3, concat_axis=2, tiled=True)
        hats.append(along(as_five(lines), 1.0, 2))
    returned = as_four(along(contract(weights, *hats), -1.0, 2))
    sites = lax.all_to_all(returned, "space", split_axis=2, concat_axis=3, tiled=True)
    return differences(as_four(along_depth(along(as_five(sites), -1.0, 3), True)))


def solution(mesh):
    devices = mesh.shape["space"]
    times = mesh.shape["tm"]

    def program(field_a, field_b, pairs, signs):
        _, components, size, flat = field_a.shape
        depth = flat // size // 2
        wide = LANES // 2
        fits = (
            depth == size
            and 2 * depth == 3 * wide
            and components == SUB
            and pairs.shape[0] == 4
            and size % (2 * devices) == 0
            and devices & (devices - 1) == 0
            and (size // devices) * 4 % SUB == 0
            and size % (2 * SUB) == 0
        )
        if fits:
            tables = (
                rows_forward(devices, size),
                rows_inverse(devices, size),
                columns_forward(devices, size),
                columns_inverse(devices, size),
                depth_forward(depth, wide, depth - wide),
                depth_forward(depth, 0, wide),
                depth_inverse(depth, wide, depth - wide, 2),
                depth_inverse(depth, 0, wide, 1),
            )
            per_device = functools.partial(fast_device, tables)
        else:
            per_device = functools.partial(any_device, depth)
        spec = P("tm", None, "space", None)
        return jax.shard_map(
            per_device,
            mesh=mesh,
            in_specs=(spec, spec, P(), P()),
            out_specs=(spec, spec, spec),
            check_vma=False,
        )(field_a, field_b, pairs, signs)

    return program
```
